32 devices in a mesh: seq: 8 (over z, y), dp: 4 (over x, core).
Axes of the slice: x: 2, y: 2, z: 4, core: 2. Of those that a mesh axis runs over, the one named last changes fastest.
Arguments:
- queries: bfloat16 [4, 2048, 4096], P('dp', None, 'seq'), may hold values from -6 to 6
- keys: bfloat16 [4, 2048, 4096], P('dp', None, 'seq'), may hold values from -6 to 6
- values: bfloat16 [4, 2048, 4096], P('dp', None, 'seq'), may hold values from -6 to 6
- random_blocks: int32 [4, 32, 64, 3], P('dp', 'seq'), may hold values from 0 to 63
- global_blocks: int32 [4, 2], P('dp'), may hold values from 0 to 63, as said below
- out_weight: bfloat16 [2048, 2048], P('dp'), may hold values from -0.125 to 0.125
Outputs:
- projected: bfloat16 [4, 4096, 2048], P('dp', 'seq')
The draws below stay inside these ranges and needn't reach their ends.
Inputs may be any that keep to these rules, and one draw needn't show every extreme that they name: `global_blocks`: the two global blocks of a sequence differ; some sequence has block 0 and some has block 63.
All inputs are finite; a program needn't handle non-finite values.
Results may differ from the reference program's by a relative error of at most 0.01.
Values may be sent and summed in bfloat16 or wider, within the bound.
No kernel may reach another device: no remote copies, remote signals or barrier semaphores. Data moves between devices by JAX's collectives and lax.ppermute only.
A program may use at most 128 MiB of HBM per device.

```python
import jax
import jax.numpy as jnp
from jax import lax

H = 32
HD = 64
BLK = 64
R = 3
D = 2048
L = 4096
NB = 64
B = 4


def global_choice(key):
    half = NB // 2
    first = jax.random.randint(jax.random.fold_in(key, 777), (B,), 0, half)
    second = jax.random.randint(jax.random.fold_in(key, 778), (B,), half, NB)
    low_item = jax.random.randint(jax.random.fold_in(key, 779), (), 0, B)
    high_item = jax.random.randint(jax.random.fold_in(key, 780), (), 0, B)
    items = jnp.arange(B)
    first = jnp.where(items == low_item, 0, first)
    second = jnp.where(items == high_item, NB - 1, second)
    return jnp.stack([first, second], axis=1).astype(jnp.int32)


def shared_direction(key):
    picks = jax.random.bernoulli(jax.random.fold_in(key, 555), 0.5, (B, D))
    return jnp.where(picks, 1.0, -1.0).astype(jnp.float32)


def base_field(key):
    return jnp.clip(jax.random.normal(key, (B, D, L), jnp.float32), -4.5, 4.5)


def draw_global_blocks(key, part):
    return global_choice(key)


def draw_queries(key, part):
    field = base_field(jax.random.fold_in(key, 11))
    glob = global_choice(key)
    direction = shared_direction(key)
    block_of = (jnp.arange(L) // BLK).astype(jnp.int32)
    in_global = jnp.any(glob[:, :, None] == block_of[None, None, :], axis=1)
    field = jnp.where(in_global[:, None, :], field + direction[:, :, None], field)
    return field.astype(jnp.bfloat16)


def draw_keys(key, part):
    field = base_field(jax.random.fold_in(key, 23))
    direction = shared_direction(key)
    planted_count = 16
    spots = jax.random.randint(jax.random.fold_in(key, 888), (B, planted_count), 0, L)
    weights = jax.random.uniform(jax.random.fold_in(key, 999), (B, planted_count), jnp.float32, 0.8, 1.4)
    hits = spots[:, :, None] == jnp.arange(L)[None, None, :]
    planted = jnp.any(hits, axis=1)
    weight_at = jnp.max(jnp.where(hits, weights[:, :, None], 0.0), axis=1)
    field = jnp.where(planted[:, None, :], weight_at[:, None, :] * direction[:, :, None] + 0.3 * field, field)
    return field.astype(jnp.bfloat16)


def with_ends(values, key, least, largest):
    shape = values.shape
    index_at = [jax.random.randint(jax.random.fold_in(key, axis), (), 0, shape[axis]) for axis in range(len(shape))]
    values = values.at[tuple(index_at)].set(least)
    longest = shape.index(max(shape))
    index_at[longest] = (index_at[longest] + 1) % shape[longest]
    return values.at[tuple(index_at)].set(largest)


def block_levels(key, dims, shards, least, largest):
    gain = 1.0
    for axis_at, parts in shards:
        draws = jax.random.uniform(jax.random.fold_in(jax.random.fold_in(key, 6), axis_at), (parts,), jnp.float32, least / len(shards), largest / len(shards))
        gain = gain * jnp.repeat(jnp.exp(draws), dims[axis_at] // parts).reshape((-1,) + (1,) * (len(dims) - 1 - axis_at))
    return gain


def scatter_about(rng, extent, scale, reach, shards=(), held_as=jnp.bfloat16):
    entries = jax.random.normal(rng, extent, jnp.float32) * scale
    if len(shards) > 0:
        entries = block_levels(rng, extent, shards, -0.22, 0.18) * entries
    return jnp.clip(entries, min=-reach, max=reach).astype(held_as)


def setup_inputs(seed: int = 0) -> dict:
    key_of = jax.random.split(jax.random.key(seed), 7)
    return {
        "queries": draw_queries(jax.random.fold_in(key_of[6], 71), 0),
        "keys": draw_keys(jax.random.fold_in(key_of[6], 71), 0),
        "values": scatter_about(key_of[2], (B, D, L), 1.0, 6.0, ((0, 4), (2, 8))),
        "random_blocks": with_ends(jax.random.randint(key_of[3], (B, H, NB, R), 0, NB), jax.random.fold_in(key_of[3], 1), 0, NB - 1).astype(jnp.int32),
        "global_blocks": draw_global_blocks(jax.random.fold_in(key_of[6], 71), 0),
        "out_weight": scatter_about(key_of[5], (D, D), D ** -0.5, 0.125, ((0, 4),)),
    }


def candidate_blocks(nblocks, glob, rand_h):
    rows = jnp.arange(nblocks, dtype=jnp.int32)
    window = jnp.stack([rows - 1, rows, rows + 1], axis=1)
    globs = jnp.broadcast_to(glob[None, :].astype(jnp.int32), (nblocks, glob.shape[0]))
    cand = jnp.concatenate([window, globs, rand_h.astype(jnp.int32)], axis=1)
    inside = (cand >= 0) & (cand < nblocks)
    width = cand.shape[1]
    equal = cand[:, :, None] == cand[:, None, :]
    earlier = jnp.arange(width)[None, :] < jnp.arange(width)[:, None]
    repeated = jnp.any(equal & earlier[None, :, :], axis=2)
    return jnp.clip(cand, 0, nblocks - 1).astype(jnp.int32), inside & (~repeated)


def head_attention(q_head, k_head, v_head, rand_h, glob):
    length = q_head.shape[1]
    nblocks = length // BLK
    scale = HD ** -0.5
    qb = q_head.astype(jnp.float32).reshape(HD, nblocks, BLK)
    kb = k_head.astype(jnp.float32).reshape(HD, nblocks, BLK)
    vb = v_head.astype(jnp.float32).reshape(HD, nblocks, BLK)
    index, valid = candidate_blocks(nblocks, glob, rand_h)
    kg = jnp.take(kb, index, axis=1)
    vg = jnp.take(vb, index, axis=1)
    scores = jnp.einsum('dnq,dnck->nqck', qb, kg) * scale
    scores = jnp.where(valid[:, None, :, None], scores, -jnp.inf)
    top = jnp.max(scores, axis=(2, 3), keepdims=True)
    expo = jnp.exp(scores - top)
    probs = (expo / jnp.sum(expo, axis=(2, 3), keepdims=True)).astype(jnp.bfloat16)
    sparse = jnp.einsum('nqck,dnck->dnq', probs.astype(jnp.float32), vg)
    qglob = jnp.take(qb, glob, axis=1)
    gscore = jnp.einsum('dgq,dk->gqk', qglob, k_head.astype(jnp.float32)) * scale
    gtop = jnp.max(gscore, axis=2, keepdims=True)
    gexp = jnp.exp(gscore - gtop)
    gprob = (gexp / jnp.sum(gexp, axis=2, keepdims=True)).astype(jnp.bfloat16)
    full = jnp.einsum('gqk,dk->dgq', gprob.astype(jnp.float32), v_head.astype(jnp.float32))
    sparse = sparse.at[:, glob, :].set(full)
    return sparse.astype(jnp.bfloat16).reshape(HD, length)


def reference(queries, keys, values, random_blocks, global_blocks, out_weight):
    batch = queries.shape[0]
    length = queries.shape[2]

    def one_item(item):
        seq_id = item // H
        head_id = item % H
        start = (head_id * HD).astype(jnp.int32)
        q_head = lax.dynamic_slice_in_dim(queries[seq_id], start, HD, 0)
        k_head = lax.dynamic_slice_in_dim(keys[seq_id], start, HD, 0)
        v_head = lax.dynamic_slice_in_dim(values[seq_id], start, HD, 0)
        return head_attention(q_head, k_head, v_head, random_blocks[seq_id, head_id], global_blocks[seq_id])

    heads = lax.map(one_item, jnp.arange(batch * H, dtype=jnp.int32))
    attended = heads.reshape(batch, H * HD, length)

    def project(item):
        return jnp.dot(attended[item].T, out_weight, preferred_element_type=jnp.float32).astype(jnp.bfloat16)

    return lax.map(project, jnp.arange(batch, dtype=jnp.int32))
```

```python
import functools
import math

import jax
import jax.numpy as jnp
from jax import lax
from jax.experimental import pallas as pl
from jax.experimental.pallas import tpu as pltpu
from jax.sharding import PartitionSpec as P

HD = 64
BLK = 64
PAIR = 2 * HD
EXP_SCALE = HD ** (-0.5) * math.log2(math.e)
BIG = 1e30


def candidate_blocks(nblocks, glob, rand_h):
    rows = jnp.arange(nblocks, dtype=jnp.int32)
    window = jnp.stack([rows - 1, rows, rows + 1], axis=1)
    globs = jnp.broadcast_to(glob[None, :], (nblocks, glob.shape[0]))
    cand = jnp.concatenate([window, globs, rand_h], axis=1)
    inside = (cand >= 0) & (cand < nblocks)
    width = cand.shape[1]
    equal = cand[:, :, None] == cand[:, None, :]
    earlier = jnp.arange(width)[None, :] < jnp.arange(width)[:, None]
    repeated = jnp.any(equal & earlier[None, :, :], axis=2)
    return (jnp.clip(cand, 0, nblocks - 1), inside & ~repeated)


def head_attention(q_head, k_head, v_head, rand_h, glob):
    length = q_head.shape[1]
    nblocks = length // BLK
    scale = HD ** (-0.5)
    qb = q_head.reshape(HD, nblocks, BLK)
    kb = k_head.reshape(HD, nblocks, BLK)
    vb = v_head.reshape(HD, nblocks, BLK)
    index, valid = candidate_blocks(nblocks, glob, rand_h)
    group = math.gcd(nblocks, 32)
    turns = nblocks // group

    def one_group(turn):
        first = turn * group
        rows_index = lax.dynamic_slice_in_dim(index, first, group, 0)
        rows_valid = lax.dynamic_slice_in_dim(valid, first, group, 0)
        q_rows = lax.dynamic_slice_in_dim(qb, first, group, 1)
        k_rows = jnp.take(kb, rows_index, axis=1)
        v_rows = jnp.take(vb, rows_index, axis=1)
        scores = (
            jnp.einsum("dnq,dnck->nqck", q_rows, k_rows, preferred_element_type=jnp.float32) * scale
        )
        scores = jnp.where(rows_valid[:, None, :, None], scores, -jnp.inf)
        top = jnp.max(scores, axis=(2, 3), keepdims=True)
        expo = jnp.exp(scores - top)
        probs = (expo / jnp.sum(expo, axis=(2, 3), keepdims=True)).astype(jnp.bfloat16)
        return jnp.einsum(
            "nqck,dnck->dnq", probs, v_rows, preferred_element_type=jnp.float32
        ).astype(jnp.bfloat16)

    parts = lax.map(one_group, jnp.arange(turns, dtype=jnp.int32))
    blocks = jnp.transpose(parts, (1, 0, 2, 3)).reshape(HD, nblocks, BLK)
    qglob = jnp.take(qb, glob, axis=1)
    gscore = jnp.einsum("dgq,dk->gqk", qglob, k_head, preferred_element_type=jnp.float32) * scale
    gtop = jnp.max(gscore, axis=2, keepdims=True)
    gexp = jnp.exp(gscore - gtop)
    gprob = (gexp / jnp.sum(gexp, axis=2, keepdims=True)).astype(jnp.bfloat16)
    full = jnp.einsum("gqk,dk->dgq", gprob, v_head, preferred_element_type=jnp.float32).astype(
        jnp.bfloat16
    )
    blocks = blocks.at[:, glob, :].set(full)
    return blocks.reshape(HD, length)


def local_plain(queries, keys, values, random_blocks, global_blocks, out_weight):
    q_heads, k_heads, v_heads = (
        lax.all_to_all(queries[0], "seq", split_axis=0, concat_axis=1, tiled=True),
        lax.all_to_all(keys[0], "seq", split_axis=0, concat_axis=1, tiled=True),
        lax.all_to_all(values[0], "seq", split_axis=0, concat_axis=1, tiled=True),
    )
    count = q_heads.shape[0] // HD
    length = q_heads.shape[1]
    glob = global_blocks[0]

    def one_head(packed):
        q_head, k_head, v_head, rand_h = packed
        return head_attention(q_head, k_head, v_head, rand_h, glob)

    outputs = lax.map(
        one_head,
        (
            q_heads.reshape(count, HD, length),
            k_heads.reshape(count, HD, length),
            v_heads.reshape(count, HD, length),
            random_blocks[0],
        ),
    )
    attended = lax.all_to_all(
        outputs.reshape(count * HD, length), "seq", split_axis=1, concat_axis=0, tiled=True
    )
    result = lax.dot_general(
        attended,
        lax.all_gather(out_weight, "dp", axis=0, tiled=True),
        (((0,), (0,)), ((), ())),
        preferred_element_type=jnp.float32,
    )
    return result.astype(jnp.bfloat16)[None]


def cut_kernel(n, feats, row, me_ref, q_ref, k_ref, v_ref, *rest):
    outs = rest[: n - 1]
    held, in_sems, out_sems = rest[n - 1 :]
    me = me_ref[0]
    order = range(n - 1, 0, -1)

    def read(k, i):
        start = pl.multiple_of(lax.rem(me + k, n) * feats + row, PAIR)
        src = (q_ref, k_ref, v_ref)[i]
        return pltpu.make_async_copy(
            src.at[0, pl.ds(start, PAIR), :], held.at[k - 1, i], in_sems.at[k - 1, i]
        )

    def write(k):
        return pltpu.make_async_copy(held.at[k - 1], outs[k - 1], out_sems.at[k - 1])

    for k in order:
        for i in range(3):
            read(k, i).start()
    for k in order:
        for i in range(3):
            read(k, i).wait()
        write(k).start()
    for k in order:
        write(k).wait()


def cut(n, row, me, queries, keys, values):
    feats = queries.shape[1] // n
    length = queries.shape[2]
    hbm = pl.BlockSpec(memory_space=pl.ANY)
    return pl.pallas_call(
        functools.partial(cut_kernel, n, feats, row),
        out_shape=[jax.ShapeDtypeStruct((3, PAIR, length), queries.dtype)] * (n - 1),
        in_specs=[pl.BlockSpec(memory_space=pltpu.SMEM), hbm, hbm, hbm],
        out_specs=[hbm] * (n - 1),
        scratch_shapes=[
            pltpu.VMEM((n - 1, 3, PAIR, length), queries.dtype),
            pltpu.SemaphoreType.DMA((n - 1, 3)),
            pltpu.SemaphoreType.DMA((n - 1,)),
        ],
        name="cut",
    )(me, queries, keys, values)


def swap_halves(x):
    return jnp.concatenate([x[:, BLK:], x[:, :BLK]], axis=1)


def attend_kernel(
    n, nblocks, feats, row, me_ref, rand_ref, glob_ref, pen_ref, q_ref, k_ref, v_ref, *rest
):
    parts, outs = rest[: n - 1], rest[n - 1 : 2 * n - 1]
    raw, kt, vv, ob, sg, in_sems, own_sems, out_sems = rest[2 * n - 1 :]
    me = me_ref[0]
    shard = raw.shape[3]
    per = shard // BLK
    tiles = shard // PAIR
    f32, bf16 = jnp.float32, jnp.bfloat16

    own = pl.multiple_of(me * feats + row, PAIR)
    arrivals = []
    for i, src in enumerate((q_ref, k_ref, v_ref)):
        copy = pltpu.make_async_copy(
            src.at[0, pl.ds(own, PAIR), :], raw.at[me, i], own_sems.at[i]
        )
        copy.start()
        arrivals.append(copy)
    for k in range(1, n):
        came = lax.rem(me - k + n, n)
        copy = pltpu.make_async_copy(parts[k - 1], raw.at[came], in_sems.at[k - 1])
        copy.start()
        arrivals.append(copy)
    for copy in arrivals:
        copy.wait()

    def prepare(s, carry):
        for t in range(tiles):
            lanes = slice(t * PAIR, (t + 1) * PAIR)
            first = pl.multiple_of(s * shard + t * PAIR, PAIR)
            kt[pl.ds(first, PAIR), :] = raw[s, 1, :, lanes].T
            v = raw[s, 2, :, lanes]
            vv[0, s * tiles + t] = v
            vv[1, s * tiles + t] = swap_halves(v)
        return carry

    lax.fori_loop(0, n, prepare, 0)

    low = lax.broadcasted_iota(jnp.int32, (BLK, PAIR), 1) < BLK
    zero = jnp.zeros((HD, PAIR), bf16)

    def queries_of(x, odd):
        y = swap_halves(x)
        a, b = (y, x) if odd else (x, y)
        return jnp.concatenate(
            [jnp.where(low, a[:HD], zero), jnp.where(low, zero, b[HD:])], axis=0
        )

    def key_rows(b):
        return kt[pl.ds(pl.multiple_of(b * BLK, BLK), BLK), :]

    def value_half(head, b, place):
        side = lax.rem(b + place, 2)
        return vv[side, lax.div(b, 2), head * HD : (head + 1) * HD, :]

    def finish(ot, total):
        t = (ot / total).astype(bf16).T
        return jnp.where(low, t[:BLK], t[BLK:])

    def sparse(j, qbd):
        shared = [jnp.maximum(j - 1, 0), j, jnp.minimum(j + 1, nblocks - 1), glob_ref[0], glob_ref[1]]
        cand = [
            shared + [rand_ref[(h * nblocks + j) * 3 + c] for c in range(3)] for h in range(2)
        ]
        k_rows = [key_rows(b) for b in shared]
        for c in range(5, 8):
            k_rows.append(jnp.where(low, key_rows(cand[0][c]), key_rows(cand[1][c])))
        scores = jnp.dot(jnp.concatenate(k_rows, axis=0), qbd, preferred_element_type=f32)
        top = jnp.max(scores, axis=0, keepdims=True) * EXP_SCALE
        shift = pen_ref[j] + top
        probs = [
            jnp.exp2(scores[c * BLK : (c + 1) * BLK] * EXP_SCALE - shift[c : c + 1])
            for c in range(8)
        ]
        total = functools.reduce(
            jnp.add, [jnp.sum(p, axis=0, keepdims=True) for p in probs]
        )
        pt = jnp.concatenate([p.astype(bf16) for p in probs], axis=0)
        vcat = []
        for c in range(0, 8, 2):
            vcat.append(
                jnp.concatenate(
                    [
                        jnp.where(
                            low, value_half(h, cand[h][c], 0), value_half(h, cand[h][c + 1], 1)
                        )
                        for h in range(2)
                    ],
                    axis=0,
                )
            )
        ot = jnp.dot(jnp.concatenate(vcat, axis=1), pt, preferred_element_type=f32)
        return finish(ot, total)

    def tile_of(i):
        s = lax.div(i, tiles)
        first = pl.multiple_of(lax.rem(i, tiles) * PAIR, PAIR)
        return s, first

    def two_blocks(i, carry):
        s, first = tile_of(i)
        x = raw[s, 0, :, pl.ds(first, PAIR)]
        a = sparse(2 * i, queries_of(x, False))
        b = sparse(2 * i + 1, queries_of(x, True))
        ob[s, pl.ds(first, PAIR), :] = jnp.concatenate([a, b], axis=0)
        return carry

    lax.fori_loop(0, nblocks // 2, two_blocks, 0)

    for g in range(2):
        block = glob_ref[g]
        s, first = tile_of(lax.div(block, 2))
        x = raw[s, 0, :, pl.ds(first, PAIR)]
        odd = lax.rem(block, 2)
        qbd = jnp.where(odd == 1, queries_of(x, True), queries_of(x, False))

        def scan_scores(t, top):
            rows = pl.ds(pl.multiple_of(t * shard, shard), shard)
            scores = jnp.dot(kt[rows, :], qbd, preferred_element_type=f32)
            sg[rows, :] = scores
            return jnp.maximum(top, jnp.max(scores, axis=0, keepdims=True))

        top = lax.fori_loop(0, n, scan_scores, jnp.full((1, PAIR), -jnp.inf, f32))
        top = top * EXP_SCALE

        def scan_values(t, carry):
            total, ot = carry
            rows = pl.ds(pl.multiple_of(t * shard, shard), shard)
            p = jnp.exp2(sg[rows, :] * EXP_SCALE - top)
            total = total + jnp.sum(p, axis=0, keepdims=True)
            ot = ot + jnp.dot(raw[t, 2], p.astype(bf16), preferred_element_type=f32)
            return total, ot

        total, ot = lax.fori_loop(
            0, n, scan_values, (jnp.zeros((1, PAIR), f32), jnp.zeros((PAIR, PAIR), f32))
        )
        place = pl.multiple_of(lax.rem(block, per) * BLK, BLK)
        ob[s, pl.ds(place, BLK), :] = finish(ot, total)

    leaving = []
    for k in range(n):
        to = lax.rem(me + k, n)
        copy = pltpu.make_async_copy(ob.at[to], outs[k], out_sems.at[k])
        copy.start()
        leaving.append(copy)
    for copy in leaving:
        copy.wait()


def attend(n, row, me, rand, glob, pen, queries, keys, values, parts):
    feats = queries.shape[1] // n
    shard = queries.shape[2]
    length = n * shard
    nblocks = length // BLK
    hbm = pl.BlockSpec(memory_space=pl.ANY)
    smem = pl.BlockSpec(memory_space=pltpu.SMEM)
    vmem = pl.BlockSpec(memory_space=pltpu.VMEM)
    return pl.pallas_call(
        functools.partial(attend_kernel, n, nblocks, feats, row),
        out_shape=[jax.ShapeDtypeStruct((shard, PAIR), jnp.bfloat16)] * n,
        in_specs=[smem, smem, smem, vmem, hbm, hbm, hbm] + [hbm] * (n - 1),
        out_specs=[hbm] * n,
        scratch_shapes=[
            pltpu.VMEM((n, 3, PAIR, shard), jnp.bfloat16),
            pltpu.VMEM((length, PAIR), jnp.bfloat16),
            pltpu.VMEM((2, nblocks // 2, PAIR, PAIR), jnp.bfloat16),
            pltpu.VMEM((n, shard, PAIR), jnp.bfloat16),
            pltpu.VMEM((length, PAIR), jnp.float32),
            pltpu.SemaphoreType.DMA((n - 1,)),
            pltpu.SemaphoreType.DMA((3,)),
            pltpu.SemaphoreType.DMA((n,)),
        ],
        compiler_params=pltpu.CompilerParams(vmem_limit_bytes=40 * 1024 * 1024),
        cost_estimate=pl.CostEstimate(
            flops=20_000_000_000, bytes_accessed=4_000_000, transcendentals=0
        ),
        name="attend",
    )(me, rand, glob, pen, queries, keys, values, *parts)


def project_kernel(n, pairs, me_ref, *rest):
    pieces, w_ref, o_ref, a = rest[: n * pairs], rest[-3], rest[-2], rest[-1]
    me = me_ref[0]

    @pl.when(pl.program_id(0) == 0)
    def _():
        for p in range(pairs):
            for k in range(n):
                came = lax.rem(me - k + n, n)
                first = pl.multiple_of((came * pairs + p) * PAIR, PAIR)
                a[:, pl.ds(first, PAIR)] = pieces[p * n + k][...]

    o_ref[0] = jnp.dot(a[...], w_ref[...], preferred_element_type=jnp.float32).astype(o_ref.dtype)


def project(n, me, pieces, weight):
    pairs = len(pieces) // n
    shard = pieces[0].shape[0]
    depth, width = weight.shape
    tile = 256
    piece = pl.BlockSpec((shard, PAIR), lambda i: (0, 0))
    return pl.pallas_call(
        functools.partial(project_kernel, n, pairs),
        grid=(width // tile,),
        out_shape=jax.ShapeDtypeStruct((1, shard, width), jnp.bfloat16),
        in_specs=[pl.BlockSpec(memory_space=pltpu.SMEM)]
        + [piece] * (n * pairs)
        + [pl.BlockSpec((depth, tile), lambda i: (0, i))],
        out_specs=pl.BlockSpec((1, shard, tile), lambda i: (0, 0, i)),
        scratch_shapes=[pltpu.VMEM((shard, depth), jnp.bfloat16)],
        compiler_params=pltpu.CompilerParams(vmem_limit_bytes=40 * 1024 * 1024),
        name="project",
    )(me, *pieces, weight)


def local_paired(n, queries, keys, values, random_blocks, global_blocks, out_weight):
    me = lax.axis_index("seq").astype(jnp.int32)[None]
    feats = queries.shape[1] // n
    length = queries.shape[2] * n
    nblocks = length // BLK
    pairs = feats // PAIR
    glob = global_blocks[0]
    weight = lax.all_gather(out_weight, "dp", axis=0, tiled=True)

    def turn(x, k):
        return lax.ppermute(x, "seq", [(i, (i + k) % n) for i in range(n)])

    valid = jax.vmap(lambda r: candidate_blocks(nblocks, glob, r)[1])(random_blocks[0])
    pen = jnp.where(valid, 0.0, BIG).astype(jnp.float32)

    arrived = []
    for p in range(pairs):
        sent = cut(n, p * PAIR, me, queries, keys, values)
        arrived.append([turn(sent[k - 1], k) for k in range(1, n)])
    pieces = []
    for p in range(pairs):
        rand = random_blocks[0, 2 * p : 2 * p + 2].reshape(-1)
        lanes = jnp.repeat(jnp.transpose(pen[2 * p : 2 * p + 2], (1, 2, 0)), HD, axis=2)
        outs = attend(n, p * PAIR, me, rand, glob, lanes, queries, keys, values, arrived[p])
        pieces.append(outs[0])
        pieces.extend(turn(outs[k], k) for k in range(1, n))
    return project(n, me, pieces, weight)


def solution(mesh):
    n = mesh.shape["seq"]
    in_specs = (
        P("dp", None, "seq"),
        P("dp", None, "seq"),
        P("dp", None, "seq"),
        P("dp", "seq", None, None),
        P("dp", None),
        P("dp", None),
    )
    out_specs = P("dp", "seq", None)

    def local(queries, keys, *rest):
        feats, shard = queries.shape[1] // n, queries.shape[2]
        paired = feats % PAIR == 0 and shard % PAIR == 0
        body = functools.partial(local_paired, n) if paired else local_plain
        return body(queries, keys, *rest)

    return jax.shard_map(local, mesh=mesh, in_specs=in_specs, out_specs=out_specs, check_vma=False)
```

```python
import functools
import math

import jax
import jax.numpy as jnp
from jax import lax
from jax.experimental import pallas as pl
from jax.experimental.pallas import tpu as pltpu
from jax.sharding import PartitionSpec as P

HD = 64
BLK = 64
PAIR = 2 * HD
EXP_SCALE = HD ** (-0.5) * math.log2(math.e)
BIG = 1e30
APART_IN = (False, True)
APART_OUT = (False, True)


def candidate_blocks(nblocks, glob, rand_h):
    rows = jnp.arange(nblocks, dtype=jnp.int32)
    window = jnp.stack([rows - 1, rows, rows + 1], axis=1)
    globs = jnp.broadcast_to(glob[None, :], (nblocks, glob.shape[0]))
    cand = jnp.concatenate([window, globs, rand_h], axis=1)
    inside = (cand >= 0) & (cand < nblocks)
    width = cand.shape[1]
    equal = cand[:, :, None] == cand[:, None, :]
    earlier = jnp.arange(width)[None, :] < jnp.arange(width)[:, None]
    repeated = jnp.any(equal & earlier[None, :, :], axis=2)
    return (jnp.clip(cand, 0, nblocks - 1), inside & ~repeated)


def head_attention(q_head, k_head, v_head, rand_h, glob):
    length = q_head.shape[1]
    nblocks = length // BLK
    scale = HD ** (-0.5)
    qb = q_head.reshape(HD, nblocks, BLK)
    kb = k_head.reshape(HD, nblocks, BLK)
    vb = v_head.reshape(HD, nblocks, BLK)
    index, valid = candidate_blocks(nblocks, glob, rand_h)
    group = math.gcd(nblocks, 32)
    turns = nblocks // group

    def one_group(turn):
        first = turn * group
        rows_index = lax.dynamic_slice_in_dim(index, first, group, 0)
        rows_valid = lax.dynamic_slice_in_dim(valid, first, group, 0)
        q_rows = lax.dynamic_slice_in_dim(qb, first, group, 1)
        k_rows = jnp.take(kb, rows_index, axis=1)
        v_rows = jnp.take(vb, rows_index, axis=1)
        scores = (
            jnp.einsum("dnq,dnck->nqck", q_rows, k_rows, preferred_element_type=jnp.float32) * scale
        )
        scores = jnp.where(rows_valid[:, None, :, None], scores, -jnp.inf)
        top = jnp.max(scores, axis=(2, 3), keepdims=True)
        expo = jnp.exp(scores - top)
        probs = (expo / jnp.sum(expo, axis=(2, 3), keepdims=True)).astype(jnp.bfloat16)
        return jnp.einsum(
            "nqck,dnck->dnq", probs, v_rows, preferred_element_type=jnp.float32
        ).astype(jnp.bfloat16)

    parts = lax.map(one_group, jnp.arange(turns, dtype=jnp.int32))
    blocks = jnp.transpose(parts, (1, 0, 2, 3)).reshape(HD, nblocks, BLK)
    qglob = jnp.take(qb, glob, axis=1)
    gscore = jnp.einsum("dgq,dk->gqk", qglob, k_head, preferred_element_type=jnp.float32) * scale
    gtop = jnp.max(gscore, axis=2, keepdims=True)
    gexp = jnp.exp(gscore - gtop)
    gprob = (gexp / jnp.sum(gexp, axis=2, keepdims=True)).astype(jnp.bfloat16)
    full = jnp.einsum("gqk,dk->dgq", gprob, v_head, preferred_element_type=jnp.float32).astype(
        jnp.bfloat16
    )
    blocks = blocks.at[:, glob, :].set(full)
    return blocks.reshape(HD, length)


def local_plain(queries, keys, values, random_blocks, global_blocks, out_weight):
    q_heads, k_heads, v_heads = (
        lax.all_to_all(queries[0], "seq", split_axis=0, concat_axis=1, tiled=True),
        lax.all_to_all(keys[0], "seq", split_axis=0, concat_axis=1, tiled=True),
        lax.all_to_all(values[0], "seq", split_axis=0, concat_axis=1, tiled=True),
    )
    count = q_heads.shape[0] // HD
    length = q_heads.shape[1]
    glob = global_blocks[0]

    def one_head(packed):
        q_head, k_head, v_head, rand_h = packed
        return head_attention(q_head, k_head, v_head, rand_h, glob)

    outputs = lax.map(
        one_head,
        (
            q_heads.reshape(count, HD, length),
            k_heads.reshape(count, HD, length),
            v_heads.reshape(count, HD, length),
            random_blocks[0],
        ),
    )
    attended = lax.all_to_all(
        outputs.reshape(count * HD, length), "seq", split_axis=1, concat_axis=0, tiled=True
    )
    result = lax.dot_general(
        attended,
        lax.all_gather(out_weight, "dp", axis=0, tiled=True),
        (((0,), (0,)), ((), ())),
        preferred_element_type=jnp.float32,
    )
    return result.astype(jnp.bfloat16)[None]


def cut_kernel(n, feats, row, q_ref, k_ref, v_ref, out, held, in_sems, out_sems):
    def read(to, i):
        src = (q_ref, k_ref, v_ref)[i]
        return pltpu.make_async_copy(
            src.at[0, pl.ds(to * feats + row, PAIR), :], held.at[to, i], in_sems.at[to, i]
        )

    def write(to):
        return pltpu.make_async_copy(held.at[to], out.at[to], out_sems.at[to])

    for to in range(n):
        for i in range(3):
            read(to, i).start()
    for to in range(n):
        for i in range(3):
            read(to, i).wait()
        write(to).start()
    for to in range(n):
        write(to).wait()


def cut(n, row, queries, keys, values):
    feats = queries.shape[1] // n
    length = queries.shape[2]
    hbm = pl.BlockSpec(memory_space=pl.ANY)
    return pl.pallas_call(
        functools.partial(cut_kernel, n, feats, row),
        out_shape=jax.ShapeDtypeStruct((n, 3, PAIR, length), queries.dtype),
        in_specs=[hbm, hbm, hbm],
        out_specs=hbm,
        scratch_shapes=[
            pltpu.VMEM((n, 3, PAIR, length), queries.dtype),
            pltpu.SemaphoreType.DMA((n, 3)),
            pltpu.SemaphoreType.DMA((n,)),
        ],
        name="cut",
    )(queries, keys, values)


def cut_apart_kernel(n, feats, row, me_ref, q_ref, k_ref, v_ref, *rest):
    outs = rest[: n - 1]
    held, in_sems, out_sems = rest[n - 1 :]
    me = me_ref[0]
    order = range(n - 1, 0, -1)

    def read(k, i):
        start = pl.multiple_of(lax.rem(me + k, n) * feats + row, PAIR)
        src = (q_ref, k_ref, v_ref)[i]
        return pltpu.make_async_copy(
            src.at[0, pl.ds(start, PAIR), :], held.at[k - 1, i], in_sems.at[k - 1, i]
        )

    def write(k):
        return pltpu.make_async_copy(held.at[k - 1], outs[k - 1], out_sems.at[k - 1])

    for k in order:
        for i in range(3):
            read(k, i).start()
    for k in order:
        for i in range(3):
            read(k, i).wait()
        write(k).start()
    for k in order:
        write(k).wait()


def cut_apart(n, row, me, queries, keys, values):
    feats = queries.shape[1] // n
    length = queries.shape[2]
    hbm = pl.BlockSpec(memory_space=pl.ANY)
    return pl.pallas_call(
        functools.partial(cut_apart_kernel, n, feats, row),
        out_shape=[jax.ShapeDtypeStruct((3, PAIR, length), queries.dtype)] * (n - 1),
        in_specs=[pl.BlockSpec(memory_space=pltpu.SMEM), hbm, hbm, hbm],
        out_specs=[hbm] * (n - 1),
        scratch_shapes=[
            pltpu.VMEM((n - 1, 3, PAIR, length), queries.dtype),
            pltpu.SemaphoreType.DMA((n - 1, 3)),
            pltpu.SemaphoreType.DMA((n - 1,)),
        ],
        name="cut_apart",
    )(me, queries, keys, values)


def swap_halves(x):
    return jnp.concatenate([x[:, BLK:], x[:, :BLK]], axis=1)


def attend_kernel(n, nblocks, feats, row, apart_in, apart_out, me_ref, rand_ref, glob_ref, *rest):
    pen_ref, rest = rest[0], rest[1:]
    ins, rest = (rest[: n + 2], rest[n + 2 :]) if apart_in else (rest[:1], rest[1:])
    outs, rest = (rest[:n], rest[n:]) if apart_out else (rest[:1], rest[1:])
    raw, kt, vv, ob, sg, own_sems, in_sems, out_sems = rest
    me = me_ref[0]
    shard = raw.shape[3]
    per = shard // BLK
    tiles = shard // PAIR
    f32, bf16 = jnp.float32, jnp.bfloat16

    arrivals = []
    if apart_in:
        own = pl.multiple_of(me * feats + row, PAIR)
        arrivals.append(
            (
                me,
                [
                    pltpu.make_async_copy(
                        ins[i].at[0, pl.ds(own, PAIR), :], raw.at[me, i], own_sems.at[i]
                    )
                    for i in range(3)
                ],
            )
        )
        for k in range(1, n):
            came = lax.rem(me - k + n, n)
            arrivals.append(
                (came, [pltpu.make_async_copy(ins[2 + k], raw.at[came], in_sems.at[k])])
            )
    else:
        for s in range(n):
            arrivals.append(
                (s, [pltpu.make_async_copy(ins[0].at[s], raw.at[s], in_sems.at[s])])
            )
    for _, copies in arrivals:
        for copy in copies:
            copy.start()

    for s, copies in arrivals:
        for copy in copies:
            copy.wait()
        for t in range(tiles):
            lanes = slice(t * PAIR, (t + 1) * PAIR)
            first = pl.multiple_of(s * shard + t * PAIR, PAIR)
            kt[pl.ds(first, PAIR), :] = raw[s, 1, :, lanes].T
            v = raw[s, 2, :, lanes]
            vv[0, s * tiles + t] = v
            vv[1, s * tiles + t] = swap_halves(v)

    low = lax.broadcasted_iota(jnp.int32, (BLK, PAIR), 1) < BLK
    zero = jnp.zeros((HD, PAIR), bf16)

    def queries_of(x, odd):
        y = swap_halves(x)
        a, b = (y, x) if odd else (x, y)
        return jnp.concatenate(
            [jnp.where(low, a[:HD], zero), jnp.where(low, zero, b[HD:])], axis=0
        )

    def key_rows(b):
        return kt[pl.ds(pl.multiple_of(b * BLK, BLK), BLK), :]

    def value_half(head, b, place):
        side = lax.rem(b + place, 2)
        return vv[side, lax.div(b, 2), head * HD : (head + 1) * HD, :]

    def finish(ot, total):
        t = (ot / total).astype(bf16).T
        return jnp.where(low, t[:BLK], t[BLK:])

    def sparse(j, qbd):
        shared = [jnp.maximum(j - 1, 0), j, jnp.minimum(j + 1, nblocks - 1), glob_ref[0], glob_ref[1]]
        cand = [
            shared + [rand_ref[(h * nblocks + j) * 3 + c] for c in range(3)] for h in range(2)
        ]
        k_rows = [key_rows(b) for b in shared]
        for c in range(5, 8):
            k_rows.append(jnp.where(low, key_rows(cand[0][c]), key_rows(cand[1][c])))
        scores = jnp.dot(jnp.concatenate(k_rows, axis=0), qbd, preferred_element_type=f32)
        top = jnp.max(scores, axis=0, keepdims=True) * EXP_SCALE
        pen = pen_ref[j]
        shift = jnp.where(low[:8], pen[:, 0:1], pen[:, 1:2]) + top
        probs = [
            jnp.exp2(scores[c * BLK : (c + 1) * BLK] * EXP_SCALE - shift[c : c + 1])
            for c in range(8)
        ]
        total = functools.reduce(
            jnp.add, [jnp.sum(p, axis=0, keepdims=True) for p in probs]
        )
        pt = jnp.concatenate([p.astype(bf16) for p in probs], axis=0)
        vcat = []
        for c in range(0, 8, 2):
            vcat.append(
                jnp.concatenate(
                    [
                        jnp.where(
                            low, value_half(h, cand[h][c], 0), value_half(h, cand[h][c + 1], 1)
                        )
                        for h in range(2)
                    ],
                    axis=0,
                )
            )
        ot = jnp.dot(jnp.concatenate(vcat, axis=1), pt, preferred_element_type=f32)
        return finish(ot, total)

    def tile_of(i):
        s = lax.div(i, tiles)
        first = pl.multiple_of(lax.rem(i, tiles) * PAIR, PAIR)
        return s, first

    def two_blocks(i, carry):
        s, first = tile_of(i)
        x = raw[s, 0, :, pl.ds(first, PAIR)]
        a = sparse(2 * i, queries_of(x, False))
        b = sparse(2 * i + 1, queries_of(x, True))
        ob[s, pl.ds(first, PAIR), :] = jnp.concatenate([a, b], axis=0)
        return carry

    lax.fori_loop(0, nblocks // 2, two_blocks, 0, unroll=8)

    places, columns = [], []
    for g in range(2):
        s, first = tile_of(lax.div(glob_ref[g], 2))
        x = raw[s, 0, :, pl.ds(first, PAIR)]
        odd = lax.rem(glob_ref[g], 2)
        columns.append(jnp.where(odd == 1, queries_of(x, True), queries_of(x, False)))
        places.append((s, pl.multiple_of(lax.rem(glob_ref[g], per) * BLK, BLK)))
    qbd = jnp.concatenate(columns, axis=1)
    top = jnp.full((1, 2 * PAIR), -jnp.inf, f32)
    for t in range(n):
        rows = slice(t * shard, (t + 1) * shard)
        scores = jnp.dot(kt[rows, :], qbd, preferred_element_type=f32)
        sg[rows, :] = scores
        top = jnp.maximum(top, jnp.max(scores, axis=0, keepdims=True))
    top = top * EXP_SCALE
    total = jnp.zeros((1, 2 * PAIR), f32)
    ot = jnp.zeros((PAIR, 2 * PAIR), f32)
    for t in range(n):
        p = jnp.exp2(sg[t * shard : (t + 1) * shard, :] * EXP_SCALE - top)
        total = total + jnp.sum(p, axis=0, keepdims=True)
        ot = ot + jnp.dot(raw[t, 2], p.astype(bf16), preferred_element_type=f32)
    for g, (s, place) in enumerate(places):
        lanes = slice(g * PAIR, (g + 1) * PAIR)
        ob[s, pl.ds(place, BLK), :] = finish(ot[:, lanes], total[:, lanes])

    if apart_out:
        leaving = [
            pltpu.make_async_copy(ob.at[lax.rem(me + k, n)], outs[k], out_sems.at[k])
            for k in range(n)
        ]
    else:
        leaving = [pltpu.make_async_copy(ob, outs[0], out_sems.at[0])]
    for copy in leaving:
        copy.start()
    for copy in leaving:
        copy.wait()


def attend(n, row, me, rand, glob, pen, arrays, feats, apart_out):
    apart_in = len(arrays) > 1
    shard = arrays[0].shape[-1]
    length = n * shard
    nblocks = length // BLK
    hbm = pl.BlockSpec(memory_space=pl.ANY)
    smem = pl.BlockSpec(memory_space=pltpu.SMEM)
    vmem = pl.BlockSpec(memory_space=pltpu.VMEM)
    if apart_out:
        out_shape = [jax.ShapeDtypeStruct((shard, PAIR), jnp.bfloat16)] * n
    else:
        out_shape = [jax.ShapeDtypeStruct((n, shard, PAIR), jnp.bfloat16)]
    return pl.pallas_call(
        functools.partial(attend_kernel, n, nblocks, feats, row, apart_in, apart_out),
        out_shape=out_shape,
        in_specs=[smem, smem, smem, vmem] + [hbm] * len(arrays),
        out_specs=[hbm] * len(out_shape),
        scratch_shapes=[
            pltpu.VMEM((n, 3, PAIR, shard), jnp.bfloat16),
            pltpu.VMEM((length, PAIR), jnp.bfloat16),
            pltpu.VMEM((2, nblocks // 2, PAIR, PAIR), jnp.bfloat16),
            pltpu.VMEM((n, shard, PAIR), jnp.bfloat16),
            pltpu.VMEM((length, 2 * PAIR), jnp.float32),
            pltpu.SemaphoreType.DMA((3,)),
            pltpu.SemaphoreType.DMA((n,)),
            pltpu.SemaphoreType.DMA((n,)),
        ],
        compiler_params=pltpu.CompilerParams(vmem_limit_bytes=32 * 1024 * 1024),
        cost_estimate=pl.CostEstimate(
            flops=15_000_000_000, bytes_accessed=4_000_000, transcendentals=0
        ),
        name="attend",
    )(me, rand, glob, pen, *arrays)


def project_kernel(n, count, before, me_ref, *rest):
    pieces, w_ref, rest = rest[:count], rest[count], rest[count + 1 :]
    o_ref, a = rest[-2], rest[-1]

    @pl.when(pl.program_id(0) == 0)
    def _():
        if count == 1:
            for s in range(n):
                a[:, s * PAIR : (s + 1) * PAIR] = pieces[0][s]
        else:
            for k in range(n):
                came = lax.rem(me_ref[0] - k + n, n)
                a[:, pl.ds(pl.multiple_of(came * PAIR, PAIR), PAIR)] = pieces[k][...]

    w = w_ref[...].reshape(a.shape[1], w_ref.shape[2])
    total = jnp.dot(a[...], w, preferred_element_type=jnp.float32)
    if before:
        total = total + rest[0][0]
    o_ref[0] = total.astype(o_ref.dtype)


def project(n, p, me, pieces, weight, before, dtype):
    shard = pieces[0].shape[-2]
    depth, width = weight.shape
    tile = 512
    rows = weight.reshape(n, depth // n // PAIR, PAIR, width)
    column = pl.BlockSpec((1, shard, tile), lambda i: (0, 0, i))
    return pl.pallas_call(
        functools.partial(project_kernel, n, len(pieces), before is not None),
        grid=(width // tile,),
        out_shape=jax.ShapeDtypeStruct((1, shard, width), dtype),
        in_specs=[pl.BlockSpec(memory_space=pltpu.SMEM)]
        + [pl.BlockSpec(x.shape, lambda i, r=x.ndim: (0,) * r) for x in pieces]
        + [pl.BlockSpec((n, None, PAIR, tile), lambda i: (0, p, 0, i))]
        + ([] if before is None else [column]),
        out_specs=column,
        scratch_shapes=[pltpu.VMEM((shard, n * PAIR), jnp.bfloat16)],
        compiler_params=pltpu.CompilerParams(vmem_limit_bytes=24 * 1024 * 1024),
        cost_estimate=pl.CostEstimate(
            flops=2 * shard * n * PAIR * width, bytes_accessed=10_000_000, transcendentals=0
        ),
        name="project",
    )(me, *pieces, rows, *([] if before is None else [before]))


def local_paired(n, queries, keys, values, random_blocks, global_blocks, out_weight):
    me = lax.axis_index("seq").astype(jnp.int32)[None]
    feats = queries.shape[1] // n
    length = queries.shape[2] * n
    nblocks = length // BLK
    pairs = feats // PAIR
    glob = global_blocks[0]
    weight = lax.all_gather(out_weight, "dp", axis=0, tiled=True)

    def exchange(x):
        return lax.all_to_all(x, "seq", split_axis=0, concat_axis=0, tiled=True)

    def turn(x, k):
        return lax.ppermute(x, "seq", [(i, (i + k) % n) for i in range(n)])

    valid = jax.vmap(lambda r: candidate_blocks(nblocks, glob, r)[1])(random_blocks[0])
    pen = jnp.where(valid, 0.0, BIG).astype(jnp.float32)
    pen = jnp.transpose(pen.reshape(pairs, 2, nblocks, -1), (0, 2, 3, 1))
    rand = random_blocks[0].reshape(pairs, -1)

    arrived = []
    for p in range(pairs):
        if APART_IN[p % 2]:
            sent = cut_apart(n, p * PAIR, me, queries, keys, values)
            got = [turn(sent[k - 1], k) for k in range(1, n)]
            arrived.append([queries, keys, values] + got)
        else:
            arrived.append([exchange(cut(n, p * PAIR, queries, keys, values))])
    total = None
    for p in range(pairs):
        apart = APART_OUT[p % 2]
        outs = attend(n, p * PAIR, me, rand[p], glob, pen[p], arrived[p], feats, apart)
        if apart:
            pieces = [outs[0]] + [turn(outs[k], k) for k in range(1, n)]
        else:
            pieces = [exchange(outs[0])]
        dtype = jnp.bfloat16 if p == pairs - 1 else jnp.float32
        total = project(n, p, me, pieces, weight, total, dtype)
    return total


def solution(mesh):
    n = mesh.shape["seq"]
    in_specs = (
        P("dp", None, "seq"),
        P("dp", None, "seq"),
        P("dp", None, "seq"),
        P("dp", "seq", None, None),
        P("dp", None),
        P("dp", None),
    )
    out_specs = P("dp", "seq", None)

    def local(queries, keys, *rest):
        feats, shard = queries.shape[1] // n, queries.shape[2]
        paired = feats % PAIR == 0 and shard % PAIR == 0
        body = functools.partial(local_paired, n) if paired else local_plain
        return body(queries, keys, *rest)

    return jax.shard_map(local, mesh=mesh, in_specs=in_specs, out_specs=out_specs, check_vma=False)
```

```python
import functools
import math

import jax
import jax.numpy as jnp
from jax import lax
from jax.experimental import pallas as pl
from jax.experimental.pallas import tpu as pltpu
from jax.sharding import PartitionSpec as P

HD = 64
BLK = 64
PAIR = 2 * HD
EXP_SCALE = HD ** (-0.5) * math.log2(math.e)
BIG = 1e30
APART_IN = (False, True)
APART_OUT = (False, True)


def candidate_blocks(nblocks, glob, rand_h):
    rows = jnp.arange(nblocks, dtype=jnp.int32)
    window = jnp.stack([rows - 1, rows, rows + 1], axis=1)
    globs = jnp.broadcast_to(glob[None, :], (nblocks, glob.shape[0]))
    cand = jnp.concatenate([window, globs, rand_h], axis=1)
    inside = (cand >= 0) & (cand < nblocks)
    width = cand.shape[1]
    equal = cand[:, :, None] == cand[:, None, :]
    earlier = jnp.arange(width)[None, :] < jnp.arange(width)[:, None]
    repeated = jnp.any(equal & earlier[None, :, :], axis=2)
    return (jnp.clip(cand, 0, nblocks - 1), inside & ~repeated)


def head_attention(q_head, k_head, v_head, rand_h, glob):
    length = q_head.shape[1]
    nblocks = length // BLK
    scale = HD ** (-0.5)
    qb = q_head.reshape(HD, nblocks, BLK)
    kb = k_head.reshape(HD, nblocks, BLK)
    vb = v_head.reshape(HD, nblocks, BLK)
    index, valid = candidate_blocks(nblocks, glob, rand_h)
    group = math.gcd(nblocks, 32)
    turns = nblocks // group

    def one_group(turn):
        first = turn * group
        rows_index = lax.dynamic_slice_in_dim(index, first, group, 0)
        rows_valid = lax.dynamic_slice_in_dim(valid, first, group, 0)
        q_rows = lax.dynamic_slice_in_dim(qb, first, group, 1)
        k_rows = jnp.take(kb, rows_index, axis=1)
        v_rows = jnp.take(vb, rows_index, axis=1)
        scores = (
            jnp.einsum("dnq,dnck->nqck", q_rows, k_rows, preferred_element_type=jnp.float32) * scale
        )
        scores = jnp.where(rows_valid[:, None, :, None], scores, -jnp.inf)
        top = jnp.max(scores, axis=(2, 3), keepdims=True)
        expo = jnp.exp(scores - top)
        probs = (expo / jnp.sum(expo, axis=(2, 3), keepdims=True)).astype(jnp.bfloat16)
        return jnp.einsum(
            "nqck,dnck->dnq", probs, v_rows, preferred_element_type=jnp.float32
        ).astype(jnp.bfloat16)

    parts = lax.map(one_group, jnp.arange(turns, dtype=jnp.int32))
    blocks = jnp.transpose(parts, (1, 0, 2, 3)).reshape(HD, nblocks, BLK)
    qglob = jnp.take(qb, glob, axis=1)
    gscore = jnp.einsum("dgq,dk->gqk", qglob, k_head, preferred_element_type=jnp.float32) * scale
    gtop = jnp.max(gscore, axis=2, keepdims=True)
    gexp = jnp.exp(gscore - gtop)
    gprob = (gexp / jnp.sum(gexp, axis=2, keepdims=True)).astype(jnp.bfloat16)
    full = jnp.einsum("gqk,dk->dgq", gprob, v_head, preferred_element_type=jnp.float32).astype(
        jnp.bfloat16
    )
    blocks = blocks.at[:, glob, :].set(full)
    return blocks.reshape(HD, length)


def local_plain(queries, keys, values, random_blocks, global_blocks, out_weight):
    q_heads, k_heads, v_heads = (
        lax.all_to_all(queries[0], "seq", split_axis=0, concat_axis=1, tiled=True),
        lax.all_to_all(keys[0], "seq", split_axis=0, concat_axis=1, tiled=True),
        lax.all_to_all(values[0], "seq", split_axis=0, concat_axis=1, tiled=True),
    )
    count = q_heads.shape[0] // HD
    length = q_heads.shape[1]
    glob = global_blocks[0]

    def one_head(packed):
        q_head, k_head, v_head, rand_h = packed
        return head_attention(q_head, k_head, v_head, rand_h, glob)

    outputs = lax.map(
        one_head,
        (
            q_heads.reshape(count, HD, length),
            k_heads.reshape(count, HD, length),
            v_heads.reshape(count, HD, length),
            random_blocks[0],
        ),
    )
    attended = lax.all_to_all(
        outputs.reshape(count * HD, length), "seq", split_axis=1, concat_axis=0, tiled=True
    )
    result = lax.dot_general(
        attended,
        lax.all_gather(out_weight, "dp", axis=0, tiled=True),
        (((0,), (0,)), ((), ())),
        preferred_element_type=jnp.float32,
    )
    return result.astype(jnp.bfloat16)[None]


def cut_kernel(n, feats, row, q_ref, k_ref, v_ref, out, held, in_sems, out_sems):
    def read(to, i):
        src = (q_ref, k_ref, v_ref)[i]
        return pltpu.make_async_copy(
            src.at[0, pl.ds(to * feats + row, PAIR), :], held.at[to, i], in_sems.at[to, i]
        )

    def write(to):
        return pltpu.make_async_copy(held.at[to], out.at[to], out_sems.at[to])

    for to in range(n):
        for i in range(3):
            read(to, i).start()
    for to in range(n):
        for i in range(3):
            read(to, i).wait()
        write(to).start()
    for to in range(n):
        write(to).wait()


def cut(n, row, queries, keys, values):
    feats = queries.shape[1] // n
    length = queries.shape[2]
    hbm = pl.BlockSpec(memory_space=pl.ANY)
    return pl.pallas_call(
        functools.partial(cut_kernel, n, feats, row),
        out_shape=jax.ShapeDtypeStruct((n, 3, PAIR, length), queries.dtype),
        in_specs=[hbm, hbm, hbm],
        out_specs=hbm,
        scratch_shapes=[
            pltpu.VMEM((n, 3, PAIR, length), queries.dtype),
            pltpu.SemaphoreType.DMA((n, 3)),
            pltpu.SemaphoreType.DMA((n,)),
        ],
        name="cut",
    )(queries, keys, values)


def cut_apart_kernel(n, feats, row, me_ref, q_ref, k_ref, v_ref, *rest):
    outs = rest[: n - 1]
    held, in_sems, out_sems = rest[n - 1 :]
    me = me_ref[0]
    order = range(n - 1, 0, -1)

    def read(k, i):
        start = pl.multiple_of((me ^ k) * feats + row, PAIR)
        src = (q_ref, k_ref, v_ref)[i]
        return pltpu.make_async_copy(
            src.at[0, pl.ds(start, PAIR), :], held.at[k - 1, i], in_sems.at[k - 1, i]
        )

    def write(k):
        return pltpu.make_async_copy(held.at[k - 1], outs[k - 1], out_sems.at[k - 1])

    for k in order:
        for i in range(3):
            read(k, i).start()
    for k in order:
        for i in range(3):
            read(k, i).wait()
        write(k).start()
    for k in order:
        write(k).wait()


def cut_apart(n, row, me, queries, keys, values):
    feats = queries.shape[1] // n
    length = queries.shape[2]
    hbm = pl.BlockSpec(memory_space=pl.ANY)
    return pl.pallas_call(
        functools.partial(cut_apart_kernel, n, feats, row),
        out_shape=[jax.ShapeDtypeStruct((3, PAIR, length), queries.dtype)] * (n - 1),
        in_specs=[pl.BlockSpec(memory_space=pltpu.SMEM), hbm, hbm, hbm],
        out_specs=[hbm] * (n - 1),
        scratch_shapes=[
            pltpu.VMEM((n - 1, 3, PAIR, length), queries.dtype),
            pltpu.SemaphoreType.DMA((n - 1, 3)),
            pltpu.SemaphoreType.DMA((n - 1,)),
        ],
        name="cut_apart",
    )(me, queries, keys, values)


def swap_halves(x):
    return jnp.concatenate([x[:, BLK:], x[:, :BLK]], axis=1)


def attend_kernel(n, nblocks, feats, row, apart_in, apart_out, me_ref, rand_ref, glob_ref, *rest):
    pen_ref, rest = rest[0], rest[1:]
    ins, rest = (rest[: n + 2], rest[n + 2 :]) if apart_in else (rest[:1], rest[1:])
    outs, rest = (rest[:n], rest[n:]) if apart_out else (rest[:1], rest[1:])
    raw, kt, vv, ob, sg, own_sems, in_sems, out_sems = rest
    me = me_ref[0]
    shard = raw.shape[3]
    per = shard // BLK
    tiles = shard // PAIR
    f32, bf16 = jnp.float32, jnp.bfloat16

    arrivals = []
    if apart_in:
        own = pl.multiple_of(me * feats + row, PAIR)
        arrivals.append(
            (
                me,
                [
                    pltpu.make_async_copy(
                        ins[i].at[0, pl.ds(own, PAIR), :], raw.at[me, i], own_sems.at[i]
                    )
                    for i in range(3)
                ],
            )
        )
        for k in range(1, n):
            came = me ^ k
            arrivals.append(
                (came, [pltpu.make_async_copy(ins[2 + k], raw.at[came], in_sems.at[k])])
            )
    else:
        for s in range(n):
            arrivals.append(
                (s, [pltpu.make_async_copy(ins[0].at[s], raw.at[s], in_sems.at[s])])
            )
    for _, copies in arrivals:
        for copy in copies:
            copy.start()

    for s, copies in arrivals:
        for copy in copies:
            copy.wait()
        for t in range(tiles):
            lanes = slice(t * PAIR, (t + 1) * PAIR)
            first = pl.multiple_of(s * shard + t * PAIR, PAIR)
            kt[pl.ds(first, PAIR), :] = raw[s, 1, :, lanes].T
            v = raw[s, 2, :, lanes]
            vv[0, s * tiles + t] = v
            vv[1, s * tiles + t] = swap_halves(v)

    low = lax.broadcasted_iota(jnp.int32, (BLK, PAIR), 1) < BLK
    zero = jnp.zeros((HD, PAIR), bf16)

    def queries_of(x, odd):
        y = swap_halves(x)
        a, b = (y, x) if odd else (x, y)
        return jnp.concatenate(
            [jnp.where(low, a[:HD], zero), jnp.where(low, zero, b[HD:])], axis=0
        )

    def key_rows(b):
        return kt[pl.ds(pl.multiple_of(b * BLK, BLK), BLK), :]

    def value_half(head, b, place):
        side = lax.rem(b + place, 2)
        return vv[side, lax.div(b, 2), head * HD : (head + 1) * HD, :]

    def finish(ot, total):
        t = (ot / total).astype(bf16).T
        return jnp.where(low, t[:BLK], t[BLK:])

    def sparse(j, qbd):
        shared = [jnp.maximum(j - 1, 0), j, jnp.minimum(j + 1, nblocks - 1), glob_ref[0], glob_ref[1]]
        cand = [
            shared + [rand_ref[(h * nblocks + j) * 3 + c] for c in range(3)] for h in range(2)
        ]
        k_rows = [key_rows(b) for b in shared]
        for c in range(5, 8):
            k_rows.append(jnp.where(low, key_rows(cand[0][c]), key_rows(cand[1][c])))
        scores = jnp.dot(jnp.concatenate(k_rows, axis=0), qbd, preferred_element_type=f32)
        top = jnp.max(scores, axis=0, keepdims=True) * EXP_SCALE
        pen = pen_ref[j]
        shift = jnp.where(low[:8], pen[:, 0:1], pen[:, 1:2]) + top
        probs = [
            jnp.exp2(scores[c * BLK : (c + 1) * BLK] * EXP_SCALE - shift[c : c + 1])
            for c in range(8)
        ]
        total = functools.reduce(
            jnp.add, [jnp.sum(p, axis=0, keepdims=True) for p in probs]
        )
        pt = jnp.concatenate([p.astype(bf16) for p in probs], axis=0)
        vcat = []
        for c in range(0, 8, 2):
            vcat.append(
                jnp.concatenate(
                    [
                        jnp.where(
                            low, value_half(h, cand[h][c], 0), value_half(h, cand[h][c + 1], 1)
                        )
                        for h in range(2)
                    ],
                    axis=0,
                )
            )
        ot = jnp.dot(jnp.concatenate(vcat, axis=1), pt, preferred_element_type=f32)
        return finish(ot, total)

    def tile_of(i):
        s = lax.div(i, tiles)
        first = pl.multiple_of(lax.rem(i, tiles) * PAIR, PAIR)
        return s, first

    def two_blocks(i, carry):
        s, first = tile_of(i)
        x = raw[s, 0, :, pl.ds(first, PAIR)]
        a = sparse(2 * i, queries_of(x, False))
        b = sparse(2 * i + 1, queries_of(x, True))
        ob[s, pl.ds(first, PAIR), :] = jnp.concatenate([a, b], axis=0)
        return carry

    lax.fori_loop(0, nblocks // 2, two_blocks, 0, unroll=8)

    places, columns = [], []
    for g in range(2):
        s, first = tile_of(lax.div(glob_ref[g], 2))
        x = raw[s, 0, :, pl.ds(first, PAIR)]
        odd = lax.rem(glob_ref[g], 2)
        columns.append(jnp.where(odd == 1, queries_of(x, True), queries_of(x, False)))
        places.append((s, pl.multiple_of(lax.rem(glob_ref[g], per) * BLK, BLK)))
    qbd = jnp.concatenate(columns, axis=1)
    top = jnp.full((1, 2 * PAIR), -jnp.inf, f32)
    for t in range(n):
        rows = slice(t * shard, (t + 1) * shard)
        scores = jnp.dot(kt[rows, :], qbd, preferred_element_type=f32)
        sg[rows, :] = scores
        top = jnp.maximum(top, jnp.max(scores, axis=0, keepdims=True))
    top = top * EXP_SCALE
    total = jnp.zeros((1, 2 * PAIR), f32)
    ot = jnp.zeros((PAIR, 2 * PAIR), f32)
    for t in range(n):
        p = jnp.exp2(sg[t * shard : (t + 1) * shard, :] * EXP_SCALE - top)
        total = total + jnp.sum(p, axis=0, keepdims=True)
        ot = ot + jnp.dot(raw[t, 2], p.astype(bf16), preferred_element_type=f32)
    for g, (s, place) in enumerate(places):
        lanes = slice(g * PAIR, (g + 1) * PAIR)
        ob[s, pl.ds(place, BLK), :] = finish(ot[:, lanes], total[:, lanes])

    if apart_out:
        leaving = [
            pltpu.make_async_copy(ob.at[me ^ k], outs[k], out_sems.at[k])
            for k in range(n)
        ]
    else:
        leaving = [pltpu.make_async_copy(ob, outs[0], out_sems.at[0])]
    for copy in leaving:
        copy.start()
    for copy in leaving:
        copy.wait()


def attend(n, row, me, rand, glob, pen, arrays, feats, apart_out):
    apart_in = len(arrays) > 1
    shard = arrays[0].shape[-1]
    length = n * shard
    nblocks = length // BLK
    hbm = pl.BlockSpec(memory_space=pl.ANY)
    smem = pl.BlockSpec(memory_space=pltpu.SMEM)
    vmem = pl.BlockSpec(memory_space=pltpu.VMEM)
    if apart_out:
        out_shape = [jax.ShapeDtypeStruct((shard, PAIR), jnp.bfloat16)] * n
    else:
        out_shape = [jax.ShapeDtypeStruct((n, shard, PAIR), jnp.bfloat16)]
    return pl.pallas_call(
        functools.partial(attend_kernel, n, nblocks, feats, row, apart_in, apart_out),
        out_shape=out_shape,
        in_specs=[smem, smem, smem, vmem] + [hbm] * len(arrays),
        out_specs=[hbm] * len(out_shape),
        scratch_shapes=[
            pltpu.VMEM((n, 3, PAIR, shard), jnp.bfloat16),
            pltpu.VMEM((length, PAIR), jnp.bfloat16),
            pltpu.VMEM((2, nblocks // 2, PAIR, PAIR), jnp.bfloat16),
            pltpu.VMEM((n, shard, PAIR), jnp.bfloat16),
            pltpu.VMEM((length, 2 * PAIR), jnp.float32),
            pltpu.SemaphoreType.DMA((3,)),
            pltpu.SemaphoreType.DMA((n,)),
            pltpu.SemaphoreType.DMA((n,)),
        ],
        compiler_params=pltpu.CompilerParams(vmem_limit_bytes=32 * 1024 * 1024),
        cost_estimate=pl.CostEstimate(
            flops=15_000_000_000, bytes_accessed=4_000_000, transcendentals=0
        ),
        name="attend",
    )(me, rand, glob, pen, *arrays)


def project_kernel(n, ndp, count, before, me_ref, *rest):
    pieces, rest = rest[:count], rest[count:]
    weights, rest = rest[:ndp], rest[ndp:]
    o_ref, a = rest[-2], rest[-1]
    held = n // ndp

    @pl.when(pl.program_id(0) == 0)
    def _():
        if count == 1:
            for r in range(ndp):
                for u in range(held):
                    first = (r * held + u) * PAIR
                    a[:, first : first + PAIR] = pieces[0][(me_ref[1] ^ r) * held + u]
        else:
            for k in range(n):
                came = me_ref[0] ^ k
                place = (lax.div(came, held) ^ me_ref[1]) * held + lax.rem(came, held)
                a[:, pl.ds(pl.multiple_of(place * PAIR, PAIR), PAIR)] = pieces[k][...]

    w = jnp.concatenate([w_ref[...].reshape(held * PAIR, -1) for w_ref in weights], axis=0)
    total = jnp.dot(a[...], w, preferred_element_type=jnp.float32)
    if before:
        total = total + rest[0][0]
    o_ref[0] = total.astype(o_ref.dtype)


def project(n, p, me, pieces, weights, before, dtype):
    shard = pieces[0].shape[-2]
    ndp = len(weights)
    depth, width = weights[0].shape
    held = n // ndp
    tile = 512
    rows = [w.reshape(held, depth // held // PAIR, PAIR, width) for w in weights]
    column = pl.BlockSpec((1, shard, tile), lambda i: (0, 0, i))
    return pl.pallas_call(
        functools.partial(project_kernel, n, ndp, len(pieces), before is not None),
        grid=(width // tile,),
        out_shape=jax.ShapeDtypeStruct((1, shard, width), dtype),
        in_specs=[pl.BlockSpec(memory_space=pltpu.SMEM)]
        + [pl.BlockSpec(x.shape, lambda i, r=x.ndim: (0,) * r) for x in pieces]
        + [pl.BlockSpec((held, None, PAIR, tile), lambda i: (0, p, 0, i))] * ndp
        + ([] if before is None else [column]),
        out_specs=column,
        scratch_shapes=[pltpu.VMEM((shard, n * PAIR), jnp.bfloat16)],
        compiler_params=pltpu.CompilerParams(vmem_limit_bytes=24 * 1024 * 1024),
        cost_estimate=pl.CostEstimate(
            flops=2 * shard * n * PAIR * width, bytes_accessed=10_000_000, transcendentals=0
        ),
        name="project",
    )(me, *pieces, *rows, *([] if before is None else [before]))


def gather_weight(ndp, weight):
    parts = {0: weight}
    bit = ndp // 2
    while bit:
        for r in list(parts):
            parts[r + bit] = lax.ppermute(parts[r], "dp", [(i, i ^ bit) for i in range(ndp)])
        bit //= 2
    return [parts[r] for r in range(ndp)]


def local_paired(n, ndp, queries, keys, values, random_blocks, global_blocks, out_weight):
    me = jnp.stack([lax.axis_index("seq"), lax.axis_index("dp")]).astype(jnp.int32)
    feats = queries.shape[1] // n
    length = queries.shape[2] * n
    nblocks = length // BLK
    pairs = feats // PAIR
    glob = global_blocks[0]

    def exchange(x):
        return lax.all_to_all(x, "seq", split_axis=0, concat_axis=0, tiled=True)

    def swap(arrays, order):
        got = {k: lax.ppermute(arrays[k - 1], "seq", [(i, i ^ k) for i in range(n)]) for k in order}
        return [got[k] for k in range(1, n)]

    near, far = list(range(1, n // 2)), list(range(n // 2, n))

    valid = jax.vmap(lambda r: candidate_blocks(nblocks, glob, r)[1])(random_blocks[0])
    pen = jnp.where(valid, 0.0, BIG).astype(jnp.float32)
    pen = jnp.transpose(pen.reshape(pairs, 2, nblocks, -1), (0, 2, 3, 1))
    rand = random_blocks[0].reshape(pairs, -1)

    arrived = []
    for p in range(pairs):
        if APART_IN[p % 2]:
            sent = cut_apart(n, p * PAIR, me, queries, keys, values)
            arrived.append([queries, keys, values] + swap(sent, near + far))
        else:
            arrived.append([exchange(cut(n, p * PAIR, queries, keys, values))])
    weights = gather_weight(ndp, lax.optimization_barrier((out_weight, arrived[1][3]))[0])
    total = None
    for p in range(pairs):
        apart = APART_OUT[p % 2]
        outs = attend(n, p * PAIR, me, rand[p], glob, pen[p], arrived[p], feats, apart)
        if apart:
            pieces = [outs[0]] + swap(outs[1:], far + near)
        else:
            pieces = [exchange(outs[0])]
        dtype = jnp.bfloat16 if p == pairs - 1 else jnp.float32
        total = project(n, p, me, pieces, weights, total, dtype)
    return total


def solution(mesh):
    n, ndp = mesh.shape["seq"], mesh.shape["dp"]
    in_specs = (
        P("dp", None, "seq"),
        P("dp", None, "seq"),
        P("dp", None, "seq"),
        P("dp", "seq", None, None),
        P("dp", None),
        P("dp", None),
    )
    out_specs = P("dp", "seq", None)

    def local(queries, keys, *rest):
        feats, shard = queries.shape[1] // n, queries.shape[2]
        paired = feats % PAIR == 0 and shard % PAIR == 0 and n % ndp == 0
        paired = paired and n & (n - 1) == 0 and ndp & (ndp - 1) == 0
        body = functools.partial(local_paired, n, ndp) if paired else local_plain
        return body(queries, keys, *rest)

    return jax.shard_map(local, mesh=mesh, in_specs=in_specs, out_specs=out_specs, check_vma=False)
```

```python
import functools
import math

import jax
import jax.numpy as jnp
from jax import lax
from jax.experimental import pallas as pl
from jax.experimental.pallas import tpu as pltpu
from jax.sharding import PartitionSpec as P

HD = 64
BLK = 64
PAIR = 2 * HD
EXP_SCALE = HD ** (-0.5) * math.log2(math.e)
BIG = 1e30


def candidate_blocks(nblocks, glob, rand_h):
    rows = jnp.arange(nblocks, dtype=jnp.int32)
    window = jnp.stack([rows - 1, rows, rows + 1], axis=1)
    globs = jnp.broadcast_to(glob[None, :], (nblocks, glob.shape[0]))
    cand = jnp.concatenate([window, globs, rand_h], axis=1)
    inside = (cand >= 0) & (cand < nblocks)
    width = cand.shape[1]
    equal = cand[:, :, None] == cand[:, None, :]
    earlier = jnp.arange(width)[None, :] < jnp.arange(width)[:, None]
    repeated = jnp.any(equal & earlier[None, :, :], axis=2)
    return (jnp.clip(cand, 0, nblocks - 1), inside & ~repeated)


def head_attention(q_head, k_head, v_head, rand_h, glob):
    length = q_head.shape[1]
    nblocks = length // BLK
    scale = HD ** (-0.5)
    qb = q_head.reshape(HD, nblocks, BLK)
    kb = k_head.reshape(HD, nblocks, BLK)
    vb = v_head.reshape(HD, nblocks, BLK)
    index, valid = candidate_blocks(nblocks, glob, rand_h)
    group = math.gcd(nblocks, 32)
    turns = nblocks // group

    def one_group(turn):
        first = turn * group
        rows_index = lax.dynamic_slice_in_dim(index, first, group, 0)
        rows_valid = lax.dynamic_slice_in_dim(valid, first, group, 0)
        q_rows = lax.dynamic_slice_in_dim(qb, first, group, 1)
        k_rows = jnp.take(kb, rows_index, axis=1)
        v_rows = jnp.take(vb, rows_index, axis=1)
        scores = (
            jnp.einsum("dnq,dnck->nqck", q_rows, k_rows, preferred_element_type=jnp.float32) * scale
        )
        scores = jnp.where(rows_valid[:, None, :, None], scores, -jnp.inf)
        top = jnp.max(scores, axis=(2, 3), keepdims=True)
        expo = jnp.exp(scores - top)
        probs = (expo / jnp.sum(expo, axis=(2, 3), keepdims=True)).astype(jnp.bfloat16)
        return jnp.einsum(
            "nqck,dnck->dnq", probs, v_rows, preferred_element_type=jnp.float32
        ).astype(jnp.bfloat16)

    parts = lax.map(one_group, jnp.arange(turns, dtype=jnp.int32))
    blocks = jnp.transpose(parts, (1, 0, 2, 3)).reshape(HD, nblocks, BLK)
    qglob = jnp.take(qb, glob, axis=1)
    gscore = jnp.einsum("dgq,dk->gqk", qglob, k_head, preferred_element_type=jnp.float32) * scale
    gtop = jnp.max(gscore, axis=2, keepdims=True)
    gexp = jnp.exp(gscore - gtop)
    gprob = (gexp / jnp.sum(gexp, axis=2, keepdims=True)).astype(jnp.bfloat16)
    full = jnp.einsum("gqk,dk->dgq", gprob, v_head, preferred_element_type=jnp.float32).astype(
        jnp.bfloat16
    )
    blocks = blocks.at[:, glob, :].set(full)
    return blocks.reshape(HD, length)


def local_plain(queries, keys, values, random_blocks, global_blocks, out_weight):
    q_heads, k_heads, v_heads = (
        lax.all_to_all(queries[0], "seq", split_axis=0, concat_axis=1, tiled=True),
        lax.all_to_all(keys[0], "seq", split_axis=0, concat_axis=1, tiled=True),
        lax.all_to_all(values[0], "seq", split_axis=0, concat_axis=1, tiled=True),
    )
    count = q_heads.shape[0] // HD
    length = q_heads.shape[1]
    glob = global_blocks[0]

    def one_head(packed):
        q_head, k_head, v_head, rand_h = packed
        return head_attention(q_head, k_head, v_head, rand_h, glob)

    outputs = lax.map(
        one_head,
        (
            q_heads.reshape(count, HD, length),
            k_heads.reshape(count, HD, length),
            v_heads.reshape(count, HD, length),
            random_blocks[0],
        ),
    )
    attended = lax.all_to_all(
        outputs.reshape(count * HD, length), "seq", split_axis=1, concat_axis=0, tiled=True
    )
    result = lax.dot_general(
        attended,
        lax.all_gather(out_weight, "dp", axis=0, tiled=True),
        (((0,), (0,)), ((), ())),
        preferred_element_type=jnp.float32,
    )
    return result.astype(jnp.bfloat16)[None]


def cut_kernel(n, feats, row, q_ref, k_ref, v_ref, out, held, in_sems, out_sems):
    def read(to, i):
        src = (q_ref, k_ref, v_ref)[i]
        return pltpu.make_async_copy(
            src.at[0, pl.ds(to * feats + row, PAIR), :], held.at[to, i], in_sems.at[to, i]
        )

    def write(to):
        return pltpu.make_async_copy(held.at[to], out.at[to], out_sems.at[to])

    for to in range(n):
        for i in range(3):
            read(to, i).start()
    for to in range(n):
        for i in range(3):
            read(to, i).wait()
        write(to).start()
    for to in range(n):
        write(to).wait()


def cut(n, row, queries, keys, values):
    feats = queries.shape[1] // n
    length = queries.shape[2]
    hbm = pl.BlockSpec(memory_space=pltpu.HBM)
    return pl.pallas_call(
        functools.partial(cut_kernel, n, feats, row),
        out_shape=jax.ShapeDtypeStruct((n, 3, PAIR, length), queries.dtype),
        in_specs=[hbm, hbm, hbm],
        out_specs=hbm,
        scratch_shapes=[
            pltpu.VMEM((n, 3, PAIR, length), queries.dtype),
            pltpu.SemaphoreType.DMA((n, 3)),
            pltpu.SemaphoreType.DMA((n,)),
        ],
        name="cut",
    )(queries, keys, values)


def cut_apart_kernel(n, feats, row, me_ref, q_ref, k_ref, v_ref, *rest):
    outs = rest[:n]
    held, in_sems, out_sems = rest[n:]
    me = me_ref[0]

    def read(k, i):
        start = pl.multiple_of((me ^ k) * feats + row, PAIR)
        src = (q_ref, k_ref, v_ref)[i]
        return pltpu.make_async_copy(
            src.at[0, pl.ds(start, PAIR), :], held.at[k, i], in_sems.at[k, i]
        )

    def write(k):
        return pltpu.make_async_copy(held.at[k], outs[k], out_sems.at[k])

    for k in range(n):
        for i in range(3):
            read(k, i).start()
    for k in range(n):
        for i in range(3):
            read(k, i).wait()
        write(k).start()
    for k in range(n):
        write(k).wait()


def cut_apart(n, row, me, queries, keys, values):
    feats = queries.shape[1] // n
    length = queries.shape[2]
    hbm = pl.BlockSpec(memory_space=pltpu.HBM)
    return pl.pallas_call(
        functools.partial(cut_apart_kernel, n, feats, row),
        out_shape=[jax.ShapeDtypeStruct((3, PAIR, length), queries.dtype)] * n,
        in_specs=[pl.BlockSpec(memory_space=pltpu.SMEM), hbm, hbm, hbm],
        out_specs=[hbm] * n,
        scratch_shapes=[
            pltpu.VMEM((n, 3, PAIR, length), queries.dtype),
            pltpu.SemaphoreType.DMA((n, 3)),
            pltpu.SemaphoreType.DMA((n,)),
        ],
        name="cut_apart",
    )(me, queries, keys, values)


def swap_halves(x):
    return jnp.concatenate([x[:, BLK:], x[:, :BLK]], axis=1)


def attend_kernel(n, nblocks, apart_in, apart_out, me_ref, rand_ref, glob_ref, *rest):
    pen_ref, rest = rest[0], rest[1:]
    ins, rest = (rest[:n], rest[n:]) if apart_in else (rest[:1], rest[1:])
    outs, rest = (rest[:n], rest[n:]) if apart_out else (rest[:1], rest[1:])
    raw, kt, vv, ob, sg, in_sems, out_sems = rest
    me = me_ref[0]
    shard = raw.shape[3]
    per = shard // BLK
    tiles = shard // PAIR
    f32, bf16 = jnp.float32, jnp.bfloat16

    shards = [me ^ k for k in range(n)] if apart_in else list(range(n))
    arrivals = []
    for i, s in enumerate(shards):
        src = ins[i] if apart_in else ins[0].at[i]
        arrivals.append(pltpu.make_async_copy(src, raw.at[s], in_sems.at[i]))
    for copy in arrivals:
        copy.start()

    for s, copy in zip(shards, arrivals):
        copy.wait()
        for t in range(tiles):
            lanes = slice(t * PAIR, (t + 1) * PAIR)
            first = pl.multiple_of(s * shard + t * PAIR, PAIR)
            kt[pl.ds(first, PAIR), :] = raw[s, 1, :, lanes].T
            v = raw[s, 2, :, lanes]
            vv[0, s * tiles + t] = v
            vv[1, s * tiles + t] = swap_halves(v)

    low = lax.broadcasted_iota(jnp.int32, (BLK, PAIR), 1) < BLK
    zero = jnp.zeros((HD, PAIR), bf16)

    def queries_of(x, odd):
        y = swap_halves(x)
        a, b = (y, x) if odd else (x, y)
        return jnp.concatenate(
            [jnp.where(low, a[:HD], zero), jnp.where(low, zero, b[HD:])], axis=0
        )

    def key_rows(b):
        return kt[pl.ds(pl.multiple_of(b * BLK, BLK), BLK), :]

    def value_half(head, b, place):
        side = lax.rem(b + place, 2)
        return vv[side, lax.div(b, 2), head * HD : (head + 1) * HD, :]

    def finish(ot, total):
        t = (ot / total).astype(bf16).T
        return jnp.where(low, t[:BLK], t[BLK:])

    def sparse(j, qbd):
        shared = [jnp.maximum(j - 1, 0), j, jnp.minimum(j + 1, nblocks - 1), glob_ref[0], glob_ref[1]]
        cand = [
            shared + [rand_ref[(h * nblocks + j) * 3 + c] for c in range(3)] for h in range(2)
        ]
        k_rows = [key_rows(b) for b in shared]
        for c in range(5, 8):
            k_rows.append(jnp.where(low, key_rows(cand[0][c]), key_rows(cand[1][c])))
        scores = jnp.dot(jnp.concatenate(k_rows, axis=0), qbd, preferred_element_type=f32)
        top = jnp.max(scores, axis=0, keepdims=True) * EXP_SCALE
        pen = pen_ref[j]
        shift = jnp.where(low[:8], pen[:, 0:1], pen[:, 1:2]) + top
        probs = [
            jnp.exp2(scores[c * BLK : (c + 1) * BLK] * EXP_SCALE - shift[c : c + 1])
            for c in range(8)
        ]
        total = functools.reduce(
            jnp.add, [jnp.sum(p, axis=0, keepdims=True) for p in probs]
        )
        pt = jnp.concatenate([p.astype(bf16) for p in probs], axis=0)
        vcat = []
        for c in range(0, 8, 2):
            vcat.append(
                jnp.concatenate(
                    [
                        jnp.where(
                            low, value_half(h, cand[h][c], 0), value_half(h, cand[h][c + 1], 1)
                        )
                        for h in range(2)
                    ],
                    axis=0,
                )
            )
        ot = jnp.dot(jnp.concatenate(vcat, axis=1), pt, preferred_element_type=f32)
        return finish(ot, total)

    def tile_of(i):
        s = lax.div(i, tiles)
        first = pl.multiple_of(lax.rem(i, tiles) * PAIR, PAIR)
        return s, first

    def two_blocks(i, carry):
        s, first = tile_of(i)
        x = raw[s, 0, :, pl.ds(first, PAIR)]
        a = sparse(2 * i, queries_of(x, False))
        b = sparse(2 * i + 1, queries_of(x, True))
        ob[s, pl.ds(first, PAIR), :] = jnp.concatenate([a, b], axis=0)
        return carry

    lax.fori_loop(0, nblocks // 2, two_blocks, 0, unroll=8)

    places, columns = [], []
    for g in range(2):
        s, first = tile_of(lax.div(glob_ref[g], 2))
        x = raw[s, 0, :, pl.ds(first, PAIR)]
        odd = lax.rem(glob_ref[g], 2)
        columns.append(jnp.where(odd == 1, queries_of(x, True), queries_of(x, False)))
        places.append((s, pl.multiple_of(lax.rem(glob_ref[g], per) * BLK, BLK)))
    qbd = jnp.concatenate(columns, axis=1)
    top = jnp.full((1, 2 * PAIR), -jnp.inf, f32)
    for t in range(n):
        rows = slice(t * shard, (t + 1) * shard)
        scores = jnp.dot(kt[rows, :], qbd, preferred_element_type=f32)
        sg[rows, :] = scores
        top = jnp.maximum(top, jnp.max(scores, axis=0, keepdims=True))
    top = top * EXP_SCALE
    total = jnp.zeros((1, 2 * PAIR), f32)
    ot = jnp.zeros((PAIR, 2 * PAIR), f32)
    for t in range(n):
        p = jnp.exp2(sg[t * shard : (t + 1) * shard, :] * EXP_SCALE - top)
        total = total + jnp.sum(p, axis=0, keepdims=True)
        ot = ot + jnp.dot(raw[t, 2], p.astype(bf16), preferred_element_type=f32)
    for g, (s, place) in enumerate(places):
        lanes = slice(g * PAIR, (g + 1) * PAIR)
        ob[s, pl.ds(place, BLK), :] = finish(ot[:, lanes], total[:, lanes])

    if apart_out:
        leaving = [
            pltpu.make_async_copy(ob.at[me ^ k], outs[k], out_sems.at[k])
            for k in range(n)
        ]
    else:
        leaving = [pltpu.make_async_copy(ob, outs[0], out_sems.at[0])]
    for copy in leaving:
        copy.start()
    for copy in leaving:
        copy.wait()


def attend(n, me, rand, glob, pen, arrays, apart_out):
    apart_in = len(arrays) > 1
    shard = arrays[0].shape[-1]
    length = n * shard
    nblocks = length // BLK
    hbm = pl.BlockSpec(memory_space=pltpu.HBM)
    smem = pl.BlockSpec(memory_space=pltpu.SMEM)
    vmem = pl.BlockSpec(memory_space=pltpu.VMEM)
    if apart_out:
        out_shape = [jax.ShapeDtypeStruct((shard, PAIR), jnp.bfloat16)] * n
    else:
        out_shape = [jax.ShapeDtypeStruct((n, shard, PAIR), jnp.bfloat16)]
    return pl.pallas_call(
        functools.partial(attend_kernel, n, nblocks, apart_in, apart_out),
        out_shape=out_shape,
        in_specs=[smem, smem, smem, vmem] + [hbm] * len(arrays),
        out_specs=[hbm] * len(out_shape),
        scratch_shapes=[
            pltpu.VMEM((n, 3, PAIR, shard), jnp.bfloat16),
            pltpu.VMEM((length, PAIR), jnp.bfloat16),
            pltpu.VMEM((2, nblocks // 2, PAIR, PAIR), jnp.bfloat16),
            pltpu.VMEM((n, shard, PAIR), jnp.bfloat16),
            pltpu.VMEM((length, 2 * PAIR), jnp.float32),
            pltpu.SemaphoreType.DMA((n,)),
            pltpu.SemaphoreType.DMA((n,)),
        ],
        compiler_params=pltpu.CompilerParams(vmem_limit_bytes=60 * 1024 * 1024),
        cost_estimate=pl.CostEstimate(
            flops=15_000_000_000, bytes_accessed=4_000_000, transcendentals=0
        ),
        name="attend",
    )(me, rand, glob, pen, *arrays)


def project_kernel(n, ndp, slots, before, me_ref, *rest):
    arrays = sorted({i for i, _, _ in slots})
    pieces, rest = rest[: len(arrays)], rest[len(arrays) :]
    weights, rest = rest[:ndp], rest[ndp:]
    if before:
        before_ref, rest = rest[0], rest[1:]
        acc, rest = rest[1], rest[:1] + rest[2:]
    o_ref, a, w, a_sems, w_sems, acc_sems = rest
    me, dp = me_ref[0], me_ref[1]
    held = n // ndp
    feats = weights[0].shape[0] // held
    width = weights[0].shape[1]
    tile = width // 4

    def piece_copy(slot):
        i, _, k = slots[slot]
        src = pieces[arrays.index(i)]
        src = src.at[me ^ k] if len(src.shape) == 3 else src
        dst = a.at[:, pl.ds(slot * PAIR, PAIR)]
        return pltpu.make_async_copy(src, dst, a_sems.at[slot])

    def weight_copy(slot, part):
        _, p, k = slots[slot]
        row = pl.multiple_of(lax.rem(me ^ k, held) * feats + p * PAIR, PAIR)
        dst = w.at[pl.ds(slot * PAIR, PAIR), :]
        return pltpu.make_async_copy(weights[part].at[pl.ds(row, PAIR), :], dst, w_sems.at[slot])

    def acc_copy(t):
        columns = pl.ds(t * tile, tile)
        return pltpu.make_async_copy(
            before_ref.at[0, :, columns], acc.at[:, columns], acc_sems.at[t]
        )

    every = range(len(slots))
    for slot in every:
        piece_copy(slot).start()
    own = lax.div(me, held) ^ dp
    for r in range(ndp):

        @pl.when(own == r)
        def _():
            for slot in every:
                weight_copy(slot, r ^ (slots[slot][2] // held)).start()

    if before:
        for t in range(4):
            acc_copy(t).start()
    for slot in every:
        piece_copy(slot).wait()
    for slot in every:
        weight_copy(slot, 0).wait()
    for t in range(4):
        columns = slice(t * tile, (t + 1) * tile)
        total = jnp.dot(a[...], w[:, columns], preferred_element_type=jnp.float32)
        if before:
            acc_copy(t).wait()
            total = total + acc[:, columns]
        o_ref[0, :, columns] = total.astype(o_ref.dtype)


def project(n, me, pieces, slots, weights, before, dtype):
    shard = pieces[0].shape[-2]
    ndp = len(weights)
    width = weights[0].shape[1]
    depth = len(slots) * PAIR
    hbm = pl.BlockSpec(memory_space=pl.ANY)
    more = [] if before is None else [before]
    return pl.pallas_call(
        functools.partial(project_kernel, n, ndp, slots, before is not None),
        out_shape=jax.ShapeDtypeStruct((1, shard, width), dtype),
        in_specs=[pl.BlockSpec(memory_space=pltpu.SMEM)]
        + [hbm] * (len(pieces) + ndp + len(more)),
        out_specs=pl.BlockSpec(memory_space=pltpu.VMEM),
        scratch_shapes=[pltpu.VMEM((shard, width), jnp.float32)] * len(more)
        + [
            pltpu.VMEM((shard, depth), jnp.bfloat16),
            pltpu.VMEM((depth, width), jnp.bfloat16),
            pltpu.SemaphoreType.DMA((len(slots),)),
            pltpu.SemaphoreType.DMA((len(slots),)),
            pltpu.SemaphoreType.DMA((4,)),
        ],
        compiler_params=pltpu.CompilerParams(vmem_limit_bytes=24 * 1024 * 1024),
        cost_estimate=pl.CostEstimate(
            flops=2 * shard * depth * width, bytes_accessed=10_000_000, transcendentals=0
        ),
        name="project",
    )(me, *pieces, *weights, *more)


def gather_weight(ndp, weight):
    parts = {0: weight}
    bit = ndp // 2
    while bit:
        for r in list(parts):
            parts[r + bit] = lax.ppermute(parts[r], "dp", [(i, i ^ bit) for i in range(ndp)])
        bit //= 2
    return [parts[r] for r in range(ndp)]


def local_paired(n, ndp, queries, keys, values, random_blocks, global_blocks, out_weight):
    me = jnp.stack([lax.axis_index("seq"), lax.axis_index("dp")]).astype(jnp.int32)
    feats = queries.shape[1] // n
    length = queries.shape[2] * n
    nblocks = length // BLK
    pairs = feats // PAIR
    glob = global_blocks[0]

    def exchange(x):
        return lax.all_to_all(x, "seq", split_axis=0, concat_axis=0, tiled=True)

    def swap(arrays, order):
        got = {k: lax.ppermute(arrays[k], "seq", [(i, i ^ k) for i in range(n)]) for k in order}
        return [arrays[0]] + [got[k] for k in range(1, n)]

    near, far = list(range(1, n // 2)), list(range(n // 2, n))

    valid = jax.vmap(lambda r: candidate_blocks(nblocks, glob, r)[1])(random_blocks[0])
    pen = jnp.where(valid, 0.0, BIG).astype(jnp.float32)
    pen = jnp.transpose(pen.reshape(pairs, 2, nblocks, -1), (0, 2, 3, 1))
    rand = random_blocks[0].reshape(pairs, -1)

    last = pairs - 1
    arrived = [exchange(cut(n, p * PAIR, queries, keys, values)) for p in range(last)]
    messages = swap(cut_apart(n, last * PAIR, me, queries, keys, values), near + far)
    weights = gather_weight(ndp, lax.optimization_barrier((out_weight, messages[1]))[0])

    pieces, slots = [], []
    for p in range(last):
        outs = attend(n, me, rand[p], glob, pen[p], [arrived[p]], False)
        pieces.append(exchange(outs[0]))
        slots += [(p, p, k) for k in range(n)]
    outs = attend(n, me, rand[last], glob, pen[last], messages, True)
    outs, weights = lax.optimization_barrier((list(outs), weights))
    results = swap(outs, far + near)
    pieces += [results[k] for k in [0] + near]
    slots += [(last + i, last, k) for i, k in enumerate([0] + near)]
    total = project(n, me, pieces, slots, weights, None, jnp.float32)
    slots = [(i, last, k) for i, k in enumerate(far)]
    return project(n, me, [results[k] for k in far], slots, weights, total, jnp.bfloat16)


def solution(mesh):
    n, ndp = mesh.shape["seq"], mesh.shape["dp"]
    in_specs = (
        P("dp", None, "seq"),
        P("dp", None, "seq"),
        P("dp", None, "seq"),
        P("dp", "seq", None, None),
        P("dp", None),
        P("dp", None),
    )
    out_specs = P("dp", "seq", None)

    def local(queries, keys, *rest):
        feats, shard = queries.shape[1] // n, queries.shape[2]
        paired = feats % PAIR == 0 and shard % PAIR == 0 and n % ndp == 0
        paired = paired and n & (n - 1) == 0 and ndp & (ndp - 1) == 0
        body = functools.partial(local_paired, n, ndp) if paired else local_plain
        return body(queries, keys, *rest)

    return jax.shard_map(local, mesh=mesh, in_specs=in_specs, out_specs=out_specs, check_vma=False)
```

```python
import functools
import math

import jax
import jax.numpy as jnp
from jax import lax
from jax.experimental import pallas as pl
from jax.experimental.pallas import tpu as pltpu
from jax.sharding import PartitionSpec as P

HD = 64
BLK = 64
PAIR = 2 * HD
EXP_SCALE = HD ** (-0.5) * math.log2(math.e)
BIG = 1e30


def candidate_blocks(nblocks, glob, rand_h):
    rows = jnp.arange(nblocks, dtype=jnp.int32)
    window = jnp.stack([rows - 1, rows, rows + 1], axis=1)
    globs = jnp.broadcast_to(glob[None, :], (nblocks, glob.shape[0]))
    cand = jnp.concatenate([window, globs, rand_h], axis=1)
    inside = (cand >= 0) & (cand < nblocks)
    width = cand.shape[1]
    equal = cand[:, :, None] == cand[:, None, :]
    earlier = jnp.arange(width)[None, :] < jnp.arange(width)[:, None]
    repeated = jnp.any(equal & earlier[None, :, :], axis=2)
    return (jnp.clip(cand, 0, nblocks - 1), inside & ~repeated)


def head_attention(q_head, k_head, v_head, rand_h, glob):
    length = q_head.shape[1]
    nblocks = length // BLK
    scale = HD ** (-0.5)
    qb = q_head.reshape(HD, nblocks, BLK)
    kb = k_head.reshape(HD, nblocks, BLK)
    vb = v_head.reshape(HD, nblocks, BLK)
    index, valid = candidate_blocks(nblocks, glob, rand_h)
    group = math.gcd(nblocks, 32)
    turns = nblocks // group

    def one_group(turn):
        first = turn * group
        rows_index = lax.dynamic_slice_in_dim(index, first, group, 0)
        rows_valid = lax.dynamic_slice_in_dim(valid, first, group, 0)
        q_rows = lax.dynamic_slice_in_dim(qb, first, group, 1)
        k_rows = jnp.take(kb, rows_index, axis=1)
        v_rows = jnp.take(vb, rows_index, axis=1)
        scores = (
            jnp.einsum("dnq,dnck->nqck", q_rows, k_rows, preferred_element_type=jnp.float32) * scale
        )
        scores = jnp.where(rows_valid[:, None, :, None], scores, -jnp.inf)
        top = jnp.max(scores, axis=(2, 3), keepdims=True)
        expo = jnp.exp(scores - top)
        probs = (expo / jnp.sum(expo, axis=(2, 3), keepdims=True)).astype(jnp.bfloat16)
        return jnp.einsum(
            "nqck,dnck->dnq", probs, v_rows, preferred_element_type=jnp.float32
        ).astype(jnp.bfloat16)

    parts = lax.map(one_group, jnp.arange(turns, dtype=jnp.int32))
    blocks = jnp.transpose(parts, (1, 0, 2, 3)).reshape(HD, nblocks, BLK)
    qglob = jnp.take(qb, glob, axis=1)
    gscore = jnp.einsum("dgq,dk->gqk", qglob, k_head, preferred_element_type=jnp.float32) * scale
    gtop = jnp.max(gscore, axis=2, keepdims=True)
    gexp = jnp.exp(gscore - gtop)
    gprob = (gexp / jnp.sum(gexp, axis=2, keepdims=True)).astype(jnp.bfloat16)
    full = jnp.einsum("gqk,dk->dgq", gprob, v_head, preferred_element_type=jnp.float32).astype(
        jnp.bfloat16
    )
    blocks = blocks.at[:, glob, :].set(full)
    return blocks.reshape(HD, length)


def local_plain(queries, keys, values, random_blocks, global_blocks, out_weight):
    q_heads, k_heads, v_heads = (
        lax.all_to_all(queries[0], "seq", split_axis=0, concat_axis=1, tiled=True),
        lax.all_to_all(keys[0], "seq", split_axis=0, concat_axis=1, tiled=True),
        lax.all_to_all(values[0], "seq", split_axis=0, concat_axis=1, tiled=True),
    )
    count = q_heads.shape[0] // HD
    length = q_heads.shape[1]
    glob = global_blocks[0]

    def one_head(packed):
        q_head, k_head, v_head, rand_h = packed
        return head_attention(q_head, k_head, v_head, rand_h, glob)

    outputs = lax.map(
        one_head,
        (
            q_heads.reshape(count, HD, length),
            k_heads.reshape(count, HD, length),
            v_heads.reshape(count, HD, length),
            random_blocks[0],
        ),
    )
    attended = lax.all_to_all(
        outputs.reshape(count * HD, length), "seq", split_axis=1, concat_axis=0, tiled=True
    )
    result = lax.dot_general(
        attended,
        lax.all_gather(out_weight, "dp", axis=0, tiled=True),
        (((0,), (0,)), ((), ())),
        preferred_element_type=jnp.float32,
    )
    return result.astype(jnp.bfloat16)[None]


def cut_kernel(n, feats, row, q_ref, k_ref, v_ref, out, held, in_sems, out_sems):
    def read(to, i):
        src = (q_ref, k_ref, v_ref)[i]
        return pltpu.make_async_copy(
            src.at[0, pl.ds(to * feats + row, PAIR), :], held.at[to, i], in_sems.at[to, i]
        )

    def write(to):
        return pltpu.make_async_copy(held.at[to], out.at[to], out_sems.at[to])

    for to in range(n):
        for i in range(3):
            read(to, i).start()
    for to in range(n):
        for i in range(3):
            read(to, i).wait()
        write(to).start()
    for to in range(n):
        write(to).wait()


def cut(n, row, queries, keys, values):
    feats = queries.shape[1] // n
    length = queries.shape[2]
    hbm = pl.BlockSpec(memory_space=pltpu.HBM)
    return pl.pallas_call(
        functools.partial(cut_kernel, n, feats, row),
        out_shape=jax.ShapeDtypeStruct((n, 3, PAIR, length), queries.dtype),
        in_specs=[hbm, hbm, hbm],
        out_specs=hbm,
        scratch_shapes=[
            pltpu.VMEM((n, 3, PAIR, length), queries.dtype),
            pltpu.SemaphoreType.DMA((n, 3)),
            pltpu.SemaphoreType.DMA((n,)),
        ],
        name="cut",
    )(queries, keys, values)


def cut_apart_kernel(n, feats, row, me_ref, q_ref, k_ref, v_ref, *rest):
    outs = rest[:n]
    held, in_sems, out_sems = rest[n:]
    me = me_ref[0]

    def read(k, i):
        start = pl.multiple_of((me ^ k) * feats + row, PAIR)
        src = (q_ref, k_ref, v_ref)[i]
        return pltpu.make_async_copy(
            src.at[0, pl.ds(start, PAIR), :], held.at[k, i], in_sems.at[k, i]
        )

    def write(k):
        return pltpu.make_async_copy(held.at[k], outs[k], out_sems.at[k])

    for k in range(n):
        for i in range(3):
            read(k, i).start()
    for k in range(n):
        for i in range(3):
            read(k, i).wait()
        write(k).start()
    for k in range(n):
        write(k).wait()


def cut_apart(n, row, me, queries, keys, values):
    feats = queries.shape[1] // n
    length = queries.shape[2]
    hbm = pl.BlockSpec(memory_space=pltpu.HBM)
    return pl.pallas_call(
        functools.partial(cut_apart_kernel, n, feats, row),
        out_shape=[jax.ShapeDtypeStruct((3, PAIR, length), queries.dtype)] * n,
        in_specs=[pl.BlockSpec(memory_space=pltpu.SMEM), hbm, hbm, hbm],
        out_specs=[hbm] * n,
        scratch_shapes=[
            pltpu.VMEM((n, 3, PAIR, length), queries.dtype),
            pltpu.SemaphoreType.DMA((n, 3)),
            pltpu.SemaphoreType.DMA((n,)),
        ],
        name="cut_apart",
    )(me, queries, keys, values)


def swap_halves(x):
    return jnp.concatenate([x[:, BLK:], x[:, :BLK]], axis=1)


def attend_kernel(n, nblocks, apart_in, apart_out, me_ref, rand_ref, glob_ref, *rest):
    pen_ref, rest = rest[0], rest[1:]
    ins, rest = (rest[:n], rest[n:]) if apart_in else (rest[:1], rest[1:])
    outs, rest = (rest[:n], rest[n:]) if apart_out else (rest[:1], rest[1:])
    raw, kt, vv, ob, sg, in_sems, out_sems = rest
    me = me_ref[0]
    shard = raw.shape[3]
    per = shard // BLK
    tiles = shard // PAIR
    f32, bf16 = jnp.float32, jnp.bfloat16

    shards = [me ^ k for k in range(n)] if apart_in else list(range(n))
    arrivals = []
    for i, s in enumerate(shards):
        src = ins[i] if apart_in else ins[0].at[i]
        arrivals.append(pltpu.make_async_copy(src, raw.at[s], in_sems.at[i]))
    for copy in arrivals:
        copy.start()

    for s, copy in zip(shards, arrivals):
        copy.wait()
        for t in range(tiles):
            lanes = slice(t * PAIR, (t + 1) * PAIR)
            first = pl.multiple_of(s * shard + t * PAIR, PAIR)
            kt[pl.ds(first, PAIR), :] = raw[s, 1, :, lanes].T
            v = raw[s, 2, :, lanes]
            vv[0, s * tiles + t] = v
            vv[1, s * tiles + t] = swap_halves(v)

    low = lax.broadcasted_iota(jnp.int32, (BLK, PAIR), 1) < BLK
    zero = jnp.zeros((HD, PAIR), bf16)

    def queries_of(x, odd):
        y = swap_halves(x)
        a, b = (y, x) if odd else (x, y)
        return jnp.concatenate(
            [jnp.where(low, a[:HD], zero), jnp.where(low, zero, b[HD:])], axis=0
        )

    def key_rows(b):
        return kt[pl.ds(pl.multiple_of(b * BLK, BLK), BLK), :]

    def value_half(head, b, place):
        side = lax.rem(b + place, 2)
        return vv[side, lax.div(b, 2), head * HD : (head + 1) * HD, :]

    def finish(ot, total):
        t = (ot / total).astype(bf16).T
        return jnp.where(low, t[:BLK], t[BLK:])

    def sparse(j, qbd):
        shared = [jnp.maximum(j - 1, 0), j, jnp.minimum(j + 1, nblocks - 1), glob_ref[0], glob_ref[1]]
        cand = [
            shared + [rand_ref[(h * nblocks + j) * 3 + c] for c in range(3)] for h in range(2)
        ]
        k_rows = [key_rows(b) for b in shared]
        for c in range(5, 8):
            k_rows.append(jnp.where(low, key_rows(cand[0][c]), key_rows(cand[1][c])))
        scores = jnp.dot(jnp.concatenate(k_rows, axis=0), qbd, preferred_element_type=f32)
        top = jnp.max(scores, axis=0, keepdims=True) * EXP_SCALE
        pen = pen_ref[j]
        shift = jnp.where(low[:8], pen[:, 0:1], pen[:, 1:2]) + top
        probs = [
            jnp.exp2(scores[c * BLK : (c + 1) * BLK] * EXP_SCALE - shift[c : c + 1])
            for c in range(8)
        ]
        total = functools.reduce(
            jnp.add, [jnp.sum(p, axis=0, keepdims=True) for p in probs]
        )
        pt = jnp.concatenate([p.astype(bf16) for p in probs], axis=0)
        vcat = []
        for c in range(0, 8, 2):
            vcat.append(
                jnp.concatenate(
                    [
                        jnp.where(
                            low, value_half(h, cand[h][c], 0), value_half(h, cand[h][c + 1], 1)
                        )
                        for h in range(2)
                    ],
                    axis=0,
                )
            )
        ot = jnp.dot(jnp.concatenate(vcat, axis=1), pt, preferred_element_type=f32)
        return finish(ot, total)

    def tile_of(i):
        s = lax.div(i, tiles)
        first = pl.multiple_of(lax.rem(i, tiles) * PAIR, PAIR)
        return s, first

    def two_blocks(i, carry):
        s, first = tile_of(i)
        x = raw[s, 0, :, pl.ds(first, PAIR)]
        a = sparse(2 * i, queries_of(x, False))
        b = sparse(2 * i + 1, queries_of(x, True))
        ob[s, pl.ds(first, PAIR), :] = jnp.concatenate([a, b], axis=0)
        return carry

    lax.fori_loop(0, nblocks // 2, two_blocks, 0, unroll=8)

    places, columns = [], []
    for g in range(2):
        s, first = tile_of(lax.div(glob_ref[g], 2))
        x = raw[s, 0, :, pl.ds(first, PAIR)]
        odd = lax.rem(glob_ref[g], 2)
        columns.append(jnp.where(odd == 1, queries_of(x, True), queries_of(x, False)))
        places.append((s, pl.multiple_of(lax.rem(glob_ref[g], per) * BLK, BLK)))
    qbd = jnp.concatenate(columns, axis=1)
    top = jnp.full((1, 2 * PAIR), -jnp.inf, f32)
    for t in range(n):
        rows = slice(t * shard, (t + 1) * shard)
        scores = jnp.dot(kt[rows, :], qbd, preferred_element_type=f32)
        sg[rows, :] = scores
        top = jnp.maximum(top, jnp.max(scores, axis=0, keepdims=True))
    top = top * EXP_SCALE
    total = jnp.zeros((1, 2 * PAIR), f32)
    ot = jnp.zeros((PAIR, 2 * PAIR), f32)
    for t in range(n):
        p = jnp.exp2(sg[t * shard : (t + 1) * shard, :] * EXP_SCALE - top)
        total = total + jnp.sum(p, axis=0, keepdims=True)
        ot = ot + jnp.dot(raw[t, 2], p.astype(bf16), preferred_element_type=f32)
    for g, (s, place) in enumerate(places):
        lanes = slice(g * PAIR, (g + 1) * PAIR)
        ob[s, pl.ds(place, BLK), :] = finish(ot[:, lanes], total[:, lanes])

    if apart_out:
        leaving = [
            pltpu.make_async_copy(ob.at[me ^ k], outs[k], out_sems.at[k])
            for k in range(n)
        ]
    else:
        leaving = [pltpu.make_async_copy(ob, outs[0], out_sems.at[0])]
    for copy in leaving:
        copy.start()
    for copy in leaving:
        copy.wait()


def attend(n, me, rand, glob, pen, arrays, apart_out):
    apart_in = len(arrays) > 1
    shard = arrays[0].shape[-1]
    length = n * shard
    nblocks = length // BLK
    hbm = pl.BlockSpec(memory_space=pltpu.HBM)
    smem = pl.BlockSpec(memory_space=pltpu.SMEM)
    vmem = pl.BlockSpec(memory_space=pltpu.VMEM)
    if apart_out:
        out_shape = [jax.ShapeDtypeStruct((shard, PAIR), jnp.bfloat16)] * n
    else:
        out_shape = [jax.ShapeDtypeStruct((n, shard, PAIR), jnp.bfloat16)]
    return pl.pallas_call(
        functools.partial(attend_kernel, n, nblocks, apart_in, apart_out),
        out_shape=out_shape,
        in_specs=[smem, smem, smem, vmem] + [hbm] * len(arrays),
        out_specs=[hbm] * len(out_shape),
        scratch_shapes=[
            pltpu.VMEM((n, 3, PAIR, shard), jnp.bfloat16),
            pltpu.VMEM((length, PAIR), jnp.bfloat16),
            pltpu.VMEM((2, nblocks // 2, PAIR, PAIR), jnp.bfloat16),
            pltpu.VMEM((n, shard, PAIR), jnp.bfloat16),
            pltpu.VMEM((length, 2 * PAIR), jnp.float32),
            pltpu.SemaphoreType.DMA((n,)),
            pltpu.SemaphoreType.DMA((n,)),
        ],
        compiler_params=pltpu.CompilerParams(vmem_limit_bytes=60 * 1024 * 1024),
        cost_estimate=pl.CostEstimate(
            flops=15_000_000_000, bytes_accessed=4_000_000, transcendentals=0
        ),
        name="attend",
    )(me, rand, glob, pen, *arrays)


def project_kernel(n, ndp, slots, ahead, before, me_ref, *rest):
    arrays = sorted({i for i, _, _ in slots})
    pieces, rest = rest[: len(arrays)], rest[len(arrays) :]
    if before:
        before_ref, w, o_ref, a, a_sems = rest
    else:
        weights, rest = rest[:ndp], rest[ndp:]
        o_ref, ahead_ref, a, w, a_sems, w_sems, ahead_sems = rest
    me, dp = me_ref[0], me_ref[1]
    width = w.shape[1]
    tile = width // 4

    def piece_copy(slot):
        i, _, k = slots[slot]
        src = pieces[arrays.index(i)]
        src = src.at[me ^ k] if len(src.shape) == 3 else src
        dst = a.at[:, pl.ds(slot * PAIR, PAIR)]
        return pltpu.make_async_copy(src, dst, a_sems.at[slot])

    for slot in range(len(slots)):
        piece_copy(slot).start()
    if not before:
        held = n // ndp
        feats = weights[0].shape[0] // held

        def weight_copy(which, slot, part):
            _, p, k = which[slot]
            row = pl.multiple_of(lax.rem(me ^ k, held) * feats + p * PAIR, PAIR)
            dst, sems = (w, w_sems) if which is slots else (ahead_ref, ahead_sems)
            return pltpu.make_async_copy(
                weights[part].at[pl.ds(row, PAIR), :],
                dst.at[pl.ds(slot * PAIR, PAIR), :],
                sems.at[slot],
            )

        own = lax.div(me, held) ^ dp
        for r in range(ndp):

            @pl.when(own == r)
            def _():
                for which in (slots, ahead):
                    for slot in range(len(which)):
                        weight_copy(which, slot, r ^ (which[slot][2] // held)).start()

        for slot in range(len(slots)):
            weight_copy(slots, slot, 0).wait()
    for slot in range(len(slots)):
        piece_copy(slot).wait()
    for t in range(4):
        columns = slice(t * tile, (t + 1) * tile)
        total = jnp.dot(a[...], w[:, columns], preferred_element_type=jnp.float32)
        if before:
            total = total + before_ref[0, :, columns]
        o_ref[0, :, columns] = total.astype(o_ref.dtype)
    if not before:
        for slot in range(len(ahead)):
            weight_copy(ahead, slot, 0).wait()


def project_early(n, me, pieces, slots, ahead, weights):
    shard = pieces[0].shape[-2]
    ndp = len(weights)
    width = weights[0].shape[1]
    depth = len(slots) * PAIR
    hbm = pl.BlockSpec(memory_space=pl.ANY)
    return pl.pallas_call(
        functools.partial(project_kernel, n, ndp, slots, ahead, False),
        out_shape=[
            pltpu.VMEM((1, shard, width), jnp.float32),
            pltpu.VMEM((len(ahead) * PAIR, width), jnp.bfloat16),
        ],
        in_specs=[pl.BlockSpec(memory_space=pltpu.SMEM)] + [hbm] * (len(pieces) + ndp),
        out_specs=[pl.BlockSpec(memory_space=pltpu.VMEM)] * 2,
        scratch_shapes=[
            pltpu.VMEM((shard, depth), jnp.bfloat16),
            pltpu.VMEM((depth, width), jnp.bfloat16),
            pltpu.SemaphoreType.DMA((len(slots),)),
            pltpu.SemaphoreType.DMA((len(slots),)),
            pltpu.SemaphoreType.DMA((len(ahead),)),
        ],
        compiler_params=pltpu.CompilerParams(vmem_limit_bytes=24 * 1024 * 1024),
        cost_estimate=pl.CostEstimate(
            flops=2 * shard * depth * width, bytes_accessed=10_000_000, transcendentals=0
        ),
        name="project_early",
    )(me, *pieces, *weights)


def project_late(n, me, pieces, slots, before, rows):
    shard = pieces[0].shape[-2]
    width = rows.shape[1]
    depth = len(slots) * PAIR
    hbm = pl.BlockSpec(memory_space=pl.ANY)
    vmem = pl.BlockSpec(memory_space=pltpu.VMEM)
    before, rows = (pltpu.with_memory_space_constraint(x, pltpu.VMEM) for x in (before, rows))
    return pl.pallas_call(
        functools.partial(project_kernel, n, 0, slots, [], True),
        out_shape=jax.ShapeDtypeStruct((1, shard, width), jnp.bfloat16),
        in_specs=[pl.BlockSpec(memory_space=pltpu.SMEM)] + [hbm] * len(pieces) + [vmem, vmem],
        out_specs=vmem,
        scratch_shapes=[
            pltpu.VMEM((shard, depth), jnp.bfloat16),
            pltpu.SemaphoreType.DMA((len(slots),)),
        ],
        compiler_params=pltpu.CompilerParams(vmem_limit_bytes=24 * 1024 * 1024),
        cost_estimate=pl.CostEstimate(
            flops=2 * shard * depth * width, bytes_accessed=10_000_000, transcendentals=0
        ),
        name="project_late",
    )(me, *pieces, before, rows)


def gather_weight(ndp, weight):
    parts = {0: weight}
    bit = ndp // 2
    while bit:
        for r in list(parts):
            parts[r + bit] = lax.ppermute(parts[r], "dp", [(i, i ^ bit) for i in range(ndp)])
        bit //= 2
    return [parts[r] for r in range(ndp)]


def local_paired(n, ndp, queries, keys, values, random_blocks, global_blocks, out_weight):
    me = jnp.stack([lax.axis_index("seq"), lax.axis_index("dp")]).astype(jnp.int32)
    feats = queries.shape[1] // n
    length = queries.shape[2] * n
    nblocks = length // BLK
    pairs = feats // PAIR
    glob = global_blocks[0]

    def exchange(x):
        return lax.all_to_all(x, "seq", split_axis=0, concat_axis=0, tiled=True)

    def swap(arrays, order):
        got = {k: lax.ppermute(arrays[k], "seq", [(i, i ^ k) for i in range(n)]) for k in order}
        return [arrays[0]] + [got[k] for k in range(1, n)]

    near, far = list(range(1, n // 2)), list(range(n // 2, n))

    valid = jax.vmap(lambda r: candidate_blocks(nblocks, glob, r)[1])(random_blocks[0])
    pen = jnp.where(valid, 0.0, BIG).astype(jnp.float32)
    pen = jnp.transpose(pen.reshape(pairs, 2, nblocks, -1), (0, 2, 3, 1))
    rand = random_blocks[0].reshape(pairs, -1)

    last = pairs - 1
    arrived = [exchange(cut(n, p * PAIR, queries, keys, values)) for p in range(last)]
    messages = swap(cut_apart(n, last * PAIR, me, queries, keys, values), near + far)
    weights = gather_weight(ndp, lax.optimization_barrier((out_weight, messages[1]))[0])

    pieces, slots = [], []
    for p in range(last):
        outs = attend(n, me, rand[p], glob, pen[p], [arrived[p]], False)
        pieces.append(exchange(outs[0]))
        slots += [(p, p, k) for k in range(n)]
    outs = attend(n, me, rand[last], glob, pen[last], messages, True)
    outs, weights = lax.optimization_barrier((list(outs), weights))
    results = swap(outs, far + near)
    pieces += [results[k] for k in [0] + near]
    slots += [(last + i, last, k) for i, k in enumerate([0] + near)]
    late = [(i, last, k) for i, k in enumerate(far)]
    total, rows = project_early(n, me, pieces, slots, late, weights)
    return project_late(n, me, [results[k] for k in far], late, total, rows)


def solution(mesh):
    n, ndp = mesh.shape["seq"], mesh.shape["dp"]
    in_specs = (
        P("dp", None, "seq"),
        P("dp", None, "seq"),
        P("dp", None, "seq"),
        P("dp", "seq", None, None),
        P("dp", None),
        P("dp", None),
    )
    out_specs = P("dp", "seq", None)

    def local(queries, keys, *rest):
        feats, shard = queries.shape[1] // n, queries.shape[2]
        paired = feats % PAIR == 0 and shard % PAIR == 0 and n % ndp == 0
        paired = paired and n & (n - 1) == 0 and ndp & (ndp - 1) == 0
        body = functools.partial(local_paired, n, ndp) if paired else local_plain
        return body(queries, keys, *rest)

    return jax.shard_map(local, mesh=mesh, in_specs=in_specs, out_specs=out_specs, check_vma=False)
```

```python
import functools
import math

import jax
import jax.numpy as jnp
from jax import lax
from jax.experimental import pallas as pl
from jax.experimental.pallas import tpu as pltpu
from jax.sharding import PartitionSpec as P

HD = 64
BLK = 64
PAIR = 2 * HD
EXP_SCALE = HD ** (-0.5) * math.log2(math.e)
BIG = 1e30


def candidate_blocks(nblocks, glob, rand_h):
    rows = jnp.arange(nblocks, dtype=jnp.int32)
    window = jnp.stack([rows - 1, rows, rows + 1], axis=1)
    globs = jnp.broadcast_to(glob[None, :], (nblocks, glob.shape[0]))
    cand = jnp.concatenate([window, globs, rand_h], axis=1)
    inside = (cand >= 0) & (cand < nblocks)
    width = cand.shape[1]
    equal = cand[:, :, None] == cand[:, None, :]
    earlier = jnp.arange(width)[None, :] < jnp.arange(width)[:, None]
    repeated = jnp.any(equal & earlier[None, :, :], axis=2)
    return (jnp.clip(cand, 0, nblocks - 1), inside & ~repeated)


def head_attention(q_head, k_head, v_head, rand_h, glob):
    length = q_head.shape[1]
    nblocks = length // BLK
    scale = HD ** (-0.5)
    qb = q_head.reshape(HD, nblocks, BLK)
    kb = k_head.reshape(HD, nblocks, BLK)
    vb = v_head.reshape(HD, nblocks, BLK)
    index, valid = candidate_blocks(nblocks, glob, rand_h)
    group = math.gcd(nblocks, 32)
    turns = nblocks // group

    def one_group(turn):
        first = turn * group
        rows_index = lax.dynamic_slice_in_dim(index, first, group, 0)
        rows_valid = lax.dynamic_slice_in_dim(valid, first, group, 0)
        q_rows = lax.dynamic_slice_in_dim(qb, first, group, 1)
        k_rows = jnp.take(kb, rows_index, axis=1)
        v_rows = jnp.take(vb, rows_index, axis=1)
        scores = (
            jnp.einsum("dnq,dnck->nqck", q_rows, k_rows, preferred_element_type=jnp.float32) * scale
        )
        scores = jnp.where(rows_valid[:, None, :, None], scores, -jnp.inf)
        top = jnp.max(scores, axis=(2, 3), keepdims=True)
        expo = jnp.exp(scores - top)
        probs = (expo / jnp.sum(expo, axis=(2, 3), keepdims=True)).astype(jnp.bfloat16)
        return jnp.einsum(
            "nqck,dnck->dnq", probs, v_rows, preferred_element_type=jnp.float32
        ).astype(jnp.bfloat16)

    parts = lax.map(one_group, jnp.arange(turns, dtype=jnp.int32))
    blocks = jnp.transpose(parts, (1, 0, 2, 3)).reshape(HD, nblocks, BLK)
    qglob = jnp.take(qb, glob, axis=1)
    gscore = jnp.einsum("dgq,dk->gqk", qglob, k_head, preferred_element_type=jnp.float32) * scale
    gtop = jnp.max(gscore, axis=2, keepdims=True)
    gexp = jnp.exp(gscore - gtop)
    gprob = (gexp / jnp.sum(gexp, axis=2, keepdims=True)).astype(jnp.bfloat16)
    full = jnp.einsum("gqk,dk->dgq", gprob, v_head, preferred_element_type=jnp.float32).astype(
        jnp.bfloat16
    )
    blocks = blocks.at[:, glob, :].set(full)
    return blocks.reshape(HD, length)


def local_plain(queries, keys, values, random_blocks, global_blocks, out_weight):
    q_heads, k_heads, v_heads = (
        lax.all_to_all(queries[0], "seq", split_axis=0, concat_axis=1, tiled=True),
        lax.all_to_all(keys[0], "seq", split_axis=0, concat_axis=1, tiled=True),
        lax.all_to_all(values[0], "seq", split_axis=0, concat_axis=1, tiled=True),
    )
    count = q_heads.shape[0] // HD
    length = q_heads.shape[1]
    glob = global_blocks[0]

    def one_head(packed):
        q_head, k_head, v_head, rand_h = packed
        return head_attention(q_head, k_head, v_head, rand_h, glob)

    outputs = lax.map(
        one_head,
        (
            q_heads.reshape(count, HD, length),
            k_heads.reshape(count, HD, length),
            v_heads.reshape(count, HD, length),
            random_blocks[0],
        ),
    )
    attended = lax.all_to_all(
        outputs.reshape(count * HD, length), "seq", split_axis=1, concat_axis=0, tiled=True
    )
    result = lax.dot_general(
        attended,
        lax.all_gather(out_weight, "dp", axis=0, tiled=True),
        (((0,), (0,)), ((), ())),
        preferred_element_type=jnp.float32,
    )
    return result.astype(jnp.bfloat16)[None]


def cut_kernel(n, feats, row, q_ref, k_ref, v_ref, out, sems):
    copies = []
    for to in range(n):
        for i, src in enumerate((q_ref, k_ref, v_ref)):
            src = src.at[0, pl.ds(to * feats + row, PAIR), :]
            copies.append(pltpu.make_async_copy(src, out.at[to, i], sems.at[to, i]))
    for copy in copies:
        copy.start()
    for copy in copies:
        copy.wait()


def cut(n, row, queries, keys, values):
    feats = queries.shape[1] // n
    length = queries.shape[2]
    hbm = pl.BlockSpec(memory_space=pl.ANY)
    return pl.pallas_call(
        functools.partial(cut_kernel, n, feats, row),
        out_shape=pltpu.VMEM((n, 3, PAIR, length), queries.dtype),
        in_specs=[hbm, hbm, hbm],
        out_specs=pl.BlockSpec(memory_space=pltpu.VMEM),
        scratch_shapes=[pltpu.SemaphoreType.DMA((n, 3))],
        compiler_params=pltpu.CompilerParams(vmem_limit_bytes=56 * 1024 * 1024),
        name="cut",
    )(queries, keys, values)


def cut_apart_kernel(n, feats, row, me_ref, q_ref, k_ref, v_ref, *rest):
    outs = rest[:n]
    held, in_sems, out_sems = rest[n:]
    me = me_ref[0]

    def read(k, i):
        start = pl.multiple_of((me ^ k) * feats + row, PAIR)
        src = (q_ref, k_ref, v_ref)[i]
        return pltpu.make_async_copy(
            src.at[0, pl.ds(start, PAIR), :], held.at[k, i], in_sems.at[k, i]
        )

    def write(k):
        return pltpu.make_async_copy(held.at[k], outs[k], out_sems.at[k])

    for k in range(n):
        for i in range(3):
            read(k, i).start()
    for k in range(n):
        for i in range(3):
            read(k, i).wait()
        write(k).start()
    for k in range(n):
        write(k).wait()


def cut_apart(n, row, me, queries, keys, values):
    feats = queries.shape[1] // n
    length = queries.shape[2]
    hbm = pl.BlockSpec(memory_space=pltpu.HBM)
    return pl.pallas_call(
        functools.partial(cut_apart_kernel, n, feats, row),
        out_shape=[jax.ShapeDtypeStruct((3, PAIR, length), queries.dtype)] * n,
        in_specs=[pl.BlockSpec(memory_space=pltpu.SMEM), hbm, hbm, hbm],
        out_specs=[hbm] * n,
        scratch_shapes=[
            pltpu.VMEM((n, 3, PAIR, length), queries.dtype),
            pltpu.SemaphoreType.DMA((n, 3)),
            pltpu.SemaphoreType.DMA((n,)),
        ],
        name="cut_apart",
    )(me, queries, keys, values)


def swap_halves(x):
    return jnp.concatenate([x[:, BLK:], x[:, :BLK]], axis=1)


def attend_kernel(n, nblocks, apart_in, apart_out, me_ref, rand_ref, glob_ref, *rest):
    pen_ref, rest = rest[0], rest[1:]
    ins, rest = (rest[:n], rest[n:]) if apart_in else (rest[:1], rest[1:])
    outs, rest = (rest[:n], rest[n:]) if apart_out else (rest[:1], rest[1:])
    raw, kt, vv, ob, sg, in_sems, out_sems = rest
    me = me_ref[0]
    shard = raw.shape[3]
    per = shard // BLK
    tiles = shard // PAIR
    f32, bf16 = jnp.float32, jnp.bfloat16

    shards = [me ^ k for k in range(n)] if apart_in else list(range(n))
    arrivals = []
    for i, s in enumerate(shards):
        src = ins[i] if apart_in else ins[0].at[i]
        arrivals.append(pltpu.make_async_copy(src, raw.at[s], in_sems.at[i]))
    for copy in arrivals:
        copy.start()

    for s, copy in zip(shards, arrivals):
        copy.wait()
        for t in range(tiles):
            lanes = slice(t * PAIR, (t + 1) * PAIR)
            first = pl.multiple_of(s * shard + t * PAIR, PAIR)
            kt[pl.ds(first, PAIR), :] = raw[s, 1, :, lanes].T
            v = raw[s, 2, :, lanes]
            vv[0, s * tiles + t] = v
            vv[1, s * tiles + t] = swap_halves(v)

    low = lax.broadcasted_iota(jnp.int32, (BLK, PAIR), 1) < BLK
    zero = jnp.zeros((HD, PAIR), bf16)

    def queries_of(x, odd):
        y = swap_halves(x)
        a, b = (y, x) if odd else (x, y)
        return jnp.concatenate(
            [jnp.where(low, a[:HD], zero), jnp.where(low, zero, b[HD:])], axis=0
        )

    def key_rows(b):
        return kt[pl.ds(pl.multiple_of(b * BLK, BLK), BLK), :]

    def value_half(head, b, place):
        side = lax.rem(b + place, 2)
        return vv[side, lax.div(b, 2), head * HD : (head + 1) * HD, :]

    def finish(ot, total):
        t = (ot / total).astype(bf16).T
        return jnp.where(low, t[:BLK], t[BLK:])

    def sparse(j, qbd):
        shared = [jnp.maximum(j - 1, 0), j, jnp.minimum(j + 1, nblocks - 1), glob_ref[0], glob_ref[1]]
        cand = [
            shared + [rand_ref[(h * nblocks + j) * 3 + c] for c in range(3)] for h in range(2)
        ]
        k_rows = [key_rows(b) for b in shared]
        for c in range(5, 8):
            k_rows.append(jnp.where(low, key_rows(cand[0][c]), key_rows(cand[1][c])))
        scores = jnp.dot(jnp.concatenate(k_rows, axis=0), qbd, preferred_element_type=f32)
        top = jnp.max(scores, axis=0, keepdims=True) * EXP_SCALE
        pen = pen_ref[j]
        shift = jnp.where(low[:8], pen[:, 0:1], pen[:, 1:2]) + top
        probs = [
            jnp.exp2(scores[c * BLK : (c + 1) * BLK] * EXP_SCALE - shift[c : c + 1])
            for c in range(8)
        ]
        total = functools.reduce(
            jnp.add, [jnp.sum(p, axis=0, keepdims=True) for p in probs]
        )
        pt = jnp.concatenate([p.astype(bf16) for p in probs], axis=0)
        vcat = []
        for c in range(0, 8, 2):
            vcat.append(
                jnp.concatenate(
                    [
                        jnp.where(
                            low, value_half(h, cand[h][c], 0), value_half(h, cand[h][c + 1], 1)
                        )
                        for h in range(2)
                    ],
                    axis=0,
                )
            )
        ot = jnp.dot(jnp.concatenate(vcat, axis=1), pt, preferred_element_type=f32)
        return finish(ot, total)

    def tile_of(i):
        s = lax.div(i, tiles)
        first = pl.multiple_of(lax.rem(i, tiles) * PAIR, PAIR)
        return s, first

    def two_blocks(i, carry):
        s, first = tile_of(i)
        x = raw[s, 0, :, pl.ds(first, PAIR)]
        a = sparse(2 * i, queries_of(x, False))
        b = sparse(2 * i + 1, queries_of(x, True))
        ob[s, pl.ds(first, PAIR), :] = jnp.concatenate([a, b], axis=0)
        return carry

    lax.fori_loop(0, nblocks // 2, two_blocks, 0, unroll=8)

    places, columns = [], []
    for g in range(2):
        s, first = tile_of(lax.div(glob_ref[g], 2))
        x = raw[s, 0, :, pl.ds(first, PAIR)]
        odd = lax.rem(glob_ref[g], 2)
        columns.append(jnp.where(odd == 1, queries_of(x, True), queries_of(x, False)))
        places.append((s, pl.multiple_of(lax.rem(glob_ref[g], per) * BLK, BLK)))
    qbd = jnp.concatenate(columns, axis=1)
    top = jnp.full((1, 2 * PAIR), -jnp.inf, f32)
    for t in range(n):
        rows = slice(t * shard, (t + 1) * shard)
        scores = jnp.dot(kt[rows, :], qbd, preferred_element_type=f32)
        sg[rows, :] = scores
        top = jnp.maximum(top, jnp.max(scores, axis=0, keepdims=True))
    top = top * EXP_SCALE
    total = jnp.zeros((1, 2 * PAIR), f32)
    ot = jnp.zeros((PAIR, 2 * PAIR), f32)
    for t in range(n):
        p = jnp.exp2(sg[t * shard : (t + 1) * shard, :] * EXP_SCALE - top)
        total = total + jnp.sum(p, axis=0, keepdims=True)
        ot = ot + jnp.dot(raw[t, 2], p.astype(bf16), preferred_element_type=f32)
    for g, (s, place) in enumerate(places):
        lanes = slice(g * PAIR, (g + 1) * PAIR)
        ob[s, pl.ds(place, BLK), :] = finish(ot[:, lanes], total[:, lanes])

    if apart_out:
        leaving = [
            pltpu.make_async_copy(ob.at[me ^ k], outs[k], out_sems.at[k])
            for k in range(n)
        ]
    else:
        leaving = [pltpu.make_async_copy(ob, outs[0], out_sems.at[0])]
    for copy in leaving:
        copy.start()
    for copy in leaving:
        copy.wait()


def attend(n, me, rand, glob, pen, arrays, apart_out):
    apart_in = len(arrays) > 1
    shard = arrays[0].shape[-1]
    length = n * shard
    nblocks = length // BLK
    hbm = pl.BlockSpec(memory_space=pltpu.HBM)
    smem = pl.BlockSpec(memory_space=pltpu.SMEM)
    vmem = pl.BlockSpec(memory_space=pltpu.VMEM)
    if apart_out:
        out_shape = [jax.ShapeDtypeStruct((shard, PAIR), jnp.bfloat16)] * n
    else:
        out_shape = [jax.ShapeDtypeStruct((n, shard, PAIR), jnp.bfloat16)]
    return pl.pallas_call(
        functools.partial(attend_kernel, n, nblocks, apart_in, apart_out),
        out_shape=out_shape,
        in_specs=[smem, smem, smem, vmem] + [hbm] * len(arrays),
        out_specs=[hbm] * len(out_shape),
        scratch_shapes=[
            pltpu.VMEM((n, 3, PAIR, shard), jnp.bfloat16),
            pltpu.VMEM((length, PAIR), jnp.bfloat16),
            pltpu.VMEM((2, nblocks // 2, PAIR, PAIR), jnp.bfloat16),
            pltpu.VMEM((n, shard, PAIR), jnp.bfloat16),
            pltpu.VMEM((length, 2 * PAIR), jnp.float32),
            pltpu.SemaphoreType.DMA((n,)),
            pltpu.SemaphoreType.DMA((n,)),
        ],
        compiler_params=pltpu.CompilerParams(vmem_limit_bytes=60 * 1024 * 1024),
        cost_estimate=pl.CostEstimate(
            flops=15_000_000_000, bytes_accessed=4_000_000, transcendentals=0
        ),
        name="attend",
    )(me, rand, glob, pen, *arrays)


def project_kernel(n, ndp, slots, ahead, before, me_ref, *rest):
    arrays = sorted({i for i, _, _ in slots})
    pieces, rest = rest[: len(arrays)], rest[len(arrays) :]
    if before:
        before_ref, w, o_ref, a, a_sems = rest
    else:
        weights, rest = rest[:ndp], rest[ndp:]
        o_ref, ahead_ref, a, w, a_sems, w_sems, ahead_sems = rest
    me, dp = me_ref[0], me_ref[1]
    width = w.shape[1]
    tile = width // 4

    def piece_copy(slot):
        i, _, k = slots[slot]
        src = pieces[arrays.index(i)]
        src = src.at[me ^ k] if len(src.shape) == 3 else src
        dst = a.at[:, pl.ds(slot * PAIR, PAIR)]
        return pltpu.make_async_copy(src, dst, a_sems.at[slot])

    for slot in range(len(slots)):
        piece_copy(slot).start()
    if not before:
        held = n // ndp
        feats = weights[0].shape[0] // held

        def weight_copy(which, slot, part):
            _, p, k = which[slot]
            row = pl.multiple_of(lax.rem(me ^ k, held) * feats + p * PAIR, PAIR)
            dst, sems = (w, w_sems) if which is slots else (ahead_ref, ahead_sems)
            return pltpu.make_async_copy(
                weights[part].at[pl.ds(row, PAIR), :],
                dst.at[pl.ds(slot * PAIR, PAIR), :],
                sems.at[slot],
            )

        own = lax.div(me, held) ^ dp
        for r in range(ndp):

            @pl.when(own == r)
            def _():
                for which in (slots, ahead):
                    for slot in range(len(which)):
                        weight_copy(which, slot, r ^ (which[slot][2] // held)).start()

        for slot in range(len(slots)):
            weight_copy(slots, slot, 0).wait()
    for slot in range(len(slots)):
        piece_copy(slot).wait()
    for t in range(4):
        columns = slice(t * tile, (t + 1) * tile)
        total = jnp.dot(a[...], w[:, columns], preferred_element_type=jnp.float32)
        if before:
            total = total + before_ref[0, :, columns]
        o_ref[0, :, columns] = total.astype(o_ref.dtype)
    if not before:
        for slot in range(len(ahead)):
            weight_copy(ahead, slot, 0).wait()


def project_early(n, me, pieces, slots, ahead, weights):
    shard = pieces[0].shape[-2]
    ndp = len(weights)
    width = weights[0].shape[1]
    depth = len(slots) * PAIR
    hbm = pl.BlockSpec(memory_space=pl.ANY)
    return pl.pallas_call(
        functools.partial(project_kernel, n, ndp, slots, ahead, False),
        out_shape=[
            pltpu.VMEM((1, shard, width), jnp.float32),
            pltpu.VMEM((len(ahead) * PAIR, width), jnp.bfloat16),
        ],
        in_specs=[pl.BlockSpec(memory_space=pltpu.SMEM)] + [hbm] * (len(pieces) + ndp),
        out_specs=[pl.BlockSpec(memory_space=pltpu.VMEM)] * 2,
        scratch_shapes=[
            pltpu.VMEM((shard, depth), jnp.bfloat16),
            pltpu.VMEM((depth, width), jnp.bfloat16),
            pltpu.SemaphoreType.DMA((len(slots),)),
            pltpu.SemaphoreType.DMA((len(slots),)),
            pltpu.SemaphoreType.DMA((len(ahead),)),
        ],
        compiler_params=pltpu.CompilerParams(vmem_limit_bytes=24 * 1024 * 1024),
        cost_estimate=pl.CostEstimate(
            flops=2 * shard * depth * width, bytes_accessed=10_000_000, transcendentals=0
        ),
        name="project_early",
    )(me, *pieces, *weights)


def project_late(n, me, pieces, slots, before, rows):
    shard = pieces[0].shape[-2]
    width = rows.shape[1]
    depth = len(slots) * PAIR
    hbm = pl.BlockSpec(memory_space=pl.ANY)
    vmem = pl.BlockSpec(memory_space=pltpu.VMEM)
    before, rows = (pltpu.with_memory_space_constraint(x, pltpu.VMEM) for x in (before, rows))
    return pl.pallas_call(
        functools.partial(project_kernel, n, 0, slots, [], True),
        out_shape=jax.ShapeDtypeStruct((1, shard, width), jnp.bfloat16),
        in_specs=[pl.BlockSpec(memory_space=pltpu.SMEM)] + [hbm] * len(pieces) + [vmem, vmem],
        out_specs=vmem,
        scratch_shapes=[
            pltpu.VMEM((shard, depth), jnp.bfloat16),
            pltpu.SemaphoreType.DMA((len(slots),)),
        ],
        compiler_params=pltpu.CompilerParams(vmem_limit_bytes=24 * 1024 * 1024),
        cost_estimate=pl.CostEstimate(
            flops=2 * shard * depth * width, bytes_accessed=10_000_000, transcendentals=0
        ),
        name="project_late",
    )(me, *pieces, before, rows)


def gather_weight(ndp, weight):
    parts = {0: weight}
    bit = ndp // 2
    while bit:
        for r in list(parts):
            parts[r + bit] = lax.ppermute(parts[r], "dp", [(i, i ^ bit) for i in range(ndp)])
        bit //= 2
    return [parts[r] for r in range(ndp)]


def local_paired(n, ndp, queries, keys, values, random_blocks, global_blocks, out_weight):
    me = jnp.stack([lax.axis_index("seq"), lax.axis_index("dp")]).astype(jnp.int32)
    feats = queries.shape[1] // n
    length = queries.shape[2] * n
    nblocks = length // BLK
    pairs = feats // PAIR
    glob = global_blocks[0]

    def exchange(x):
        return lax.all_to_all(x, "seq", split_axis=0, concat_axis=0, tiled=True)

    def swap(arrays, order):
        got = {k: lax.ppermute(arrays[k], "seq", [(i, i ^ k) for i in range(n)]) for k in order}
        return [arrays[0]] + [got[k] for k in range(1, n)]

    near, far = list(range(1, n // 2)), list(range(n // 2, n))

    valid = jax.vmap(lambda r: candidate_blocks(nblocks, glob, r)[1])(random_blocks[0])
    pen = jnp.where(valid, 0.0, BIG).astype(jnp.float32)
    pen = jnp.transpose(pen.reshape(pairs, 2, nblocks, -1), (0, 2, 3, 1))
    rand = random_blocks[0].reshape(pairs, -1)

    last = pairs - 1
    arrived = [exchange(cut(n, p * PAIR, queries, keys, values)) for p in range(last)]
    messages = swap(cut_apart(n, last * PAIR, me, queries, keys, values), near + far)
    weights = gather_weight(ndp, lax.optimization_barrier((out_weight, messages[1]))[0])

    pieces, slots = [], []
    for p in range(last):
        outs = attend(n, me, rand[p], glob, pen[p], [arrived[p]], False)
        pieces.append(exchange(outs[0]))
        slots += [(p, p, k) for k in range(n)]
    outs = attend(n, me, rand[last], glob, pen[last], messages, True)
    outs, weights = lax.optimization_barrier((list(outs), weights))
    results = swap(outs, far + near)
    pieces += [results[k] for k in [0] + near]
    slots += [(last + i, last, k) for i, k in enumerate([0] + near)]
    late = [(i, last, k) for i, k in enumerate(far)]
    total, rows = project_early(n, me, pieces, slots, late, weights)
    return project_late(n, me, [results[k] for k in far], late, total, rows)


def solution(mesh):
    n, ndp = mesh.shape["seq"], mesh.shape["dp"]
    in_specs = (
        P("dp", None, "seq"),
        P("dp", None, "seq"),
        P("dp", None, "seq"),
        P("dp", "seq", None, None),
        P("dp", None),
        P("dp", None),
    )
    out_specs = P("dp", "seq", None)

    def local(queries, keys, *rest):
        feats, shard = queries.shape[1] // n, queries.shape[2]
        paired = feats % PAIR == 0 and shard % PAIR == 0 and n % ndp == 0
        paired = paired and n & (n - 1) == 0 and ndp & (ndp - 1) == 0
        body = functools.partial(local_paired, n, ndp) if paired else local_plain
        return body(queries, keys, *rest)

    return jax.shard_map(local, mesh=mesh, in_specs=in_specs, out_specs=out_specs, check_vma=False)
```

```python
import functools
import math

import jax
import jax.numpy as jnp
from jax import lax
from jax.experimental import pallas as pl
from jax.experimental.pallas import tpu as pltpu
from jax.sharding import PartitionSpec as P

HD = 64
BLK = 64
PAIR = 2 * HD
EXP_SCALE = HD ** (-0.5) * math.log2(math.e)
BIG = 1e30


def candidate_blocks(nblocks, glob, rand_h):
    rows = jnp.arange(nblocks, dtype=jnp.int32)
    window = jnp.stack([rows - 1, rows, rows + 1], axis=1)
    globs = jnp.broadcast_to(glob[None, :], (nblocks, glob.shape[0]))
    cand = jnp.concatenate([window, globs, rand_h], axis=1)
    inside = (cand >= 0) & (cand < nblocks)
    width = cand.shape[1]
    equal = cand[:, :, None] == cand[:, None, :]
    earlier = jnp.arange(width)[None, :] < jnp.arange(width)[:, None]
    repeated = jnp.any(equal & earlier[None, :, :], axis=2)
    return (jnp.clip(cand, 0, nblocks - 1), inside & ~repeated)


def head_attention(q_head, k_head, v_head, rand_h, glob):
    length = q_head.shape[1]
    nblocks = length // BLK
    scale = HD ** (-0.5)
    qb = q_head.reshape(HD, nblocks, BLK)
    kb = k_head.reshape(HD, nblocks, BLK)
    vb = v_head.reshape(HD, nblocks, BLK)
    index, valid = candidate_blocks(nblocks, glob, rand_h)
    group = math.gcd(nblocks, 32)
    turns = nblocks // group

    def one_group(turn):
        first = turn * group
        rows_index = lax.dynamic_slice_in_dim(index, first, group, 0)
        rows_valid = lax.dynamic_slice_in_dim(valid, first, group, 0)
        q_rows = lax.dynamic_slice_in_dim(qb, first, group, 1)
        k_rows = jnp.take(kb, rows_index, axis=1)
        v_rows = jnp.take(vb, rows_index, axis=1)
        scores = (
            jnp.einsum("dnq,dnck->nqck", q_rows, k_rows, preferred_element_type=jnp.float32) * scale
        )
        scores = jnp.where(rows_valid[:, None, :, None], scores, -jnp.inf)
        top = jnp.max(scores, axis=(2, 3), keepdims=True)
        expo = jnp.exp(scores - top)
        probs = (expo / jnp.sum(expo, axis=(2, 3), keepdims=True)).astype(jnp.bfloat16)
        return jnp.einsum(
            "nqck,dnck->dnq", probs, v_rows, preferred_element_type=jnp.float32
        ).astype(jnp.bfloat16)

    parts = lax.map(one_group, jnp.arange(turns, dtype=jnp.int32))
    blocks = jnp.transpose(parts, (1, 0, 2, 3)).reshape(HD, nblocks, BLK)
    qglob = jnp.take(qb, glob, axis=1)
    gscore = jnp.einsum("dgq,dk->gqk", qglob, k_head, preferred_element_type=jnp.float32) * scale
    gtop = jnp.max(gscore, axis=2, keepdims=True)
    gexp = jnp.exp(gscore - gtop)
    gprob = (gexp / jnp.sum(gexp, axis=2, keepdims=True)).astype(jnp.bfloat16)
    full = jnp.einsum("gqk,dk->dgq", gprob, v_head, preferred_element_type=jnp.float32).astype(
        jnp.bfloat16
    )
    blocks = blocks.at[:, glob, :].set(full)
    return blocks.reshape(HD, length)


def local_plain(queries, keys, values, random_blocks, global_blocks, out_weight):
    q_heads, k_heads, v_heads = (
        lax.all_to_all(queries[0], "seq", split_axis=0, concat_axis=1, tiled=True),
        lax.all_to_all(keys[0], "seq", split_axis=0, concat_axis=1, tiled=True),
        lax.all_to_all(values[0], "seq", split_axis=0, concat_axis=1, tiled=True),
    )
    count = q_heads.shape[0] // HD
    length = q_heads.shape[1]
    glob = global_blocks[0]

    def one_head(packed):
        q_head, k_head, v_head, rand_h = packed
        return head_attention(q_head, k_head, v_head, rand_h, glob)

    outputs = lax.map(
        one_head,
        (
            q_heads.reshape(count, HD, length),
            k_heads.reshape(count, HD, length),
            v_heads.reshape(count, HD, length),
            random_blocks[0],
        ),
    )
    attended = lax.all_to_all(
        outputs.reshape(count * HD, length), "seq", split_axis=1, concat_axis=0, tiled=True
    )
    result = lax.dot_general(
        attended,
        lax.all_gather(out_weight, "dp", axis=0, tiled=True),
        (((0,), (0,)), ((), ())),
        preferred_element_type=jnp.float32,
    )
    return result.astype(jnp.bfloat16)[None]


def cut_kernel(n, feats, row, q_ref, k_ref, v_ref, out, sems):
    copies = []
    for to in range(n):
        for i, src in enumerate((q_ref, k_ref, v_ref)):
            src = src.at[0, pl.ds(to * feats + row, PAIR), :]
            copies.append(pltpu.make_async_copy(src, out.at[to, i], sems.at[to, i]))
    for copy in copies:
        copy.start()
    for copy in copies:
        copy.wait()


def cut(n, row, queries, keys, values):
    feats = queries.shape[1] // n
    length = queries.shape[2]
    hbm = pl.BlockSpec(memory_space=pl.ANY)
    return pl.pallas_call(
        functools.partial(cut_kernel, n, feats, row),
        out_shape=pltpu.VMEM((n, 3, PAIR, length), queries.dtype),
        in_specs=[hbm, hbm, hbm],
        out_specs=pl.BlockSpec(memory_space=pltpu.VMEM),
        scratch_shapes=[pltpu.SemaphoreType.DMA((n, 3))],
        compiler_params=pltpu.CompilerParams(vmem_limit_bytes=56 * 1024 * 1024),
        name="cut",
    )(queries, keys, values)


def cut_apart_kernel(n, feats, row, me_ref, q_ref, k_ref, v_ref, *rest):
    outs = rest[:n]
    held, in_sems, out_sems = rest[n:]
    me = me_ref[0]

    def read(k, i):
        start = pl.multiple_of((me ^ k) * feats + row, PAIR)
        src = (q_ref, k_ref, v_ref)[i]
        return pltpu.make_async_copy(
            src.at[0, pl.ds(start, PAIR), :], held.at[k, i], in_sems.at[k, i]
        )

    def write(k):
        return pltpu.make_async_copy(held.at[k], outs[k], out_sems.at[k])

    for k in range(n):
        for i in range(3):
            read(k, i).start()
    for k in range(n):
        for i in range(3):
            read(k, i).wait()
        write(k).start()
    for k in range(n):
        write(k).wait()


def cut_apart(n, row, me, queries, keys, values):
    feats = queries.shape[1] // n
    length = queries.shape[2]
    hbm = pl.BlockSpec(memory_space=pltpu.HBM)
    return pl.pallas_call(
        functools.partial(cut_apart_kernel, n, feats, row),
        out_shape=[jax.ShapeDtypeStruct((3, PAIR, length), queries.dtype)] * n,
        in_specs=[pl.BlockSpec(memory_space=pltpu.SMEM), hbm, hbm, hbm],
        out_specs=[hbm] * n,
        scratch_shapes=[
            pltpu.VMEM((n, 3, PAIR, length), queries.dtype),
            pltpu.SemaphoreType.DMA((n, 3)),
            pltpu.SemaphoreType.DMA((n,)),
        ],
        name="cut_apart",
    )(me, queries, keys, values)


def swap_halves(x):
    return jnp.concatenate([x[:, BLK:], x[:, :BLK]], axis=1)


def attend_kernel(n, nblocks, apart_in, apart_out, me_ref, rand_ref, glob_ref, *rest):
    pen_ref, rest = rest[0], rest[1:]
    ins, rest = (rest[:n], rest[n:]) if apart_in else (rest[:1], rest[1:])
    outs, rest = (rest[:n], rest[n:]) if apart_out else (rest[:1], rest[1:])
    raw, kt, vv, ob, sg, in_sems, out_sems = rest
    me = me_ref[0]
    shard = raw.shape[3]
    per = shard // BLK
    tiles = shard // PAIR
    f32, bf16 = jnp.float32, jnp.bfloat16

    shards = [me ^ k for k in range(n)] if apart_in else list(range(n))
    arrivals = []
    for i, s in enumerate(shards):
        src = ins[i] if apart_in else ins[0].at[i]
        arrivals.append(pltpu.make_async_copy(src, raw.at[s], in_sems.at[i]))
    for copy in arrivals:
        copy.start()

    for s, copy in zip(shards, arrivals):
        copy.wait()
        for t in range(tiles):
            lanes = slice(t * PAIR, (t + 1) * PAIR)
            first = pl.multiple_of(s * shard + t * PAIR, PAIR)
            kt[pl.ds(first, PAIR), :] = raw[s, 1, :, lanes].T
            v = raw[s, 2, :, lanes]
            vv[0, s * tiles + t] = v
            vv[1, s * tiles + t] = swap_halves(v)

    low = lax.broadcasted_iota(jnp.int32, (BLK, PAIR), 1) < BLK
    zero = jnp.zeros((HD, PAIR), bf16)

    def queries_of(x, odd):
        y = swap_halves(x)
        a, b = (y, x) if odd else (x, y)
        return jnp.concatenate(
            [jnp.where(low, a[:HD], zero), jnp.where(low, zero, b[HD:])], axis=0
        )

    def key_rows(b):
        return kt[pl.ds(pl.multiple_of(b * BLK, BLK), BLK), :]

    def value_half(head, b, place):
        side = lax.rem(b + place, 2)
        return vv[side, lax.div(b, 2), head * HD : (head + 1) * HD, :]

    def finish(ot, total):
        t = (ot / total).astype(bf16).T
        return jnp.where(low, t[:BLK], t[BLK:])

    def sparse(j, qbd):
        shared = [jnp.maximum(j - 1, 0), j, jnp.minimum(j + 1, nblocks - 1), glob_ref[0], glob_ref[1]]
        cand = [
            shared + [rand_ref[(h * nblocks + j) * 3 + c] for c in range(3)] for h in range(2)
        ]
        k_rows = [key_rows(b) for b in shared]
        for c in range(5, 8):
            k_rows.append(jnp.where(low, key_rows(cand[0][c]), key_rows(cand[1][c])))
        scores = jnp.dot(jnp.concatenate(k_rows, axis=0), qbd, preferred_element_type=f32)
        top = jnp.max(scores, axis=0, keepdims=True) * EXP_SCALE
        pen = pen_ref[j]
        shift = jnp.where(low[:8], pen[:, 0:1], pen[:, 1:2]) + top
        probs = [
            jnp.exp2(scores[c * BLK : (c + 1) * BLK] * EXP_SCALE - shift[c : c + 1])
            for c in range(8)
        ]
        total = functools.reduce(
            jnp.add, [jnp.sum(p, axis=0, keepdims=True) for p in probs]
        )
        pt = jnp.concatenate([p.astype(bf16) for p in probs], axis=0)
        vcat = []
        for c in range(0, 8, 2):
            vcat.append(
                jnp.concatenate(
                    [
                        jnp.where(
                            low, value_half(h, cand[h][c], 0), value_half(h, cand[h][c + 1], 1)
                        )
                        for h in range(2)
                    ],
                    axis=0,
                )
            )
        ot = jnp.dot(jnp.concatenate(vcat, axis=1), pt, preferred_element_type=f32)
        return finish(ot, total)

    def tile_of(i):
        s = lax.div(i, tiles)
        first = pl.multiple_of(lax.rem(i, tiles) * PAIR, PAIR)
        return s, first

    def two_blocks(i, carry):
        s, first = tile_of(i)
        x = raw[s, 0, :, pl.ds(first, PAIR)]
        a = sparse(2 * i, queries_of(x, False))
        b = sparse(2 * i + 1, queries_of(x, True))
        ob[s, pl.ds(first, PAIR), :] = jnp.concatenate([a, b], axis=0)
        return carry

    lax.fori_loop(0, nblocks // 2, two_blocks, 0, unroll=8)

    places, columns = [], []
    for g in range(2):
        s, first = tile_of(lax.div(glob_ref[g], 2))
        x = raw[s, 0, :, pl.ds(first, PAIR)]
        odd = lax.rem(glob_ref[g], 2)
        columns.append(jnp.where(odd == 1, queries_of(x, True), queries_of(x, False)))
        places.append((s, pl.multiple_of(lax.rem(glob_ref[g], per) * BLK, BLK)))
    qbd = jnp.concatenate(columns, axis=1)
    top = jnp.full((1, 2 * PAIR), -jnp.inf, f32)
    for t in range(n):
        rows = slice(t * shard, (t + 1) * shard)
        scores = jnp.dot(kt[rows, :], qbd, preferred_element_type=f32)
        sg[rows, :] = scores
        top = jnp.maximum(top, jnp.max(scores, axis=0, keepdims=True))
    top = top * EXP_SCALE
    total = jnp.zeros((1, 2 * PAIR), f32)
    ot = jnp.zeros((PAIR, 2 * PAIR), f32)
    for t in range(n):
        p = jnp.exp2(sg[t * shard : (t + 1) * shard, :] * EXP_SCALE - top)
        total = total + jnp.sum(p, axis=0, keepdims=True)
        ot = ot + jnp.dot(raw[t, 2], p.astype(bf16), preferred_element_type=f32)
    for g, (s, place) in enumerate(places):
        lanes = slice(g * PAIR, (g + 1) * PAIR)
        ob[s, pl.ds(place, BLK), :] = finish(ot[:, lanes], total[:, lanes])

    if apart_out:
        leaving = [
            pltpu.make_async_copy(ob.at[me ^ k], outs[k], out_sems.at[k])
            for k in range(n)
        ]
    else:
        leaving = [pltpu.make_async_copy(ob, outs[0], out_sems.at[0])]
    for copy in leaving:
        copy.start()
    for copy in leaving:
        copy.wait()


def attend(n, me, rand, glob, pen, arrays, apart_out):
    apart_in = len(arrays) > 1
    shard = arrays[0].shape[-1]
    length = n * shard
    nblocks = length // BLK
    hbm = pl.BlockSpec(memory_space=pltpu.HBM)
    smem = pl.BlockSpec(memory_space=pltpu.SMEM)
    vmem = pl.BlockSpec(memory_space=pltpu.VMEM)
    if apart_out:
        out_shape = [jax.ShapeDtypeStruct((shard, PAIR), jnp.bfloat16)] * n
    else:
        out_shape = [jax.ShapeDtypeStruct((n, shard, PAIR), jnp.bfloat16)]
    return pl.pallas_call(
        functools.partial(attend_kernel, n, nblocks, apart_in, apart_out),
        out_shape=out_shape,
        in_specs=[smem, smem, smem, vmem] + [hbm] * len(arrays),
        out_specs=[hbm] * len(out_shape),
        scratch_shapes=[
            pltpu.VMEM((n, 3, PAIR, shard), jnp.bfloat16),
            pltpu.VMEM((length, PAIR), jnp.bfloat16),
            pltpu.VMEM((2, nblocks // 2, PAIR, PAIR), jnp.bfloat16),
            pltpu.VMEM((n, shard, PAIR), jnp.bfloat16),
            pltpu.VMEM((length, 2 * PAIR), jnp.float32),
            pltpu.SemaphoreType.DMA((n,)),
            pltpu.SemaphoreType.DMA((n,)),
        ],
        compiler_params=pltpu.CompilerParams(vmem_limit_bytes=60 * 1024 * 1024),
        cost_estimate=pl.CostEstimate(
            flops=15_000_000_000, bytes_accessed=4_000_000, transcendentals=0
        ),
        name="attend",
    )(me, rand, glob, pen, *arrays)


def project_kernel(n, ndp, slots, ahead, before, me_ref, *rest):
    arrays = sorted({i for i, _, _ in slots})
    pieces, rest = rest[: len(arrays)], rest[len(arrays) :]
    if before:
        before_ref, w, o_ref, a, a_sems, done, out_sems = rest
    else:
        weights, rest = rest[:ndp], rest[ndp:]
        o_ref, ahead_ref, a, w, a_sems, w_sems, ahead_sems = rest
    me, dp = me_ref[0], me_ref[1]
    width = w.shape[1]
    tile = width // 4

    def piece_copy(slot):
        i, _, k = slots[slot]
        src = pieces[arrays.index(i)]
        src = src.at[me ^ k] if len(src.shape) == 3 else src
        dst = a.at[:, pl.ds(slot * PAIR, PAIR)]
        return pltpu.make_async_copy(src, dst, a_sems.at[slot])

    def out_copy(t):
        columns = pl.ds(t * tile, tile)
        return pltpu.make_async_copy(done.at[:, columns], o_ref.at[0, :, columns], out_sems.at[t])

    for slot in range(len(slots)):
        piece_copy(slot).start()
    if not before:
        held = n // ndp
        feats = weights[0].shape[0] // held

        def weight_copy(which, slot, part):
            _, p, k = which[slot]
            row = pl.multiple_of(lax.rem(me ^ k, held) * feats + p * PAIR, PAIR)
            dst, sems = (w, w_sems) if which is slots else (ahead_ref, ahead_sems)
            return pltpu.make_async_copy(
                weights[part].at[pl.ds(row, PAIR), :],
                dst.at[pl.ds(slot * PAIR, PAIR), :],
                sems.at[slot],
            )

        own = lax.div(me, held) ^ dp
        for r in range(ndp):

            @pl.when(own == r)
            def _():
                for which in (slots, ahead):
                    for slot in range(len(which)):
                        weight_copy(which, slot, r ^ (which[slot][2] // held)).start()

        for slot in range(len(slots)):
            weight_copy(slots, slot, 0).wait()
    for slot in range(len(slots)):
        piece_copy(slot).wait()
    for t in range(4):
        columns = slice(t * tile, (t + 1) * tile)
        total = jnp.dot(a[...], w[:, columns], preferred_element_type=jnp.float32)
        if before:
            total = total + before_ref[0, :, columns]
        if before:
            done[:, columns] = total.astype(o_ref.dtype)
            out_copy(t).start()
        else:
            o_ref[0, :, columns] = total
    if before:
        for t in range(4):
            out_copy(t).wait()
    else:
        for slot in range(len(ahead)):
            weight_copy(ahead, slot, 0).wait()


def project_early(n, me, pieces, slots, ahead, weights):
    shard = pieces[0].shape[-2]
    ndp = len(weights)
    width = weights[0].shape[1]
    depth = len(slots) * PAIR
    hbm = pl.BlockSpec(memory_space=pl.ANY)
    return pl.pallas_call(
        functools.partial(project_kernel, n, ndp, slots, ahead, False),
        out_shape=[
            pltpu.VMEM((1, shard, width), jnp.float32),
            pltpu.VMEM((len(ahead) * PAIR, width), jnp.bfloat16),
        ],
        in_specs=[pl.BlockSpec(memory_space=pltpu.SMEM)] + [hbm] * (len(pieces) + ndp),
        out_specs=[pl.BlockSpec(memory_space=pltpu.VMEM)] * 2,
        scratch_shapes=[
            pltpu.VMEM((shard, depth), jnp.bfloat16),
            pltpu.VMEM((depth, width), jnp.bfloat16),
            pltpu.SemaphoreType.DMA((len(slots),)),
            pltpu.SemaphoreType.DMA((len(slots),)),
            pltpu.SemaphoreType.DMA((len(ahead),)),
        ],
        compiler_params=pltpu.CompilerParams(vmem_limit_bytes=24 * 1024 * 1024),
        cost_estimate=pl.CostEstimate(
            flops=2 * shard * depth * width, bytes_accessed=10_000_000, transcendentals=0
        ),
        name="project_early",
    )(me, *pieces, *weights)


def project_late(n, me, pieces, slots, before, rows):
    shard = pieces[0].shape[-2]
    width = rows.shape[1]
    depth = len(slots) * PAIR
    hbm = pl.BlockSpec(memory_space=pl.ANY)
    vmem = pl.BlockSpec(memory_space=pltpu.VMEM)
    before, rows = (pltpu.with_memory_space_constraint(x, pltpu.VMEM) for x in (before, rows))
    return pl.pallas_call(
        functools.partial(project_kernel, n, 0, slots, [], True),
        out_shape=jax.ShapeDtypeStruct((1, shard, width), jnp.bfloat16),
        in_specs=[pl.BlockSpec(memory_space=pltpu.SMEM)] + [hbm] * len(pieces) + [vmem, vmem],
        out_specs=hbm,
        scratch_shapes=[
            pltpu.VMEM((shard, depth), jnp.bfloat16),
            pltpu.SemaphoreType.DMA((len(slots),)),
            pltpu.VMEM((shard, width), jnp.bfloat16),
            pltpu.SemaphoreType.DMA((4,)),
        ],
        compiler_params=pltpu.CompilerParams(vmem_limit_bytes=24 * 1024 * 1024),
        cost_estimate=pl.CostEstimate(
            flops=2 * shard * depth * width, bytes_accessed=10_000_000, transcendentals=0
        ),
        name="project_late",
    )(me, *pieces, before, rows)


def gather_weight(ndp, weight):
    parts = {0: weight}
    bit = ndp // 2
    while bit:
        for r in list(parts):
            parts[r + bit] = lax.ppermute(parts[r], "dp", [(i, i ^ bit) for i in range(ndp)])
        bit //= 2
    return [parts[r] for r in range(ndp)]


def local_paired(n, ndp, queries, keys, values, random_blocks, global_blocks, out_weight):
    me = jnp.stack([lax.axis_index("seq"), lax.axis_index("dp")]).astype(jnp.int32)
    feats = queries.shape[1] // n
    length = queries.shape[2] * n
    nblocks = length // BLK
    pairs = feats // PAIR
    glob = global_blocks[0]

    def exchange(x):
        return lax.all_to_all(x, "seq", split_axis=0, concat_axis=0, tiled=True)

    def swap(arrays, order):
        got = {k: lax.ppermute(arrays[k], "seq", [(i, i ^ k) for i in range(n)]) for k in order}
        return [arrays[0]] + [got[k] for k in range(1, n)]

    near, far = list(range(1, n // 2)), list(range(n // 2, n))

    valid = jax.vmap(lambda r: candidate_blocks(nblocks, glob, r)[1])(random_blocks[0])
    pen = jnp.where(valid, 0.0, BIG).astype(jnp.float32)
    pen = jnp.transpose(pen.reshape(pairs, 2, nblocks, -1), (0, 2, 3, 1))
    rand = random_blocks[0].reshape(pairs, -1)

    last = pairs - 1
    arrived = [exchange(cut(n, p * PAIR, queries, keys, values)) for p in range(last)]
    messages = swap(cut_apart(n, last * PAIR, me, queries, keys, values), near + far)
    weights = gather_weight(ndp, lax.optimization_barrier((out_weight, messages[1]))[0])

    pieces, slots = [], []
    for p in range(last):
        outs = attend(n, me, rand[p], glob, pen[p], [arrived[p]], False)
        pieces.append(exchange(outs[0]))
        slots += [(p, p, k) for k in range(n)]
    outs = attend(n, me, rand[last], glob, pen[last], messages, True)
    outs, weights = lax.optimization_barrier((list(outs), weights))
    results = swap(outs, far + near)
    pieces += [results[k] for k in [0] + near]
    slots += [(last + i, last, k) for i, k in enumerate([0] + near)]
    late = [(i, last, k) for i, k in enumerate(far)]
    total, rows = project_early(n, me, pieces, slots, late, weights)
    return project_late(n, me, [results[k] for k in far], late, total, rows)


def solution(mesh):
    n, ndp = mesh.shape["seq"], mesh.shape["dp"]
    in_specs = (
        P("dp", None, "seq"),
        P("dp", None, "seq"),
        P("dp", None, "seq"),
        P("dp", "seq", None, None),
        P("dp", None),
        P("dp", None),
    )
    out_specs = P("dp", "seq", None)

    def local(queries, keys, *rest):
        feats, shard = queries.shape[1] // n, queries.shape[2]
        paired = feats % PAIR == 0 and shard % PAIR == 0 and n % ndp == 0
        paired = paired and n & (n - 1) == 0 and ndp & (ndp - 1) == 0
        body = functools.partial(local_paired, n, ndp) if paired else local_plain
        return body(queries, keys, *rest)

    return jax.shard_map(local, mesh=mesh, in_specs=in_specs, out_specs=out_specs, check_vma=False)
```

```python
import functools
import math

import jax
import jax.numpy as jnp
from jax import lax
from jax.experimental import pallas as pl
from jax.experimental.pallas import tpu as pltpu
from jax.sharding import PartitionSpec as P

HD = 64
BLK = 64
PAIR = 2 * HD
EXP_SCALE = HD ** (-0.5) * math.log2(math.e)
BIG = 1e30


def candidate_blocks(nblocks, glob, rand_h):
    rows = jnp.arange(nblocks, dtype=jnp.int32)
    window = jnp.stack([rows - 1, rows, rows + 1], axis=1)
    globs = jnp.broadcast_to(glob[None, :], (nblocks, glob.shape[0]))
    cand = jnp.concatenate([window, globs, rand_h], axis=1)
    inside = (cand >= 0) & (cand < nblocks)
    width = cand.shape[1]
    equal = cand[:, :, None] == cand[:, None, :]
    earlier = jnp.arange(width)[None, :] < jnp.arange(width)[:, None]
    repeated = jnp.any(equal & earlier[None, :, :], axis=2)
    return (jnp.clip(cand, 0, nblocks - 1), inside & ~repeated)


def head_attention(q_head, k_head, v_head, rand_h, glob):
    length = q_head.shape[1]
    nblocks = length // BLK
    scale = HD ** (-0.5)
    qb = q_head.reshape(HD, nblocks, BLK)
    kb = k_head.reshape(HD, nblocks, BLK)
    vb = v_head.reshape(HD, nblocks, BLK)
    index, valid = candidate_blocks(nblocks, glob, rand_h)
    group = math.gcd(nblocks, 32)
    turns = nblocks // group

    def one_group(turn):
        first = turn * group
        rows_index = lax.dynamic_slice_in_dim(index, first, group, 0)
        rows_valid = lax.dynamic_slice_in_dim(valid, first, group, 0)
        q_rows = lax.dynamic_slice_in_dim(qb, first, group, 1)
        k_rows = jnp.take(kb, rows_index, axis=1)
        v_rows = jnp.take(vb, rows_index, axis=1)
        scores = (
            jnp.einsum("dnq,dnck->nqck", q_rows, k_rows, preferred_element_type=jnp.float32) * scale
        )
        scores = jnp.where(rows_valid[:, None, :, None], scores, -jnp.inf)
        top = jnp.max(scores, axis=(2, 3), keepdims=True)
        expo = jnp.exp(scores - top)
        probs = (expo / jnp.sum(expo, axis=(2, 3), keepdims=True)).astype(jnp.bfloat16)
        return jnp.einsum(
            "nqck,dnck->dnq", probs, v_rows, preferred_element_type=jnp.float32
        ).astype(jnp.bfloat16)

    parts = lax.map(one_group, jnp.arange(turns, dtype=jnp.int32))
    blocks = jnp.transpose(parts, (1, 0, 2, 3)).reshape(HD, nblocks, BLK)
    qglob = jnp.take(qb, glob, axis=1)
    gscore = jnp.einsum("dgq,dk->gqk", qglob, k_head, preferred_element_type=jnp.float32) * scale
    gtop = jnp.max(gscore, axis=2, keepdims=True)
    gexp = jnp.exp(gscore - gtop)
    gprob = (gexp / jnp.sum(gexp, axis=2, keepdims=True)).astype(jnp.bfloat16)
    full = jnp.einsum("gqk,dk->dgq", gprob, v_head, preferred_element_type=jnp.float32).astype(
        jnp.bfloat16
    )
    blocks = blocks.at[:, glob, :].set(full)
    return blocks.reshape(HD, length)


def local_plain(queries, keys, values, random_blocks, global_blocks, out_weight):
    q_heads, k_heads, v_heads = (
        lax.all_to_all(queries[0], "seq", split_axis=0, concat_axis=1, tiled=True),
        lax.all_to_all(keys[0], "seq", split_axis=0, concat_axis=1, tiled=True),
        lax.all_to_all(values[0], "seq", split_axis=0, concat_axis=1, tiled=True),
    )
    count = q_heads.shape[0] // HD
    length = q_heads.shape[1]
    glob = global_blocks[0]

    def one_head(packed):
        q_head, k_head, v_head, rand_h = packed
        return head_attention(q_head, k_head, v_head, rand_h, glob)

    outputs = lax.map(
        one_head,
        (
            q_heads.reshape(count, HD, length),
            k_heads.reshape(count, HD, length),
            v_heads.reshape(count, HD, length),
            random_blocks[0],
        ),
    )
    attended = lax.all_to_all(
        outputs.reshape(count * HD, length), "seq", split_axis=1, concat_axis=0, tiled=True
    )
    result = lax.dot_general(
        attended,
        lax.all_gather(out_weight, "dp", axis=0, tiled=True),
        (((0,), (0,)), ((), ())),
        preferred_element_type=jnp.float32,
    )
    return result.astype(jnp.bfloat16)[None]


def cut_kernel(n, feats, row, q_ref, k_ref, v_ref, out, sems):
    copies = []
    for to in range(n):
        for i, src in enumerate((q_ref, k_ref, v_ref)):
            src = src.at[0, pl.ds(to * feats + row, PAIR), :]
            copies.append(pltpu.make_async_copy(src, out.at[to, i], sems.at[to, i]))
    for copy in copies:
        copy.start()
    for copy in copies:
        copy.wait()


def cut(n, row, queries, keys, values):
    feats = queries.shape[1] // n
    length = queries.shape[2]
    hbm = pl.BlockSpec(memory_space=pl.ANY)
    return pl.pallas_call(
        functools.partial(cut_kernel, n, feats, row),
        out_shape=pltpu.VMEM((n, 3, PAIR, length), queries.dtype),
        in_specs=[hbm, hbm, hbm],
        out_specs=pl.BlockSpec(memory_space=pltpu.VMEM),
        scratch_shapes=[pltpu.SemaphoreType.DMA((n, 3))],
        compiler_params=pltpu.CompilerParams(vmem_limit_bytes=56 * 1024 * 1024),
        name="cut",
    )(queries, keys, values)


def cut_apart_kernel(n, feats, row, me_ref, q_ref, k_ref, v_ref, *rest):
    outs = rest[:n]
    held, in_sems, out_sems = rest[n:]
    me = me_ref[0]

    def read(k, i):
        start = pl.multiple_of((me ^ k) * feats + row, PAIR)
        src = (q_ref, k_ref, v_ref)[i]
        return pltpu.make_async_copy(
            src.at[0, pl.ds(start, PAIR), :], held.at[k, i], in_sems.at[k, i]
        )

    def write(k):
        return pltpu.make_async_copy(held.at[k], outs[k], out_sems.at[k])

    for k in range(n):
        for i in range(3):
            read(k, i).start()
    for k in range(n):
        for i in range(3):
            read(k, i).wait()
        write(k).start()
    for k in range(n):
        write(k).wait()


def cut_apart(n, row, me, queries, keys, values):
    feats = queries.shape[1] // n
    length = queries.shape[2]
    hbm = pl.BlockSpec(memory_space=pltpu.HBM)
    return pl.pallas_call(
        functools.partial(cut_apart_kernel, n, feats, row),
        out_shape=[jax.ShapeDtypeStruct((3, PAIR, length), queries.dtype)] * n,
        in_specs=[pl.BlockSpec(memory_space=pltpu.SMEM), hbm, hbm, hbm],
        out_specs=[hbm] * n,
        scratch_shapes=[
            pltpu.VMEM((n, 3, PAIR, length), queries.dtype),
            pltpu.SemaphoreType.DMA((n, 3)),
            pltpu.SemaphoreType.DMA((n,)),
        ],
        name="cut_apart",
    )(me, queries, keys, values)


def swap_halves(x):
    return jnp.concatenate([x[:, BLK:], x[:, :BLK]], axis=1)


def attend_kernel(n, nblocks, apart_in, apart_out, me_ref, rand_ref, glob_ref, *rest):
    pen_ref, rest = rest[0], rest[1:]
    ins, rest = (rest[:n], rest[n:]) if apart_in else (rest[:1], rest[1:])
    outs, rest = (rest[:n], rest[n:]) if apart_out else (rest[:1], rest[1:])
    raw, kt, vv, ob, sg, in_sems, out_sems = rest
    ob = ob if apart_out else outs[0]
    me = me_ref[0]
    shard = raw.shape[3]
    per = shard // BLK
    tiles = shard // PAIR
    f32, bf16 = jnp.float32, jnp.bfloat16

    shards = [me ^ k for k in range(n)] if apart_in else list(range(n))
    arrivals = []
    for i, s in enumerate(shards):
        src = ins[i] if apart_in else ins[0].at[i]
        arrivals.append(pltpu.make_async_copy(src, raw.at[s], in_sems.at[i]))
    for copy in arrivals:
        copy.start()

    for s, copy in zip(shards, arrivals):
        copy.wait()
        for t in range(tiles):
            lanes = slice(t * PAIR, (t + 1) * PAIR)
            first = pl.multiple_of(s * shard + t * PAIR, PAIR)
            kt[pl.ds(first, PAIR), :] = raw[s, 1, :, lanes].T
            v = raw[s, 2, :, lanes]
            vv[0, s * tiles + t] = v
            vv[1, s * tiles + t] = swap_halves(v)

    low = lax.broadcasted_iota(jnp.int32, (BLK, PAIR), 1) < BLK
    zero = jnp.zeros((HD, PAIR), bf16)

    def queries_of(x, odd):
        y = swap_halves(x)
        a, b = (y, x) if odd else (x, y)
        return jnp.concatenate(
            [jnp.where(low, a[:HD], zero), jnp.where(low, zero, b[HD:])], axis=0
        )

    def key_rows(b):
        return kt[pl.ds(pl.multiple_of(b * BLK, BLK), BLK), :]

    def value_half(head, b, place):
        side = lax.rem(b + place, 2)
        return vv[side, lax.div(b, 2), head * HD : (head + 1) * HD, :]

    def finish(ot, total):
        t = (ot / total).astype(bf16).T
        return jnp.where(low, t[:BLK], t[BLK:])

    def sparse(j, qbd):
        shared = [jnp.maximum(j - 1, 0), j, jnp.minimum(j + 1, nblocks - 1), glob_ref[0], glob_ref[1]]
        cand = [
            shared + [rand_ref[(h * nblocks + j) * 3 + c] for c in range(3)] for h in range(2)
        ]
        k_rows = [key_rows(b) for b in shared]
        for c in range(5, 8):
            k_rows.append(jnp.where(low, key_rows(cand[0][c]), key_rows(cand[1][c])))
        scores = jnp.dot(jnp.concatenate(k_rows, axis=0), qbd, preferred_element_type=f32)
        top = jnp.max(scores, axis=0, keepdims=True) * EXP_SCALE
        pen = pen_ref[j]
        shift = jnp.where(low[:8], pen[:, 0:1], pen[:, 1:2]) + top
        probs = [
            jnp.exp2(scores[c * BLK : (c + 1) * BLK] * EXP_SCALE - shift[c : c + 1])
            for c in range(8)
        ]
        total = functools.reduce(
            jnp.add, [jnp.sum(p, axis=0, keepdims=True) for p in probs]
        )
        pt = jnp.concatenate([p.astype(bf16) for p in probs], axis=0)
        vcat = []
        for c in range(0, 8, 2):
            vcat.append(
                jnp.concatenate(
                    [
                        jnp.where(
                            low, value_half(h, cand[h][c], 0), value_half(h, cand[h][c + 1], 1)
                        )
                        for h in range(2)
                    ],
                    axis=0,
                )
            )
        ot = jnp.dot(jnp.concatenate(vcat, axis=1), pt, preferred_element_type=f32)
        return finish(ot, total)

    def tile_of(i):
        s = lax.div(i, tiles)
        first = pl.multiple_of(lax.rem(i, tiles) * PAIR, PAIR)
        return s, first

    def two_blocks(i, carry):
        s, first = tile_of(i)
        x = raw[s, 0, :, pl.ds(first, PAIR)]
        a = sparse(2 * i, queries_of(x, False))
        b = sparse(2 * i + 1, queries_of(x, True))
        ob[s, pl.ds(first, PAIR), :] = jnp.concatenate([a, b], axis=0)
        return carry

    lax.fori_loop(0, nblocks // 2, two_blocks, 0, unroll=8)

    places, columns = [], []
    for g in range(2):
        s, first = tile_of(lax.div(glob_ref[g], 2))
        x = raw[s, 0, :, pl.ds(first, PAIR)]
        odd = lax.rem(glob_ref[g], 2)
        columns.append(jnp.where(odd == 1, queries_of(x, True), queries_of(x, False)))
        places.append((s, pl.multiple_of(lax.rem(glob_ref[g], per) * BLK, BLK)))
    qbd = jnp.concatenate(columns, axis=1)
    top = jnp.full((1, 2 * PAIR), -jnp.inf, f32)
    for t in range(n):
        rows = slice(t * shard, (t + 1) * shard)
        scores = jnp.dot(kt[rows, :], qbd, preferred_element_type=f32)
        sg[rows, :] = scores
        top = jnp.maximum(top, jnp.max(scores, axis=0, keepdims=True))
    top = top * EXP_SCALE
    total = jnp.zeros((1, 2 * PAIR), f32)
    ot = jnp.zeros((PAIR, 2 * PAIR), f32)
    for t in range(n):
        p = jnp.exp2(sg[t * shard : (t + 1) * shard, :] * EXP_SCALE - top)
        total = total + jnp.sum(p, axis=0, keepdims=True)
        ot = ot + jnp.dot(raw[t, 2], p.astype(bf16), preferred_element_type=f32)
    for g, (s, place) in enumerate(places):
        lanes = slice(g * PAIR, (g + 1) * PAIR)
        ob[s, pl.ds(place, BLK), :] = finish(ot[:, lanes], total[:, lanes])

    if apart_out:
        leaving = [
            pltpu.make_async_copy(ob.at[me ^ k], outs[k], out_sems.at[k])
            for k in range(n)
        ]
        for copy in leaving:
            copy.start()
        for copy in leaving:
            copy.wait()


def attend(n, me, rand, glob, pen, arrays, apart_out):
    apart_in = len(arrays) > 1
    shard = arrays[0].shape[-1]
    length = n * shard
    nblocks = length // BLK
    hbm = pl.BlockSpec(memory_space=pltpu.HBM)
    smem = pl.BlockSpec(memory_space=pltpu.SMEM)
    vmem = pl.BlockSpec(memory_space=pltpu.VMEM)
    if apart_out:
        out_shape = [jax.ShapeDtypeStruct((shard, PAIR), jnp.bfloat16)] * n
    else:
        out_shape = [pltpu.VMEM((n, shard, PAIR), jnp.bfloat16)]
    return pl.pallas_call(
        functools.partial(attend_kernel, n, nblocks, apart_in, apart_out),
        out_shape=out_shape,
        in_specs=[smem, smem, smem, vmem] + [hbm] * len(arrays),
        out_specs=[hbm] * n if apart_out else [vmem],
        scratch_shapes=[
            pltpu.VMEM((n, 3, PAIR, shard), jnp.bfloat16),
            pltpu.VMEM((length, PAIR), jnp.bfloat16),
            pltpu.VMEM((2, nblocks // 2, PAIR, PAIR), jnp.bfloat16),
            pltpu.VMEM((n, shard, PAIR), jnp.bfloat16),
            pltpu.VMEM((length, 2 * PAIR), jnp.float32),
            pltpu.SemaphoreType.DMA((n,)),
            pltpu.SemaphoreType.DMA((n,)),
        ],
        compiler_params=pltpu.CompilerParams(vmem_limit_bytes=56 * 1024 * 1024),
        cost_estimate=pl.CostEstimate(
            flops=15_000_000_000, bytes_accessed=4_000_000, transcendentals=0
        ),
        name="attend",
    )(me, rand, glob, pen, *arrays)


def project_kernel(n, ndp, slots, ahead, before, me_ref, *rest):
    arrays = sorted({i for i, _, _ in slots})
    pieces, rest = rest[: len(arrays)], rest[len(arrays) :]
    if before:
        before_ref, w, o_ref, a, a_sems, done, out_sems = rest
    else:
        weights, rest = rest[:ndp], rest[ndp:]
        o_ref, ahead_ref, a, w, a_sems, w_sems, ahead_sems = rest
    me, dp = me_ref[0], me_ref[1]
    width = w.shape[1]
    tile = width // 4

    def piece_copy(slot):
        i, _, k = slots[slot]
        src = pieces[arrays.index(i)]
        src = src.at[me ^ k] if len(src.shape) == 3 else src
        dst = a.at[:, pl.ds(slot * PAIR, PAIR)]
        return pltpu.make_async_copy(src, dst, a_sems.at[slot])

    def out_copy(t):
        columns = pl.ds(t * tile, tile)
        return pltpu.make_async_copy(done.at[:, columns], o_ref.at[0, :, columns], out_sems.at[t])

    for slot in range(len(slots)):
        piece_copy(slot).start()
    if not before:
        held = n // ndp
        feats = weights[0].shape[0] // held

        def weight_copy(which, slot, part):
            _, p, k = which[slot]
            row = pl.multiple_of(lax.rem(me ^ k, held) * feats + p * PAIR, PAIR)
            dst, sems = (w, w_sems) if which is slots else (ahead_ref, ahead_sems)
            return pltpu.make_async_copy(
                weights[part].at[pl.ds(row, PAIR), :],
                dst.at[pl.ds(slot * PAIR, PAIR), :],
                sems.at[slot],
            )

        own = lax.div(me, held) ^ dp
        for r in range(ndp):

            @pl.when(own == r)
            def _():
                for which in (slots, ahead):
                    for slot in range(len(which)):
                        weight_copy(which, slot, r ^ (which[slot][2] // held)).start()

        for slot in range(len(slots)):
            weight_copy(slots, slot, 0).wait()
    for slot in range(len(slots)):
        piece_copy(slot).wait()
    for t in range(4):
        columns = slice(t * tile, (t + 1) * tile)
        total = jnp.dot(a[...], w[:, columns], preferred_element_type=jnp.float32)
        if before:
            total = total + before_ref[0, :, columns]
        if before:
            done[:, columns] = total.astype(o_ref.dtype)
            out_copy(t).start()
        else:
            o_ref[0, :, columns] = total
    if before:
        for t in range(4):
            out_copy(t).wait()
    else:
        for slot in range(len(ahead)):
            weight_copy(ahead, slot, 0).wait()


def project_early(n, me, pieces, slots, ahead, weights):
    shard = pieces[0].shape[-2]
    ndp = len(weights)
    width = weights[0].shape[1]
    depth = len(slots) * PAIR
    hbm = pl.BlockSpec(memory_space=pl.ANY)
    return pl.pallas_call(
        functools.partial(project_kernel, n, ndp, slots, ahead, False),
        out_shape=[
            pltpu.VMEM((1, shard, width), jnp.float32),
            pltpu.VMEM((len(ahead) * PAIR, width), jnp.bfloat16),
        ],
        in_specs=[pl.BlockSpec(memory_space=pltpu.SMEM)] + [hbm] * (len(pieces) + ndp),
        out_specs=[pl.BlockSpec(memory_space=pltpu.VMEM)] * 2,
        scratch_shapes=[
            pltpu.VMEM((shard, depth), jnp.bfloat16),
            pltpu.VMEM((depth, width), jnp.bfloat16),
            pltpu.SemaphoreType.DMA((len(slots),)),
            pltpu.SemaphoreType.DMA((len(slots),)),
            pltpu.SemaphoreType.DMA((len(ahead),)),
        ],
        compiler_params=pltpu.CompilerParams(vmem_limit_bytes=24 * 1024 * 1024),
        cost_estimate=pl.CostEstimate(
            flops=2 * shard * depth * width, bytes_accessed=10_000_000, transcendentals=0
        ),
        name="project_early",
    )(me, *pieces, *weights)


def project_late(n, me, pieces, slots, before, rows):
    shard = pieces[0].shape[-2]
    width = rows.shape[1]
    depth = len(slots) * PAIR
    hbm = pl.BlockSpec(memory_space=pl.ANY)
    vmem = pl.BlockSpec(memory_space=pltpu.VMEM)
    before, rows = (pltpu.with_memory_space_constraint(x, pltpu.VMEM) for x in (before, rows))
    return pl.pallas_call(
        functools.partial(project_kernel, n, 0, slots, [], True),
        out_shape=jax.ShapeDtypeStruct((1, shard, width), jnp.bfloat16),
        in_specs=[pl.BlockSpec(memory_space=pltpu.SMEM)] + [hbm] * len(pieces) + [vmem, vmem],
        out_specs=hbm,
        scratch_shapes=[
            pltpu.VMEM((shard, depth), jnp.bfloat16),
            pltpu.SemaphoreType.DMA((len(slots),)),
            pltpu.VMEM((shard, width), jnp.bfloat16),
            pltpu.SemaphoreType.DMA((4,)),
        ],
        compiler_params=pltpu.CompilerParams(vmem_limit_bytes=24 * 1024 * 1024),
        cost_estimate=pl.CostEstimate(
            flops=2 * shard * depth * width, bytes_accessed=10_000_000, transcendentals=0
        ),
        name="project_late",
    )(me, *pieces, before, rows)


def gather_weight(ndp, weight):
    parts = {0: weight}
    bit = ndp // 2
    while bit:
        for r in list(parts):
            parts[r + bit] = lax.ppermute(parts[r], "dp", [(i, i ^ bit) for i in range(ndp)])
        bit //= 2
    return [parts[r] for r in range(ndp)]


def local_paired(n, ndp, queries, keys, values, random_blocks, global_blocks, out_weight):
    me = jnp.stack([lax.axis_index("seq"), lax.axis_index("dp")]).astype(jnp.int32)
    feats = queries.shape[1] // n
    length = queries.shape[2] * n
    nblocks = length // BLK
    pairs = feats // PAIR
    glob = global_blocks[0]

    def exchange(x):
        return lax.all_to_all(x, "seq", split_axis=0, concat_axis=0, tiled=True)

    def swap(arrays, order):
        got = {k: lax.ppermute(arrays[k], "seq", [(i, i ^ k) for i in range(n)]) for k in order}
        return [arrays[0]] + [got[k] for k in range(1, n)]

    near, far = list(range(1, n // 2)), list(range(n // 2, n))

    valid = jax.vmap(lambda r: candidate_blocks(nblocks, glob, r)[1])(random_blocks[0])
    pen = jnp.where(valid, 0.0, BIG).astype(jnp.float32)
    pen = jnp.transpose(pen.reshape(pairs, 2, nblocks, -1), (0, 2, 3, 1))
    rand = random_blocks[0].reshape(pairs, -1)

    last = pairs - 1
    arrived = [exchange(cut(n, p * PAIR, queries, keys, values)) for p in range(last)]
    messages = swap(cut_apart(n, last * PAIR, me, queries, keys, values), near + far)
    weights = gather_weight(ndp, lax.optimization_barrier((out_weight, messages[1]))[0])

    pieces, slots = [], []
    for p in range(last):
        outs = attend(n, me, rand[p], glob, pen[p], [arrived[p]], False)
        pieces.append(exchange(outs[0]))
        slots += [(p, p, k) for k in range(n)]
    outs = attend(n, me, rand[last], glob, pen[last], messages, True)
    outs, weights = lax.optimization_barrier((list(outs), weights))
    results = swap(outs, far[::-1] + near)
    pieces += [results[k] for k in [0] + near]
    slots += [(last + i, last, k) for i, k in enumerate([0] + near)]
    late = [(i, last, k) for i, k in enumerate(far)]
    total, rows = project_early(n, me, pieces, slots, late, weights)
    return project_late(n, me, [results[k] for k in far], late, total, rows)


def solution(mesh):
    n, ndp = mesh.shape["seq"], mesh.shape["dp"]
    in_specs = (
        P("dp", None, "seq"),
        P("dp", None, "seq"),
        P("dp", None, "seq"),
        P("dp", "seq", None, None),
        P("dp", None),
        P("dp", None),
    )
    out_specs = P("dp", "seq", None)

    def local(queries, keys, *rest):
        feats, shard = queries.shape[1] // n, queries.shape[2]
        paired = feats % PAIR == 0 and shard % PAIR == 0 and n % ndp == 0
        paired = paired and n & (n - 1) == 0 and ndp & (ndp - 1) == 0
        body = functools.partial(local_paired, n, ndp) if paired else local_plain
        return body(queries, keys, *rest)

    return jax.shard_map(local, mesh=mesh, in_specs=in_specs, out_specs=out_specs, check_vma=False)
```

```python
import functools
import math

import jax
import jax.numpy as jnp
from jax import lax
from jax.experimental import pallas as pl
from jax.experimental.pallas import tpu as pltpu
from jax.sharding import PartitionSpec as P

HD = 64
BLK = 64
PAIR = 2 * HD
EXP_SCALE = HD ** (-0.5) * math.log2(math.e)
BIG = 1e30


def candidate_blocks(nblocks, glob, rand_h):
    rows = jnp.arange(nblocks, dtype=jnp.int32)
    window = jnp.stack([rows - 1, rows, rows + 1], axis=1)
    globs = jnp.broadcast_to(glob[None, :], (nblocks, glob.shape[0]))
    cand = jnp.concatenate([window, globs, rand_h], axis=1)
    inside = (cand >= 0) & (cand < nblocks)
    width = cand.shape[1]
    equal = cand[:, :, None] == cand[:, None, :]
    earlier = jnp.arange(width)[None, :] < jnp.arange(width)[:, None]
    repeated = jnp.any(equal & earlier[None, :, :], axis=2)
    return (jnp.clip(cand, 0, nblocks - 1), inside & ~repeated)


def head_attention(q_head, k_head, v_head, rand_h, glob):
    length = q_head.shape[1]
    nblocks = length // BLK
    scale = HD ** (-0.5)
    qb = q_head.reshape(HD, nblocks, BLK)
    kb = k_head.reshape(HD, nblocks, BLK)
    vb = v_head.reshape(HD, nblocks, BLK)
    index, valid = candidate_blocks(nblocks, glob, rand_h)
    group = math.gcd(nblocks, 32)
    turns = nblocks // group

    def one_group(turn):
        first = turn * group
        rows_index = lax.dynamic_slice_in_dim(index, first, group, 0)
        rows_valid = lax.dynamic_slice_in_dim(valid, first, group, 0)
        q_rows = lax.dynamic_slice_in_dim(qb, first, group, 1)
        k_rows = jnp.take(kb, rows_index, axis=1)
        v_rows = jnp.take(vb, rows_index, axis=1)
        scores = (
            jnp.einsum("dnq,dnck->nqck", q_rows, k_rows, preferred_element_type=jnp.float32) * scale
        )
        scores = jnp.where(rows_valid[:, None, :, None], scores, -jnp.inf)
        top = jnp.max(scores, axis=(2, 3), keepdims=True)
        expo = jnp.exp(scores - top)
        probs = (expo / jnp.sum(expo, axis=(2, 3), keepdims=True)).astype(jnp.bfloat16)
        return jnp.einsum(
            "nqck,dnck->dnq", probs, v_rows, preferred_element_type=jnp.float32
        ).astype(jnp.bfloat16)

    parts = lax.map(one_group, jnp.arange(turns, dtype=jnp.int32))
    blocks = jnp.transpose(parts, (1, 0, 2, 3)).reshape(HD, nblocks, BLK)
    qglob = jnp.take(qb, glob, axis=1)
    gscore = jnp.einsum("dgq,dk->gqk", qglob, k_head, preferred_element_type=jnp.float32) * scale
    gtop = jnp.max(gscore, axis=2, keepdims=True)
    gexp = jnp.exp(gscore - gtop)
    gprob = (gexp / jnp.sum(gexp, axis=2, keepdims=True)).astype(jnp.bfloat16)
    full = jnp.einsum("gqk,dk->dgq", gprob, v_head, preferred_element_type=jnp.float32).astype(
        jnp.bfloat16
    )
    blocks = blocks.at[:, glob, :].set(full)
    return blocks.reshape(HD, length)


def local_plain(queries, keys, values, random_blocks, global_blocks, out_weight):
    q_heads, k_heads, v_heads = (
        lax.all_to_all(queries[0], "seq", split_axis=0, concat_axis=1, tiled=True),
        lax.all_to_all(keys[0], "seq", split_axis=0, concat_axis=1, tiled=True),
        lax.all_to_all(values[0], "seq", split_axis=0, concat_axis=1, tiled=True),
    )
    count = q_heads.shape[0] // HD
    length = q_heads.shape[1]
    glob = global_blocks[0]

    def one_head(packed):
        q_head, k_head, v_head, rand_h = packed
        return head_attention(q_head, k_head, v_head, rand_h, glob)

    outputs = lax.map(
        one_head,
        (
            q_heads.reshape(count, HD, length),
            k_heads.reshape(count, HD, length),
            v_heads.reshape(count, HD, length),
            random_blocks[0],
        ),
    )
    attended = lax.all_to_all(
        outputs.reshape(count * HD, length), "seq", split_axis=1, concat_axis=0, tiled=True
    )
    result = lax.dot_general(
        attended,
        lax.all_gather(out_weight, "dp", axis=0, tiled=True),
        (((0,), (0,)), ((), ())),
        preferred_element_type=jnp.float32,
    )
    return result.astype(jnp.bfloat16)[None]


def cut_kernel(n, feats, row, q_ref, k_ref, v_ref, out, sems):
    copies = []
    for to in range(n):
        for i, src in enumerate((q_ref, k_ref, v_ref)):
            src = src.at[0, pl.ds(to * feats + row, PAIR), :]
            copies.append(pltpu.make_async_copy(src, out.at[to, i], sems.at[to, i]))
    for copy in copies:
        copy.start()
    for copy in copies:
        copy.wait()


def cut(n, row, queries, keys, values):
    feats = queries.shape[1] // n
    length = queries.shape[2]
    hbm = pl.BlockSpec(memory_space=pl.ANY)
    return pl.pallas_call(
        functools.partial(cut_kernel, n, feats, row),
        out_shape=pltpu.VMEM((n, 3, PAIR, length), queries.dtype),
        in_specs=[hbm, hbm, hbm],
        out_specs=pl.BlockSpec(memory_space=pltpu.VMEM),
        scratch_shapes=[pltpu.SemaphoreType.DMA((n, 3))],
        compiler_params=pltpu.CompilerParams(vmem_limit_bytes=56 * 1024 * 1024),
        name="cut",
    )(queries, keys, values)


def cut_apart_kernel(n, feats, row, me_ref, q_ref, k_ref, v_ref, *rest):
    outs = rest[:n]
    held, in_sems, out_sems = rest[n:]
    me = me_ref[0]

    def read(k, i):
        start = pl.multiple_of((me ^ k) * feats + row, PAIR)
        src = (q_ref, k_ref, v_ref)[i]
        return pltpu.make_async_copy(
            src.at[0, pl.ds(start, PAIR), :], held.at[k, i], in_sems.at[k, i]
        )

    def write(k):
        return pltpu.make_async_copy(held.at[k], outs[k], out_sems.at[k])

    for k in range(n):
        for i in range(3):
            read(k, i).start()
    for k in range(n):
        for i in range(3):
            read(k, i).wait()
        write(k).start()
    for k in range(n):
        write(k).wait()


def cut_apart(n, row, me, queries, keys, values):
    feats = queries.shape[1] // n
    length = queries.shape[2]
    hbm = pl.BlockSpec(memory_space=pltpu.HBM)
    return pl.pallas_call(
        functools.partial(cut_apart_kernel, n, feats, row),
        out_shape=[jax.ShapeDtypeStruct((3, PAIR, length), queries.dtype)] * n,
        in_specs=[pl.BlockSpec(memory_space=pltpu.SMEM), hbm, hbm, hbm],
        out_specs=[hbm] * n,
        scratch_shapes=[
            pltpu.VMEM((n, 3, PAIR, length), queries.dtype),
            pltpu.SemaphoreType.DMA((n, 3)),
            pltpu.SemaphoreType.DMA((n,)),
        ],
        name="cut_apart",
    )(me, queries, keys, values)


def swap_halves(x):
    return jnp.concatenate([x[:, BLK:], x[:, :BLK]], axis=1)


def attend_kernel(n, nblocks, apart_in, apart_out, me_ref, rand_ref, glob_ref, *rest):
    pen_ref, rest = rest[0], rest[1:]
    ins, rest = (rest[:n], rest[n:]) if apart_in else (rest[:1], rest[1:])
    outs, rest = (rest[:n], rest[n:]) if apart_out else (rest[:1], rest[1:])
    raw, kt, vv, ob, sg, in_sems, out_sems = rest
    me = me_ref[0]
    shard = raw.shape[3]
    per = shard // BLK
    tiles = shard // PAIR
    f32, bf16 = jnp.float32, jnp.bfloat16

    shards = [me ^ k for k in range(n)] if apart_in else list(range(n))
    arrivals = []
    for i, s in enumerate(shards):
        src = ins[i] if apart_in else ins[0].at[i]
        arrivals.append(pltpu.make_async_copy(src, raw.at[s], in_sems.at[i]))
    for copy in arrivals:
        copy.start()

    for s, copy in zip(shards, arrivals):
        copy.wait()
        for t in range(tiles):
            lanes = slice(t * PAIR, (t + 1) * PAIR)
            first = pl.multiple_of(s * shard + t * PAIR, PAIR)
            kt[pl.ds(first, PAIR), :] = raw[s, 1, :, lanes].T
            v = raw[s, 2, :, lanes]
            vv[0, s * tiles + t] = v
            vv[1, s * tiles + t] = swap_halves(v)

    low = lax.broadcasted_iota(jnp.int32, (BLK, PAIR), 1) < BLK
    zero = jnp.zeros((HD, PAIR), bf16)

    def queries_of(x, odd):
        y = swap_halves(x)
        a, b = (y, x) if odd else (x, y)
        return jnp.concatenate(
            [jnp.where(low, a[:HD], zero), jnp.where(low, zero, b[HD:])], axis=0
        )

    def key_rows(b):
        return kt[pl.ds(pl.multiple_of(b * BLK, BLK), BLK), :]

    def value_half(head, b, place):
        side = lax.rem(b + place, 2)
        return vv[side, lax.div(b, 2), head * HD : (head + 1) * HD, :]

    def finish(ot, total):
        t = (ot / total).astype(bf16).T
        return jnp.where(low, t[:BLK], t[BLK:])

    def sparse(j, qbd):
        shared = [jnp.maximum(j - 1, 0), j, jnp.minimum(j + 1, nblocks - 1), glob_ref[0], glob_ref[1]]
        cand = [
            shared + [rand_ref[(h * nblocks + j) * 3 + c] for c in range(3)] for h in range(2)
        ]
        k_rows = [key_rows(b) for b in shared]
        for c in range(5, 8):
            k_rows.append(jnp.where(low, key_rows(cand[0][c]), key_rows(cand[1][c])))
        scores = jnp.dot(jnp.concatenate(k_rows, axis=0), qbd, preferred_element_type=f32)
        top = jnp.max(scores, axis=0, keepdims=True) * EXP_SCALE
        pen = pen_ref[j]
        shift = jnp.where(low[:8], pen[:, 0:1], pen[:, 1:2]) + top
        probs = [
            jnp.exp2(scores[c * BLK : (c + 1) * BLK] * EXP_SCALE - shift[c : c + 1])
            for c in range(8)
        ]
        total = functools.reduce(
            jnp.add, [jnp.sum(p, axis=0, keepdims=True) for p in probs]
        )
        pt = jnp.concatenate([p.astype(bf16) for p in probs], axis=0)
        vcat = []
        for c in range(0, 8, 2):
            vcat.append(
                jnp.concatenate(
                    [
                        jnp.where(
                            low, value_half(h, cand[h][c], 0), value_half(h, cand[h][c + 1], 1)
                        )
                        for h in range(2)
                    ],
                    axis=0,
                )
            )
        ot = jnp.dot(jnp.concatenate(vcat, axis=1), pt, preferred_element_type=f32)
        return finish(ot, total)

    def tile_of(i):
        s = lax.div(i, tiles)
        first = pl.multiple_of(lax.rem(i, tiles) * PAIR, PAIR)
        return s, first

    def two_blocks(i, carry):
        s, first = tile_of(i)
        x = raw[s, 0, :, pl.ds(first, PAIR)]
        a = sparse(2 * i, queries_of(x, False))
        b = sparse(2 * i + 1, queries_of(x, True))
        ob[s, pl.ds(first, PAIR), :] = jnp.concatenate([a, b], axis=0)
        return carry

    lax.fori_loop(0, nblocks // 2, two_blocks, 0, unroll=8)

    places, columns = [], []
    for g in range(2):
        s, first = tile_of(lax.div(glob_ref[g], 2))
        x = raw[s, 0, :, pl.ds(first, PAIR)]
        odd = lax.rem(glob_ref[g], 2)
        columns.append(jnp.where(odd == 1, queries_of(x, True), queries_of(x, False)))
        places.append((s, pl.multiple_of(lax.rem(glob_ref[g], per) * BLK, BLK)))
    qbd = jnp.concatenate(columns, axis=1)
    top = jnp.full((1, 2 * PAIR), -jnp.inf, f32)
    for t in range(n):
        rows = slice(t * shard, (t + 1) * shard)
        scores = jnp.dot(kt[rows, :], qbd, preferred_element_type=f32)
        sg[rows, :] = scores
        top = jnp.maximum(top, jnp.max(scores, axis=0, keepdims=True))
    top = top * EXP_SCALE
    total = jnp.zeros((1, 2 * PAIR), f32)
    ot = jnp.zeros((PAIR, 2 * PAIR), f32)
    for t in range(n):
        p = jnp.exp2(sg[t * shard : (t + 1) * shard, :] * EXP_SCALE - top)
        total = total + jnp.sum(p, axis=0, keepdims=True)
        ot = ot + jnp.dot(raw[t, 2], p.astype(bf16), preferred_element_type=f32)
    for g, (s, place) in enumerate(places):
        lanes = slice(g * PAIR, (g + 1) * PAIR)
        ob[s, pl.ds(place, BLK), :] = finish(ot[:, lanes], total[:, lanes])

    if apart_out:
        leaving = [
            pltpu.make_async_copy(ob.at[me ^ k], outs[k], out_sems.at[k])
            for k in range(n)
        ]
    else:
        leaving = [pltpu.make_async_copy(ob, outs[0], out_sems.at[0])]
    for copy in leaving:
        copy.start()
    for copy in leaving:
        copy.wait()


def attend(n, me, rand, glob, pen, arrays, apart_out):
    apart_in = len(arrays) > 1
    shard = arrays[0].shape[-1]
    length = n * shard
    nblocks = length // BLK
    hbm = pl.BlockSpec(memory_space=pltpu.HBM)
    smem = pl.BlockSpec(memory_space=pltpu.SMEM)
    vmem = pl.BlockSpec(memory_space=pltpu.VMEM)
    if apart_out:
        out_shape = [jax.ShapeDtypeStruct((shard, PAIR), jnp.bfloat16)] * n
    else:
        out_shape = [jax.ShapeDtypeStruct((n, shard, PAIR), jnp.bfloat16)]
    return pl.pallas_call(
        functools.partial(attend_kernel, n, nblocks, apart_in, apart_out),
        out_shape=out_shape,
        in_specs=[smem, smem, smem, vmem] + [hbm] * len(arrays),
        out_specs=[hbm] * len(out_shape),
        scratch_shapes=[
            pltpu.VMEM((n, 3, PAIR, shard), jnp.bfloat16),
            pltpu.VMEM((length, PAIR), jnp.bfloat16),
            pltpu.VMEM((2, nblocks // 2, PAIR, PAIR), jnp.bfloat16),
            pltpu.VMEM((n, shard, PAIR), jnp.bfloat16),
            pltpu.VMEM((length, 2 * PAIR), jnp.float32),
            pltpu.SemaphoreType.DMA((n,)),
            pltpu.SemaphoreType.DMA((n,)),
        ],
        compiler_params=pltpu.CompilerParams(vmem_limit_bytes=60 * 1024 * 1024),
        cost_estimate=pl.CostEstimate(
            flops=15_000_000_000, bytes_accessed=4_000_000, transcendentals=0
        ),
        name="attend",
    )(me, rand, glob, pen, *arrays)


def project_kernel(n, ndp, slots, ahead, before, me_ref, *rest):
    arrays = sorted({i for i, _, _ in slots})
    pieces, rest = rest[: len(arrays)], rest[len(arrays) :]
    if before:
        before_ref, w, o_ref, done, out_sems = rest
    else:
        weights, rest = rest[:ndp], rest[ndp:]
        o_ref, ahead_ref, a, w, a_sems, w_sems, ahead_sems = rest
    me, dp = me_ref[0], me_ref[1]
    width = w.shape[1]
    tile = width // 4

    def piece_copy(slot):
        i, _, k = slots[slot]
        src = pieces[arrays.index(i)]
        src = src.at[me ^ k] if len(src.shape) == 3 else src
        dst = a.at[:, pl.ds(slot * PAIR, PAIR)]
        return pltpu.make_async_copy(src, dst, a_sems.at[slot])

    def out_copy(t):
        columns = pl.ds(t * tile, tile)
        return pltpu.make_async_copy(done.at[:, columns], o_ref.at[0, :, columns], out_sems.at[t])

    if not before:
        for slot in range(len(slots)):
            piece_copy(slot).start()
        held = n // ndp
        feats = weights[0].shape[0] // held

        def weight_copy(which, slot, part):
            _, p, k = which[slot]
            row = pl.multiple_of(lax.rem(me ^ k, held) * feats + p * PAIR, PAIR)
            dst, sems = (w, w_sems) if which is slots else (ahead_ref, ahead_sems)
            return pltpu.make_async_copy(
                weights[part].at[pl.ds(row, PAIR), :],
                dst.at[pl.ds(slot * PAIR, PAIR), :],
                sems.at[slot],
            )

        own = lax.div(me, held) ^ dp
        for r in range(ndp):

            @pl.when(own == r)
            def _():
                for which in (slots, ahead):
                    for slot in range(len(which)):
                        weight_copy(which, slot, r ^ (which[slot][2] // held)).start()

        for slot in range(len(slots)):
            weight_copy(slots, slot, 0).wait()
        for slot in range(len(slots)):
            piece_copy(slot).wait()
        rows = a[...]
    else:
        rows = jnp.concatenate([piece[...] for piece in pieces], axis=1)
    for t in range(4):
        columns = slice(t * tile, (t + 1) * tile)
        total = jnp.dot(rows, w[:, columns], preferred_element_type=jnp.float32)
        if before:
            total = total + before_ref[0, :, columns]
        if before:
            done[:, columns] = total.astype(o_ref.dtype)
            out_copy(t).start()
        else:
            o_ref[0, :, columns] = total
    if before:
        for t in range(4):
            out_copy(t).wait()
    else:
        for slot in range(len(ahead)):
            weight_copy(ahead, slot, 0).wait()


def project_early(n, me, pieces, slots, ahead, weights):
    shard = pieces[0].shape[-2]
    ndp = len(weights)
    width = weights[0].shape[1]
    depth = len(slots) * PAIR
    hbm = pl.BlockSpec(memory_space=pl.ANY)
    return pl.pallas_call(
        functools.partial(project_kernel, n, ndp, slots, ahead, False),
        out_shape=[
            pltpu.VMEM((1, shard, width), jnp.float32),
            pltpu.VMEM((len(ahead) * PAIR, width), jnp.bfloat16),
        ],
        in_specs=[pl.BlockSpec(memory_space=pltpu.SMEM)] + [hbm] * (len(pieces) + ndp),
        out_specs=[pl.BlockSpec(memory_space=pltpu.VMEM)] * 2,
        scratch_shapes=[
            pltpu.VMEM((shard, depth), jnp.bfloat16),
            pltpu.VMEM((depth, width), jnp.bfloat16),
            pltpu.SemaphoreType.DMA((len(slots),)),
            pltpu.SemaphoreType.DMA((len(slots),)),
            pltpu.SemaphoreType.DMA((len(ahead),)),
        ],
        compiler_params=pltpu.CompilerParams(vmem_limit_bytes=24 * 1024 * 1024),
        cost_estimate=pl.CostEstimate(
            flops=2 * shard * depth * width, bytes_accessed=10_000_000, transcendentals=0
        ),
        name="project_early",
    )(me, *pieces, *weights)


def project_late(n, me, pieces, slots, before, rows):
    shard = pieces[0].shape[-2]
    width = rows.shape[1]
    depth = len(slots) * PAIR
    hbm = pl.BlockSpec(memory_space=pl.ANY)
    vmem = pl.BlockSpec(memory_space=pltpu.VMEM)
    before, rows, *pieces = (
        pltpu.with_memory_space_constraint(x, pltpu.VMEM) for x in (before, rows, *pieces)
    )
    return pl.pallas_call(
        functools.partial(project_kernel, n, 0, slots, [], True),
        out_shape=jax.ShapeDtypeStruct((1, shard, width), jnp.bfloat16),
        in_specs=[pl.BlockSpec(memory_space=pltpu.SMEM)] + [vmem] * len(pieces) + [vmem, vmem],
        out_specs=hbm,
        scratch_shapes=[
            pltpu.VMEM((shard, width), jnp.bfloat16),
            pltpu.SemaphoreType.DMA((4,)),
        ],
        compiler_params=pltpu.CompilerParams(vmem_limit_bytes=24 * 1024 * 1024),
        cost_estimate=pl.CostEstimate(
            flops=2 * shard * depth * width, bytes_accessed=10_000_000, transcendentals=0
        ),
        name="project_late",
    )(me, *pieces, before, rows)


def gather_weight(ndp, weight):
    parts = {0: weight}
    bit = ndp // 2
    while bit:
        for r in list(parts):
            parts[r + bit] = lax.ppermute(parts[r], "dp", [(i, i ^ bit) for i in range(ndp)])
        bit //= 2
    return [parts[r] for r in range(ndp)]


def local_paired(n, ndp, queries, keys, values, random_blocks, global_blocks, out_weight):
    me = jnp.stack([lax.axis_index("seq"), lax.axis_index("dp")]).astype(jnp.int32)
    feats = queries.shape[1] // n
    length = queries.shape[2] * n
    nblocks = length // BLK
    pairs = feats // PAIR
    glob = global_blocks[0]

    def exchange(x):
        return lax.all_to_all(x, "seq", split_axis=0, concat_axis=0, tiled=True)

    def swap(arrays, order):
        got = {k: lax.ppermute(arrays[k], "seq", [(i, i ^ k) for i in range(n)]) for k in order}
        return [arrays[0]] + [got[k] for k in range(1, n)]

    near, far = list(range(1, n // 2)), list(range(n // 2, n))

    valid = jax.vmap(lambda r: candidate_blocks(nblocks, glob, r)[1])(random_blocks[0])
    pen = jnp.where(valid, 0.0, BIG).astype(jnp.float32)
    pen = jnp.transpose(pen.reshape(pairs, 2, nblocks, -1), (0, 2, 3, 1))
    rand = random_blocks[0].reshape(pairs, -1)

    last = pairs - 1
    arrived = [exchange(cut(n, p * PAIR, queries, keys, values)) for p in range(last)]
    messages = swap(cut_apart(n, last * PAIR, me, queries, keys, values), near + far)
    weights = gather_weight(ndp, lax.optimization_barrier((out_weight, messages[1]))[0])

    pieces, slots = [], []
    for p in range(last):
        outs = attend(n, me, rand[p], glob, pen[p], [arrived[p]], False)
        pieces.append(exchange(outs[0]))
        slots += [(p, p, k) for k in range(n)]
    outs = attend(n, me, rand[last], glob, pen[last], messages, True)
    outs, weights = lax.optimization_barrier((list(outs), weights))
    results = swap(outs, far + near)
    pieces += [results[k] for k in [0] + near]
    slots += [(last + i, last, k) for i, k in enumerate([0] + near)]
    late = [(i, last, k) for i, k in enumerate(far)]
    total, rows = project_early(n, me, pieces, slots, late, weights)
    return project_late(n, me, [results[k] for k in far], late, total, rows)


def solution(mesh):
    n, ndp = mesh.shape["seq"], mesh.shape["dp"]
    in_specs = (
        P("dp", None, "seq"),
        P("dp", None, "seq"),
        P("dp", None, "seq"),
        P("dp", "seq", None, None),
        P("dp", None),
        P("dp", None),
    )
    out_specs = P("dp", "seq", None)

    def local(queries, keys, *rest):
        feats, shard = queries.shape[1] // n, queries.shape[2]
        paired = feats % PAIR == 0 and shard % PAIR == 0 and n % ndp == 0
        paired = paired and n & (n - 1) == 0 and ndp & (ndp - 1) == 0
        body = functools.partial(local_paired, n, ndp) if paired else local_plain
        return body(queries, keys, *rest)

    return jax.shard_map(local, mesh=mesh, in_specs=in_specs, out_specs=out_specs, check_vma=False)
```
